32 devices in a mesh: rows: 4 (over z), cols: 2 (over y), dp: 4 (over x, core).
Axes of the slice: x: 2, y: 2, z: 4, core: 2. Of those that a mesh axis runs over, the one named last changes fastest.
Arguments:
- features: bfloat16 [4, 32, 512, 256], P('dp', 'rows', 'cols'), may hold values from -340 to 340, as said below
- upstream: bfloat16 [4, 32, 512, 256], P('dp', 'rows', 'cols'), may hold values from -6 to 6
- conv_weight: bfloat16 [3, 3, 32, 256], replicated, may hold values from -0.375 to 0.375
- norm_gain: float32 [256], replicated, may hold values from 0.25 to 1.75
- norm_bias: float32 [256], replicated, may hold values from -3 to 3
Outputs:
- input_grad: bfloat16 [4, 32, 512, 256], P('dp', 'rows', 'cols')
- weight_grad: float32 [3, 3, 32, 256], replicated
- gain_grad: float32 [256], replicated
- bias_grad: float32 [256], replicated
The draws below stay inside these ranges and needn't reach their ends.
Inputs may be any that keep to these rules, and one draw needn't show every extreme that they name: `features`: finite feature values.
All inputs are finite; a program needn't handle non-finite values.
Results may differ from the reference program's by a relative error of at most 0.0031.
Values may be sent and summed in bfloat16 or wider, within the bound.
No kernel may reach another device: no remote copies, remote signals or barrier semaphores. Data moves between devices by JAX's collectives and lax.ppermute only.
A program may use at most 128 MiB of HBM per device.

```python
import math
import jax
import jax.numpy as jnp
from jax import lax

C = 256
CHANNEL_GROUPS = 8
GS = 32
DILATION_RATE = 6
ITERS = 5
H = 32
W = 512
MOS = 4


def draw_features(key, part):
    noise_key = jax.random.fold_in(key, 11)
    channel_key = jax.random.fold_in(key, 12)
    row_key = jax.random.fold_in(key, 13)
    col_key = jax.random.fold_in(key, 14)
    base = jnp.clip(jax.random.normal(noise_key, (MOS, H, W, C), jnp.float32), -4.0, 4.0)
    channel_scale = jnp.exp(jax.random.uniform(channel_key, (C,), jnp.float32, 0.0, math.log(10.0)))
    mixed = base + 0.5 * jnp.roll(base, 1, axis=3)
    row_rise = jnp.exp(math.log(3.0) * jnp.arange(H, dtype=jnp.float32) / (H - 1))
    row_rise = row_rise * jnp.exp(jax.random.uniform(row_key, (H,), jnp.float32, 0.0, math.log(2.0)))
    col_rise = jnp.exp(math.log(3.0) * jnp.arange(W, dtype=jnp.float32) / (W - 1))
    col_rise = col_rise * jnp.exp(jax.random.uniform(col_key, (W,), jnp.float32, 0.0, math.log(2.0)))
    image_rise = jnp.exp(math.log(3.0) * jnp.arange(MOS, dtype=jnp.float32) / max(MOS - 1, 1))
    scaled = mixed * channel_scale * row_rise[None, :, None, None] * col_rise[None, None, :, None]
    scaled = scaled * image_rise[:, None, None, None] / 20.0
    return scaled.astype(jnp.bfloat16)


def level_of(rng, dims, shards, low, top_value):
    level, own = 1.0, jax.random.fold_in(rng, 6)
    for position, shards_of in shards:
        draws = jnp.exp(jax.random.uniform(jax.random.fold_in(own, position), (shards_of,), jnp.float32, low / len(shards), top_value / len(shards)))
        level = level * jnp.repeat(draws, dims[position] // shards_of).reshape([-1 if axis == position else 1 for axis in range(len(dims))])
    return level


def centred(stream_key, shape, spread, most, split=(), kind=jnp.bfloat16):
    factor_of = level_of(stream_key, shape, split, -0.22, 0.18) if split else 1.0
    result = jax.random.normal(stream_key, shape, jnp.float32) * spread * factor_of
    return jnp.minimum(jnp.maximum(result, -most), most).astype(kind)


def setup_inputs(seed: int = 0) -> dict:
    streams_of = jax.random.split(jax.random.key(seed), 6)
    features = draw_features(jax.random.fold_in(streams_of[5], 71), 0)
    upstream = centred(streams_of[1], (MOS, H, W, C), 1.0, 6.0, ((0, 4), (1, 4), (2, 2)))
    conv_weight = centred(streams_of[2], (3, 3, GS, C), (9 * GS) ** -0.5, 0.375)
    norm_gain = jnp.clip(1.0 + 0.15 * jax.random.normal(streams_of[3], (C,), jnp.float32), 0.25, 1.75)
    norm_bias = centred(streams_of[4], (C,), 0.5, 3.0, (), jnp.float32)
    return dict(features=features, upstream=upstream, conv_weight=conv_weight, norm_gain=norm_gain, norm_bias=norm_bias)


EPSILON = 1e-05

def whitening_matrix(covariance):
    trace_sum = jnp.trace(covariance, axis1=1, axis2=2)
    normed = covariance / trace_sum[:, None, None]
    identity = jnp.broadcast_to(jnp.eye(GS, dtype=jnp.float32), covariance.shape)
    iterate = identity
    for repeat in range(ITERS):
        product = jnp.einsum('gij,gjk->gik', iterate, iterate, precision=lax.Precision.HIGHEST)
        product = jnp.einsum('gij,gjk->gik', product, iterate, precision=lax.Precision.HIGHEST)
        product = jnp.einsum('gij,gjk->gik', product, normed, precision=lax.Precision.HIGHEST)
        iterate = 1.5 * iterate - 0.5 * product
    return iterate / jnp.sqrt(trace_sum)[:, None, None]

def dilated_conv(border_filled, filter_weight):
    return lax.conv_general_dilated(border_filled, filter_weight, (1, 1), 'VALID', rhs_dilation=(DILATION_RATE, DILATION_RATE), dimension_numbers=('NHWC', 'HWIO', 'NHWC'), feature_group_count=CHANNEL_GROUPS, preferred_element_type=jnp.float32)

def flipped_kernel(filter_weight):
    reordered = filter_weight.reshape(3, 3, GS, CHANNEL_GROUPS, GS)[::-1, ::-1]
    return jnp.transpose(reordered, (0, 1, 4, 3, 2)).reshape(3, 3, GS, C)

def weight_gradient(border_activation, upstream):
    row_count = upstream.shape[1]
    column_count = upstream.shape[2]
    grad_out = upstream.reshape(upstream.shape[:3] + (CHANNEL_GROUPS, GS))
    tap_list = []
    for row_offset in range(3):
        for column_offset in range(3):
            sliding_patch = border_activation[:, row_offset * DILATION_RATE:row_offset * DILATION_RATE + row_count, column_offset * DILATION_RATE:column_offset * DILATION_RATE + column_count, :]
            sliding_patch = sliding_patch.reshape(grad_out.shape)
            tap_grad = jnp.einsum('bhwgi,bhwgo->igo', sliding_patch, grad_out, preferred_element_type=jnp.float32)
            tap_list.append(tap_grad.reshape(GS, C))
    return jnp.stack(tap_list).reshape(3, 3, GS, C)

def reference(features, upstream, conv_weight, norm_gain, norm_bias):
    cell_count = MOS * H * W
    grouped = features.astype(jnp.float32).reshape(MOS, H, W, CHANNEL_GROUPS, GS)
    channel_mean = lax.optimization_barrier(jnp.sum(grouped, axis=(0, 1, 2))) / cell_count
    centered = grouped - channel_mean
    covariance = jnp.einsum('bhwgi,bhwgj->gij', centered, centered, precision=lax.Precision.HIGHEST) / cell_count
    covariance = covariance + EPSILON * jnp.eye(GS, dtype=jnp.float32)
    whitener, pullback = jax.vjp(whitening_matrix, covariance)
    whitened = jnp.einsum('goi,bhwgi->bhwgo', whitener, centered, precision=lax.Precision.HIGHEST)
    gain_group = norm_gain.reshape(CHANNEL_GROUPS, GS)
    pre_act = gain_group * whitened + norm_bias.reshape(CHANNEL_GROUPS, GS)
    activation = jax.nn.silu(pre_act).reshape(MOS, H, W, C).astype(jnp.bfloat16)
    border_widths = ((0, 0), (DILATION_RATE, DILATION_RATE), (DILATION_RATE, DILATION_RATE), (0, 0))
    border_activation = jnp.pad(activation, border_widths)
    border_upstream = jnp.pad(upstream, border_widths)
    act_grad = dilated_conv(border_upstream, flipped_kernel(conv_weight)).reshape(MOS, H, W, CHANNEL_GROUPS, GS)
    tap_sum = weight_gradient(border_activation, upstream)
    sigmoid_value = jax.nn.sigmoid(pre_act)
    pre_grad = act_grad * (sigmoid_value * (1.0 + pre_act * (1.0 - sigmoid_value)))
    gain_sum = lax.optimization_barrier(jnp.sum(pre_grad * whitened, axis=(0, 1, 2)))
    bias_sum = lax.optimization_barrier(jnp.sum(pre_grad, axis=(0, 1, 2)))
    white_grad = pre_grad * gain_group
    whitener_grad = jnp.einsum('bhwgo,bhwgi->goi', white_grad, centered, precision=lax.Precision.HIGHEST)
    cov_grad = pullback(whitener_grad)[0]
    symmetric = cov_grad + jnp.swapaxes(cov_grad, 1, 2)
    back_term = jnp.einsum('goi,bhwgo->bhwgi', whitener, white_grad, precision=lax.Precision.HIGHEST)
    mean_term = jnp.einsum('goi,go->gi', whitener, gain_group * bias_sum, precision=lax.Precision.HIGHEST) / cell_count
    cov_term = jnp.einsum('gij,bhwgj->bhwgi', symmetric, centered, precision=lax.Precision.HIGHEST) / cell_count
    input_grad = (back_term - mean_term + cov_term).reshape(MOS, H, W, C).astype(jnp.bfloat16)
    grad_scale = 1.0 / jnp.sqrt(jnp.float32(cell_count))
    return (input_grad, tap_sum * grad_scale, gain_sum.reshape(C) * grad_scale, bias_sum.reshape(C) * grad_scale)
```

```python
import functools
import math

import jax
import jax.numpy as jnp
from jax import lax
from jax.experimental import pallas as pl
from jax.experimental.pallas import tpu as pltpu
from jax.sharding import PartitionSpec as P

C = 256
CHANNEL_GROUPS = 8
GS = 32
DILATION_RATE = 6
ITERS = 5
EPSILON = 1e-05

F32 = jnp.float32
BF16 = jnp.bfloat16
VMEM_SPEC = pl.BlockSpec(memory_space=pltpu.VMEM)


def run(body, out_shapes, operands, scratch=(), limit=40, flops=0):
    many = isinstance(out_shapes, (tuple, list))
    return pl.pallas_call(
        body,
        out_shape=out_shapes,
        in_specs=[VMEM_SPEC] * len(operands),
        out_specs=[VMEM_SPEC] * len(out_shapes) if many else VMEM_SPEC,
        scratch_shapes=list(scratch),
        compiler_params=pltpu.CompilerParams(vmem_limit_bytes=limit * 2**20),
        cost_estimate=pl.CostEstimate(flops=flops, bytes_accessed=2**20, transcendentals=0),
    )(*operands)


def same_group():
    rows = lax.broadcasted_iota(jnp.int32, (C, C), 0)
    columns = lax.broadcasted_iota(jnp.int32, (C, C), 1)
    return (rows >> 5) == (columns >> 5)


def fold(full, same):
    kept = jnp.where(same, full, 0.0)
    total = kept[0:GS]
    for g in range(1, CHANNEL_GROUPS):
        total = total + kept[g * GS : (g + 1) * GS]
    return total


def spread(packed, same):
    return jnp.where(same, jnp.concatenate([packed] * CHANNEL_GROUPS, axis=0), 0)


def split(value):
    high = value.astype(BF16)
    low = (value - high.astype(F32)).astype(BF16)
    return high, low


def spread_split(packed, same):
    high, low = split(spread(packed, same))
    return high, low


def dot(a, b):
    return jnp.dot(a, b, preferred_element_type=F32)


def times(left, right):
    rows = left.shape[0]
    left_high, left_low = split(left)
    right_high, right_low = right
    both = dot(jnp.concatenate([left_high, left_low], axis=0), right_high)
    return both[:rows] + both[rows:] + dot(left_high, right_low)


def unit():
    rows = lax.broadcasted_iota(jnp.int32, (GS, C), 0)
    columns = lax.broadcasted_iota(jnp.int32, (GS, C), 1)
    return jnp.where(rows == (columns & (GS - 1)), 1.0, 0.0)


def group_total(row, same):
    wide = jnp.broadcast_to(row, (8, C))
    return jnp.dot(wide, jnp.where(same, 1.0, 0.0), precision=lax.Precision.HIGHEST)


def stats_kernel(x_ref, out_ref):
    rows = x_ref.shape[0]
    cells = rows * x_ref.shape[1]
    same = same_group()

    def add_up(r, total):
        return total + jnp.sum(x_ref[r].astype(F32), axis=0, keepdims=True)

    mean = lax.fori_loop(0, rows, add_up, jnp.zeros((1, C), F32)) / cells

    def products(r, total):
        high, low = split(x_ref[r].astype(F32) - mean)
        return total + lax.dot_general(
            high,
            jnp.concatenate([high, low], axis=1),
            (((0,), (0,)), ((), ())),
            preferred_element_type=F32,
        )

    total = lax.fori_loop(0, rows, products, jnp.zeros((C, 2 * C), F32))
    cross = total[:, C:]
    out_ref[0:GS] = fold(total[:, :C] + cross + cross.T, same) / cells
    out_ref[GS : 2 * GS] = fold(jnp.broadcast_to(mean, (C, C)).T, same)
    out_ref[2 * GS : 2 * GS + 8] = jnp.broadcast_to(mean, (8, C))


def merge_kernel(a_ref, b_ref, out_ref):
    a, b = a_ref[...], b_ref[...]
    half = 0.5 * (a + b)
    gap = b - a
    wide = jnp.concatenate([gap[2 * GS :]] * (GS // 8), axis=0)
    out_ref[0:GS] = half[0:GS] + 0.25 * gap[GS : 2 * GS] * wide
    out_ref[GS:] = half[GS:]


def conv_kernel(up_ref, top_ref, bottom_ref, left_ref, right_ref, w_ref, moved_ref, out_ref, bands_ref, weight_ref):
    rows, width = up_ref.shape[0], up_ref.shape[1]
    d = DILATION_RATE
    pad = 16
    same = same_group()
    for tap in range(9):
        tile = jnp.concatenate([w_ref[tap].astype(F32)] * CHANNEL_GROUPS, axis=0)
        weight_ref[tap] = jnp.where(same, tile, 0.0).T.astype(BF16)
    moved_ref[1, 0:d] = top_ref[...]
    moved_ref[1, d : d + rows] = up_ref[...]
    moved_ref[1, d + rows :] = bottom_ref[...]
    line = lax.broadcasted_iota(jnp.int32, (width, C), 0)

    def shift(e, carry):
        band = moved_ref[1, e].astype(F32)
        bands_ref[pad : pad + width] = band
        bands_ref[pad - d : pad] = left_ref[e].astype(F32)
        bands_ref[pad + width : pad + width + d] = right_ref[e].astype(F32)
        moved_ref[0, e] = bands_ref[pad + d : pad + d + width].astype(BF16)
        moved_ref[2, e] = bands_ref[pad - d : pad - d + width].astype(BF16)
        return carry

    lax.fori_loop(0, rows + 2 * d, shift, 0)

    def row(r, carry):
        total = jnp.zeros((width, C), F32)
        for a in range(3):
            for b in range(3):
                total = total + dot(moved_ref[b, r + (2 - a) * d], weight_ref[3 * a + b])
        out_ref[r] = total
        return carry

    lax.fori_loop(0, rows, row, 0)


def main_kernel(x_ref, stats_ref, gain_ref, bias_ref, grad_ref, turned_ref, back_ref, sums_ref, kept_ref):
    rows = x_ref.shape[0]
    same = same_group()
    eye = unit()
    gain, bias = gain_ref[0:1], bias_ref[0:1]
    mean = stats_ref[2 * GS : 2 * GS + 1]
    cov = stats_ref[0:GS] + EPSILON * eye
    trace = group_total(jnp.sum(cov * eye, axis=0, keepdims=True), same)[0:1]
    normed = cov / trace
    normed_wide = spread_split(normed, same)
    iterate = 1.5 * eye - 0.5 * normed
    for k in range(ITERS - 1):
        wide = spread_split(iterate, same)
        square = times(iterate, wide)
        scaled = times(iterate, normed_wide)
        scaled_wide = spread_split(scaled, same)
        cube_scaled = times(square, scaled_wide)
        kept_ref[k, 0] = iterate
        kept_ref[k, 1] = square
        kept_ref[k, 2] = scaled
        kept_ref[k, 3] = times(iterate, scaled_wide)
        kept_ref[k, 4] = times(square, wide)
        iterate = 1.5 * iterate - 0.5 * cube_scaled
    whitener = iterate * lax.rsqrt(trace)
    kept_ref[ITERS - 1, 0] = whitener
    kept_ref[ITERS - 1, 1] = normed
    kept_ref[ITERS - 1, 2] = jnp.broadcast_to(trace, (GS, C))
    kept_ref[ITERS - 1, 3] = jnp.zeros((GS, C), F32)
    kept_ref[ITERS - 1, 4] = jnp.zeros((GS, C), F32)
    white_high, white_low = spread_split(whitener, same)
    mean_wide = jnp.broadcast_to(mean, (8, C))
    rounded = white_high.astype(F32) + white_low.astype(F32)
    offset = jnp.dot(mean_wide, rounded, precision=lax.Precision.HIGHEST)[0:1]
    kept_ref[ITERS - 1, 3, 0:8] = mean_wide

    def row(r, carry):
        gain_sum, bias_sum, products = carry
        x = x_ref[r]
        white = dot(x, white_high) + dot(x, white_low) - offset
        pre = gain * white + bias
        gate = 0.5 * jnp.tanh(0.5 * pre) + 0.5
        act = pre * gate
        turned_ref[r] = act.T.astype(BF16)
        pre_grad = grad_ref[r] * (gate + act * (1.0 - gate))
        gain_sum = gain_sum + jnp.sum(pre_grad * white, axis=0, keepdims=True)
        bias_sum = bias_sum + jnp.sum(pre_grad, axis=0, keepdims=True)
        high, low = split(pre_grad * gain)
        back_ref[r] = dot(high, white_high) + dot(low, white_high) + dot(high, white_low)
        products = products + lax.dot_general(
            x, jnp.concatenate([high, low], axis=1), (((0,), (0,)), ((), ())), preferred_element_type=F32
        )
        return gain_sum, bias_sum, products

    nothing = jnp.zeros((1, C), F32)
    gain_sum, bias_sum, products = lax.fori_loop(0, rows, row, (nothing, nothing, jnp.zeros((C, 2 * C), F32)))
    mean_column = jnp.broadcast_to(mean, (C, C)).T
    full = products[:, :C] + products[:, C:] - mean_column * (gain * bias_sum)
    sums_ref[0:GS] = fold(full + full.T, same)
    line = lax.broadcasted_iota(jnp.int32, (8, C), 0)
    sums_ref[GS : GS + 8] = jnp.where(line == 0, gain_sum, jnp.where(line == 1, bias_sum, 0.0))


def tap_kernel(turned_ref, moved_ref, out_ref, total_ref):
    rows = turned_ref.shape[0]
    d = DILATION_RATE
    total_ref[...] = jnp.zeros_like(total_ref)

    def row(r, carry):
        turned = turned_ref[r]
        for a in range(3):
            for b in range(3):
                total_ref[3 * a + b] += dot(turned, moved_ref[b, r + (2 - a) * d])
        return carry

    lax.fori_loop(0, rows, row, 0)
    same = same_group()
    for tap in range(9):
        out_ref[tap] = fold(total_ref[tap], same)


def final_kernel(cell_count, x_ref, back_ref, sums_ref, kept_ref, gain_ref, out_ref, vector_ref):
    rows = x_ref.shape[0]
    same = same_group()
    eye = unit()
    last = ITERS - 1
    whitener, normed = kept_ref[last, 0], kept_ref[last, 1]
    trace = kept_ref[last, 2, 0:1]
    mean = kept_ref[last, 3, 0:8]
    paired = sums_ref[0:GS]
    step = paired * lax.rsqrt(trace)
    step_wide = spread_split(step, same)
    normed_wide = spread_split(normed, same)
    change = -0.5 * step
    for k in range(ITERS - 1):
        iterate, square = kept_ref[k, 0], kept_ref[k, 1]
        scaled_wide = spread_split(kept_ref[k, 2], same)
        square_scaled_wide = spread_split(kept_ref[k, 3], same)
        moved = times(kept_ref[k, 4], step_wide) + times(change, square_scaled_wide)
        moved = moved + times(iterate, spread_split(times(change, scaled_wide), same))
        moved = moved + times(square, spread_split(times(change, normed_wide), same))
        change = 1.5 * change - 0.5 * moved
    inner = jnp.sum(change * normed + 0.5 * paired * whitener, axis=0, keepdims=True)
    symmetric = (change - eye * group_total(inner, same)[0:1]) / trace
    high, low = spread_split(symmetric * (1.0 / cell_count), same)
    rounded = high.astype(F32) + low.astype(F32)
    gain_sum, bias_sum = sums_ref[GS : GS + 1], sums_ref[GS + 1 : GS + 2]
    weighted = jnp.broadcast_to(gain_ref[0:1] * bias_sum * (1.0 / cell_count), (8, C))
    constant = jnp.dot(mean, rounded, precision=lax.Precision.HIGHEST)
    constant = constant + jnp.dot(weighted, spread(whitener, same), precision=lax.Precision.HIGHEST)
    constant = constant[0:1]

    def row(r, carry):
        x = x_ref[r]
        out_ref[r] = (dot(x, high) + dot(x, low) + back_ref[r] - constant).astype(BF16)
        return carry

    lax.fori_loop(0, rows, row, 0)
    vector_ref[...] = sums_ref[GS:] * (1.0 / math.sqrt(cell_count))


def stages(axes):
    for axis in axes:
        size = lax.axis_size(axis)
        stride = 1
        while stride < size:
            yield axis, [(i, i ^ stride) for i in range(size)]
            stride *= 2


def neighbours(axis):
    size = lax.axis_size(axis)
    up = [(i, i + 1) for i in range(size - 1)]
    return up, [(j, i) for i, j in up]


def shards(features, upstream, conv_weight, norm_gain, norm_bias):
    mos_n, rows, width, _ = features.shape
    axes = ("dp", "cols", "rows")
    cell_count = mos_n * rows * width
    for axis in axes:
        cell_count *= lax.axis_size(axis)
    d = DILATION_RATE
    x = features.reshape(rows, width, C)
    up = upstream.reshape(rows, width, C)
    gain = jnp.broadcast_to(norm_gain[None], (8, C))
    bias = jnp.broadcast_to(norm_bias[None], (8, C))

    forward, backward = neighbours("rows")
    top = lax.ppermute(up[rows - d :], "rows", forward)
    bottom = lax.ppermute(up[:d], "rows", backward)

    stats = run(stats_kernel, jax.ShapeDtypeStruct((2 * GS + 8, C), F32), (x,), flops=10**9)

    forward, backward = neighbours("cols")
    tall = lambda first, stop: jnp.concatenate([part[:, first:stop] for part in (top, up, bottom)], axis=0)
    left = lax.ppermute(tall(width - d, width), "cols", forward)
    right = lax.ppermute(tall(0, d), "cols", backward)

    for axis, pairs in stages(axes):
        other = lax.ppermute(stats, axis, pairs)
        stats = run(merge_kernel, jax.ShapeDtypeStruct(stats.shape, F32), (stats, other))

    moved, act_grad = run(
        conv_kernel,
        (
            jax.ShapeDtypeStruct((3, rows + 2 * d, width, C), BF16),
            jax.ShapeDtypeStruct((rows, width, C), F32),
        ),
        (up, top, bottom, left, right, conv_weight.reshape(9, GS, C)),
        scratch=(pltpu.VMEM((width + 32, C), F32), pltpu.VMEM((9, C, C), BF16)),
        flops=3 * 10**9,
    )
    turned, back, sums, kept = run(
        main_kernel,
        (
            jax.ShapeDtypeStruct((rows, C, width), BF16),
            jax.ShapeDtypeStruct((rows, width, C), F32),
            jax.ShapeDtypeStruct((GS + 8, C), F32),
            jax.ShapeDtypeStruct((ITERS, 5, GS, C), F32),
        ),
        (x, stats, gain, bias, act_grad),
        flops=3 * 10**9,
    )
    taps = run(
        tap_kernel,
        jax.ShapeDtypeStruct((9, GS, C), F32),
        (turned, moved),
        scratch=(pltpu.VMEM((9, C, C), F32),),
        flops=3 * 10**9,
    )
    for axis, pairs in stages(axes):
        sums = sums + lax.ppermute(sums, axis, pairs)
    for axis, pairs in stages(axes):
        taps = taps + lax.ppermute(taps, axis, pairs)
    input_grad, vectors = run(
        functools.partial(final_kernel, cell_count),
        (jax.ShapeDtypeStruct((rows, width, C), BF16), jax.ShapeDtypeStruct((8, C), F32)),
        (x, back, sums, kept, gain),
        flops=10**9,
    )
    return (
        input_grad.reshape(features.shape),
        (taps * (1.0 / math.sqrt(cell_count))).reshape(3, 3, GS, C),
        vectors[0],
        vectors[1],
    )


def solution(mesh):
    placed = (P("dp", "rows", "cols", None), P("dp", "rows", "cols", None), P(), P(), P())
    return jax.shard_map(
        shards,
        mesh=mesh,
        in_specs=placed,
        out_specs=(P("dp", "rows", "cols", None), P(), P(), P()),
        check_vma=False,
    )
```

```python
import functools
import math

import jax
import jax.numpy as jnp
from jax import lax
from jax.experimental import pallas as pl
from jax.experimental.pallas import tpu as pltpu
from jax.sharding import PartitionSpec as P

C = 256
CHANNEL_GROUPS = 8
GS = 32
DILATION_RATE = 6
ITERS = 5
EPSILON = 1e-05

F32 = jnp.float32
BF16 = jnp.bfloat16
VMEM_SPEC = pl.BlockSpec(memory_space=pltpu.VMEM)


def run(body, out_shapes, operands, scratch=(), limit=32, flops=0):
    many = isinstance(out_shapes, (tuple, list))
    return pl.pallas_call(
        body,
        out_shape=out_shapes,
        in_specs=[VMEM_SPEC] * len(operands),
        out_specs=[VMEM_SPEC] * len(out_shapes) if many else VMEM_SPEC,
        scratch_shapes=list(scratch),
        compiler_params=pltpu.CompilerParams(vmem_limit_bytes=limit * 2**20),
        cost_estimate=pl.CostEstimate(flops=flops, bytes_accessed=2**20, transcendentals=0),
    )(*operands)


def same_group():
    rows = lax.broadcasted_iota(jnp.int32, (C, C), 0)
    columns = lax.broadcasted_iota(jnp.int32, (C, C), 1)
    return (rows >> 5) == (columns >> 5)


def fold(full, same):
    kept = jnp.where(same, full, 0.0)
    total = kept[0:GS]
    for g in range(1, CHANNEL_GROUPS):
        total = total + kept[g * GS : (g + 1) * GS]
    return total


def spread(packed, same):
    return jnp.where(same, jnp.concatenate([packed] * CHANNEL_GROUPS, axis=0), 0)


def split(value):
    high = value.astype(BF16)
    low = (value - high.astype(F32)).astype(BF16)
    return high, low


def spread_split(packed, same):
    high, low = split(spread(packed, same))
    return high, low


def dot(a, b):
    return jnp.dot(a, b, preferred_element_type=F32)


def times(left, right):
    rows = left.shape[0]
    left_high, left_low = split(left)
    right_high, right_low = right
    both = dot(jnp.concatenate([left_high, left_low], axis=0), right_high)
    return both[:rows] + both[rows:] + dot(left_high, right_low)


def unit():
    rows = lax.broadcasted_iota(jnp.int32, (GS, C), 0)
    columns = lax.broadcasted_iota(jnp.int32, (GS, C), 1)
    return jnp.where(rows == (columns & (GS - 1)), 1.0, 0.0)


def group_total(row, same):
    wide = jnp.broadcast_to(row, (8, C))
    return jnp.dot(wide, jnp.where(same, 1.0, 0.0), precision=lax.Precision.HIGHEST)


def stats_kernel(x_ref, out_ref):
    rows = x_ref.shape[0]
    cells = rows * x_ref.shape[1]
    same = same_group()

    def add_up(r, total):
        return total + jnp.sum(x_ref[r].astype(F32), axis=0, keepdims=True)

    mean = lax.fori_loop(0, rows, add_up, jnp.zeros((1, C), F32)) / cells

    def products(r, total):
        high, low = split(x_ref[r].astype(F32) - mean)
        return total + lax.dot_general(
            high,
            jnp.concatenate([high, low], axis=1),
            (((0,), (0,)), ((), ())),
            preferred_element_type=F32,
        )

    total = lax.fori_loop(0, rows, products, jnp.zeros((C, 2 * C), F32))
    cross = total[:, C:]
    out_ref[0:GS] = fold(total[:, :C] + cross + cross.T, same) / cells
    out_ref[GS : 2 * GS] = fold(jnp.broadcast_to(mean, (C, C)).T, same)
    out_ref[2 * GS : 2 * GS + 8] = jnp.broadcast_to(mean, (8, C))


def merge_kernel(a_ref, b_ref, out_ref):
    a, b = a_ref[...], b_ref[...]
    half = 0.5 * (a + b)
    gap = b - a
    wide = jnp.concatenate([gap[2 * GS :]] * (GS // 8), axis=0)
    out_ref[0:GS] = half[0:GS] + 0.25 * gap[GS : 2 * GS] * wide
    out_ref[GS:] = half[GS:]


def shift_band(moved_ref, bands_ref, e, middle, left, right):
    d, pad, width = DILATION_RATE, 16, middle.shape[0]
    bands_ref[pad : pad + width] = middle.astype(F32)
    bands_ref[pad - 8 : pad] = left.astype(F32)
    bands_ref[pad + width : pad + width + 8] = right.astype(F32)
    moved_ref[0, e] = bands_ref[pad + d : pad + d + width].astype(BF16)
    moved_ref[1, e] = middle
    moved_ref[2, e] = bands_ref[pad - d : pad - d + width].astype(BF16)


def tap_rows(moved_ref, weight_ref, taps):
    bands = [moved_ref[b, band] for a, band in taps for b in range(3)]
    taps = [a for a, _ in taps]
    weights = [weight_ref[3 * a + b] for a in taps for b in range(3)]
    return dot(jnp.concatenate(bands, axis=1), jnp.concatenate(weights, axis=0))


def near_kernel(up_ref, left_ref, right_ref, w_ref, moved_ref, out_ref, weight_ref, bands_ref):
    rows, width = up_ref.shape[0], up_ref.shape[1]
    d = DILATION_RATE
    same = same_group()
    for tap in range(9):
        tile = jnp.concatenate([w_ref[tap].astype(F32)] * CHANNEL_GROUPS, axis=0)
        weight_ref[tap] = jnp.where(same, tile, 0.0).T.astype(BF16)

    def inner(r, carry):
        shift_band(moved_ref, bands_ref, r, up_ref[r], left_ref[r], right_ref[r])
        return carry

    lax.fori_loop(0, rows, inner, 0)
    for first, last, taps in ((0, rows - d, {0: d, 1: 0}), (rows - d, d, {1: 0}), (d, rows, {1: 0, 2: -d})):

        def row(r, carry, taps=taps):
            out_ref[r] = tap_rows(moved_ref, weight_ref, [(a, r + step) for a, step in taps.items()])
            return carry

        lax.fori_loop(first, last, row, 0)


def far_kernel(top_ref, bottom_ref, weight_ref, near_ref, moved_ref, out_ref, bands_ref):
    rows, width = out_ref.shape[0], out_ref.shape[1]
    d = DILATION_RATE

    def outer(r, carry):
        for first, halo in ((0, top_ref), (d, bottom_ref)):
            shift_band(
                moved_ref, bands_ref, first + r,
                halo[r, 0:width], halo[r, width : width + 8], halo[r, width + 8 :],
            )
        return carry

    lax.fori_loop(0, d, outer, 0)
    back = 2 * d - rows
    for first, last, taps in ((0, rows - d, {2: 0}), (rows - d, d, {0: back, 2: 0}), (d, rows, {0: back})):

        def row(r, carry, taps=taps):
            far = tap_rows(moved_ref, weight_ref, [(a, r + step) for a, step in taps.items()])
            out_ref[r] = near_ref[r] + far
            return carry

        lax.fori_loop(first, last, row, 0)


def act_kernel(x_ref, stats_ref, gain_ref, bias_ref, turned_ref, white_ref, slope_ref, kept_ref):
    rows, width = x_ref.shape[0], x_ref.shape[1]
    same = same_group()
    eye = unit()
    gain, bias = gain_ref[0:1], bias_ref[0:1]
    mean = stats_ref[2 * GS : 2 * GS + 1]
    cov = stats_ref[0:GS] + EPSILON * eye
    trace = group_total(jnp.sum(cov * eye, axis=0, keepdims=True), same)[0:1]
    normed = cov / trace
    normed_wide = spread_split(normed, same)
    iterate = 1.5 * eye - 0.5 * normed
    for k in range(ITERS - 1):
        wide = spread_split(iterate, same)
        square = times(iterate, wide)
        scaled = times(iterate, normed_wide)
        scaled_wide = spread_split(scaled, same)
        cube_scaled = times(square, scaled_wide)
        kept_ref[k, 0] = iterate
        kept_ref[k, 1] = square
        kept_ref[k, 2] = scaled
        kept_ref[k, 3] = times(iterate, scaled_wide)
        kept_ref[k, 4] = times(square, wide)
        iterate = 1.5 * iterate - 0.5 * cube_scaled
    whitener = iterate * lax.rsqrt(trace)
    mean_wide = jnp.broadcast_to(mean, (8, C))
    kept_ref[ITERS - 1, 0] = whitener
    kept_ref[ITERS - 1, 1] = normed
    kept_ref[ITERS - 1, 2] = jnp.broadcast_to(trace, (GS, C))
    kept_ref[ITERS - 1, 3] = jnp.broadcast_to(mean, (GS, C))
    kept_ref[ITERS - 1, 4] = jnp.zeros((GS, C), F32)
    white_high, white_low = spread_split(whitener, same)
    rounded = white_high.astype(F32) + white_low.astype(F32)
    offset = jnp.dot(mean_wide, rounded, precision=lax.Precision.HIGHEST)[0:1]

    for r in range(rows):
        x = x_ref[r]
        white = dot(x, white_high) + dot(x, white_low) - offset
        pre = gain * white + bias
        gate = 0.5 * jnp.tanh(0.5 * pre) + 0.5
        act = pre * gate
        turned_ref[:, r * width : (r + 1) * width] = act.T.astype(BF16)
        white_ref[r] = white
        slope_ref[r] = gate + act * (1.0 - gate)


def tap_kernel(turned_ref, near_ref, far_ref, out_ref):
    rows, width = near_ref.shape[1], near_ref.shape[2]
    d = DILATION_RATE
    gap = rows - d
    same = same_group()

    def pair(b, first, count, ref, band):
        turned = turned_ref[:, first * width : (first + count) * width]
        return dot(turned, ref[b, band : band + count].reshape(count * width, C))

    def column(b, carry):
        out_ref[b] = fold(pair(b, 0, gap, near_ref, d) + pair(b, gap, d, far_ref, d), same)
        out_ref[3 + b] = fold(pair(b, 0, rows, near_ref, 0), same)
        out_ref[6 + b] = fold(pair(b, 0, d, far_ref, 0) + pair(b, d, gap, near_ref, 0), same)
        return carry

    lax.fori_loop(0, 3, column, 0)


def grad_kernel(x_ref, grad_ref, white_ref, slope_ref, kept_ref, gain_ref, back_ref, sums_ref):
    rows = x_ref.shape[0]
    same = same_group()
    gain = gain_ref[0:1]
    mean = kept_ref[ITERS - 1, 3, 0:1]
    white_high, white_low = spread_split(kept_ref[ITERS - 1, 0], same)

    def row(r, carry):
        gain_sum, bias_sum, products = carry
        pre_grad = grad_ref[r] * slope_ref[r]
        gain_sum = gain_sum + jnp.sum(pre_grad * white_ref[r], axis=0, keepdims=True)
        bias_sum = bias_sum + jnp.sum(pre_grad, axis=0, keepdims=True)
        high, low = split(pre_grad * gain)
        back_ref[r] = dot(high, white_high) + dot(low, white_high) + dot(high, white_low)
        products = products + lax.dot_general(
            x_ref[r], jnp.concatenate([high, low], axis=1), (((0,), (0,)), ((), ())), preferred_element_type=F32
        )
        return gain_sum, bias_sum, products

    nothing = jnp.zeros((1, C), F32)
    gain_sum, bias_sum, products = lax.fori_loop(0, rows, row, (nothing, nothing, jnp.zeros((C, 2 * C), F32)))
    mean_column = jnp.broadcast_to(mean, (C, C)).T
    full = products[:, :C] + products[:, C:] - mean_column * (gain * bias_sum)
    sums_ref[0:GS] = fold(full + full.T, same)
    line = lax.broadcasted_iota(jnp.int32, (8, C), 0)
    sums_ref[GS : GS + 8] = jnp.where(line == 0, gain_sum, jnp.where(line == 1, bias_sum, 0.0))


def final_kernel(cell_count, x_ref, back_ref, sums_ref, kept_ref, gain_ref, out_ref, vector_ref):
    rows = x_ref.shape[0]
    same = same_group()
    eye = unit()
    last = ITERS - 1
    whitener, normed = kept_ref[last, 0], kept_ref[last, 1]
    trace = kept_ref[last, 2, 0:1]
    mean = kept_ref[last, 3, 0:8]
    paired = sums_ref[0:GS]
    step = paired * lax.rsqrt(trace)
    step_wide = spread_split(step, same)
    normed_wide = spread_split(normed, same)
    change = -0.5 * step
    for k in range(ITERS - 1):
        iterate, square = kept_ref[k, 0], kept_ref[k, 1]
        scaled_wide = spread_split(kept_ref[k, 2], same)
        square_scaled_wide = spread_split(kept_ref[k, 3], same)
        moved = times(kept_ref[k, 4], step_wide) + times(change, square_scaled_wide)
        moved = moved + times(iterate, spread_split(times(change, scaled_wide), same))
        moved = moved + times(square, spread_split(times(change, normed_wide), same))
        change = 1.5 * change - 0.5 * moved
    inner = jnp.sum(change * normed + 0.5 * paired * whitener, axis=0, keepdims=True)
    symmetric = (change - eye * group_total(inner, same)[0:1]) / trace
    high, low = spread_split(symmetric * (1.0 / cell_count), same)
    rounded = high.astype(F32) + low.astype(F32)
    bias_sum = sums_ref[GS + 1 : GS + 2]
    weighted = jnp.broadcast_to(gain_ref[0:1] * bias_sum * (1.0 / cell_count), (8, C))
    constant = jnp.dot(mean, rounded, precision=lax.Precision.HIGHEST)
    constant = constant + jnp.dot(weighted, spread(whitener, same), precision=lax.Precision.HIGHEST)
    constant = constant[0:1]

    def row(r, carry):
        x = x_ref[r]
        out_ref[r] = (dot(x, high) + dot(x, low) + back_ref[r] - constant).astype(BF16)
        return carry

    lax.fori_loop(0, rows, row, 0)
    vector_ref[...] = sums_ref[GS:] * (1.0 / math.sqrt(cell_count))


def stages(axes):
    for axis in axes:
        size = lax.axis_size(axis)
        stride = 1
        while stride < size:
            yield axis, [(i, i ^ stride) for i in range(size)]
            stride *= 2


def add_over(part, pairs_of):
    for axis, pairs in pairs_of:
        part = part + lax.ppermute(part, axis, pairs)
    return part


def add_taps(taps, pairs_of):
    (axis, pairs), rest = pairs_of[0], pairs_of[1:]
    odd = lax.axis_index(axis) % 2
    halves = taps.reshape(2, -1, C)
    own = lax.dynamic_index_in_dim(halves, odd, 0, False)
    own = own + lax.ppermute(lax.dynamic_index_in_dim(halves, 1 - odd, 0, False), axis, pairs)
    own = add_over(own, rest)
    other = lax.ppermute(own, axis, pairs)
    return jnp.where(odd == 0, jnp.stack([own, other]), jnp.stack([other, own])).reshape(taps.shape)


def neighbours(axis):
    size = lax.axis_size(axis)
    up = [(i, i + 1) for i in range(size - 1)]
    return up, [(j, i) for i, j in up]


def column_halo(up):
    first, last = up[:, :8], up[:, -8:]
    if lax.axis_size("cols") == 2:
        place = lax.axis_index("cols")
        other = lax.ppermute(jnp.where(place == 0, last, first), "cols", [(0, 1), (1, 0)])
        nothing = jnp.zeros_like(other)
        return jnp.where(place == 1, other, nothing), jnp.where(place == 0, other, nothing)
    forward, backward = neighbours("cols")
    return lax.ppermute(last, "cols", forward), lax.ppermute(first, "cols", backward)


def shards(features, upstream, conv_weight, norm_gain, norm_bias):
    mos_n, rows, width, _ = features.shape
    axes = ("dp", "cols", "rows")
    cell_count = mos_n * rows * width
    for axis in axes:
        cell_count *= lax.axis_size(axis)
    pairs_of = list(stages(axes))
    d = DILATION_RATE
    x = features.reshape(rows, width, C)
    up = upstream.reshape(rows, width, C)
    gain = jnp.broadcast_to(norm_gain[None], (8, C))
    bias = jnp.broadcast_to(norm_bias[None], (8, C))
    shape = jax.ShapeDtypeStruct
    cells = (rows, width, C)

    left, right = column_halo(up)
    longer = lambda part: jnp.concatenate([up[part], left[part], right[part]], axis=1)
    forward, backward = neighbours("rows")
    top = lax.ppermute(longer(slice(rows - d, rows)), "rows", forward)
    bottom = lax.ppermute(longer(slice(0, d)), "rows", backward)

    stats = run(stats_kernel, shape((2 * GS + 8, C), F32), (x,), flops=10**9)
    for axis, pairs in pairs_of:
        other = lax.ppermute(stats, axis, pairs)
        stats = run(merge_kernel, shape(stats.shape, F32), (stats, other))

    bands = (pltpu.VMEM((width + 32, C), F32),)
    near_bands, near_grad, weights = run(
        near_kernel,
        (shape((3,) + cells, BF16), shape(cells, F32), shape((9, C, C), BF16)),
        (up, left, right, conv_weight.reshape(9, GS, C)),
        scratch=bands,
        flops=2 * 10**9,
    )
    far_bands, act_grad = run(
        far_kernel,
        (shape((3, 2 * d, width, C), BF16), shape(cells, F32)),
        (top, bottom, weights, near_grad),
        scratch=bands,
        flops=2 * 10**9,
    )
    turned, white, slope, kept = run(
        act_kernel,
        (shape((C, rows * width), BF16), shape(cells, F32), shape(cells, F32), shape((ITERS, 5, GS, C), F32)),
        (x, stats, gain, bias),
        flops=3 * 10**9,
    )
    taps = run(tap_kernel, shape((9, GS, C), F32), (turned, near_bands, far_bands), flops=3 * 10**9)
    back, sums = run(
        grad_kernel,
        (shape(cells, F32), shape((GS + 8, C), F32)),
        (x, act_grad, white, slope, kept, gain),
        flops=3 * 10**9,
    )
    sums = add_over(sums, pairs_of)
    taps = add_taps(taps, pairs_of)
    input_grad, vectors = run(
        functools.partial(final_kernel, cell_count),
        (shape(cells, BF16), shape((8, C), F32)),
        (x, back, sums, kept, gain),
        flops=10**9,
    )
    return (
        input_grad.reshape(features.shape),
        (taps * (1.0 / math.sqrt(cell_count))).reshape(3, 3, GS, C),
        vectors[0],
        vectors[1],
    )


def solution(mesh):
    placed = (P("dp", "rows", "cols", None), P("dp", "rows", "cols", None), P(), P(), P())
    return jax.shard_map(
        shards,
        mesh=mesh,
        in_specs=placed,
        out_specs=(P("dp", "rows", "cols", None), P(), P(), P()),
        check_vma=False,
    )
```

```python
import functools
import math

import jax
import jax.numpy as jnp
from jax import lax
from jax.experimental import pallas as pl
from jax.experimental.pallas import tpu as pltpu
from jax.sharding import PartitionSpec as P

C = 256
CHANNEL_GROUPS = 8
GS = 32
DILATION_RATE = 6
ITERS = 5
EPSILON = 1e-05

F32 = jnp.float32
BF16 = jnp.bfloat16
VMEM_SPEC = pl.BlockSpec(memory_space=pltpu.VMEM)


def run(body, out_shapes, operands, scratch=(), flops=0, after=()):
    many = isinstance(out_shapes, (tuple, list))
    count = len(operands)

    def kernel(*refs):
        body(*refs[:count], *refs[count + len(after) :])

    return pl.pallas_call(
        kernel,
        out_shape=out_shapes,
        in_specs=[VMEM_SPEC] * count + [pl.BlockSpec(memory_space=pl.ANY)] * len(after),
        out_specs=[VMEM_SPEC] * len(out_shapes) if many else VMEM_SPEC,
        scratch_shapes=list(scratch),
        compiler_params=pltpu.CompilerParams(vmem_limit_bytes=8 * 2**20),
        cost_estimate=pl.CostEstimate(flops=flops, bytes_accessed=2**20, transcendentals=0),
    )(*operands, *after)


TOKEN = jax.ShapeDtypeStruct((8, 128), F32)


def leave(token_ref):
    token_ref[...] = jnp.zeros(token_ref.shape, F32)


def same_group():
    rows = lax.broadcasted_iota(jnp.int32, (C, C), 0)
    columns = lax.broadcasted_iota(jnp.int32, (C, C), 1)
    return (rows >> 5) == (columns >> 5)


def fold(full, same):
    kept = jnp.where(same, full, 0.0)
    total = kept[0:GS]
    for g in range(1, CHANNEL_GROUPS):
        total = total + kept[g * GS : (g + 1) * GS]
    return total


def spread(packed, same):
    return jnp.where(same, jnp.concatenate([packed] * CHANNEL_GROUPS, axis=0), 0)


def split(value):
    high = value.astype(BF16)
    low = (value - high.astype(F32)).astype(BF16)
    return high, low


def spread_split(packed, same):
    high, low = split(spread(packed, same))
    return high, low


def dot(a, b):
    return jnp.dot(a, b, preferred_element_type=F32)


def times(left, right):
    rows = left.shape[0]
    left_high, left_low = split(left)
    right_high, right_low = right
    both = dot(jnp.concatenate([left_high, left_low], axis=0), right_high)
    return both[:rows] + both[rows:] + dot(left_high, right_low)


def unit():
    rows = lax.broadcasted_iota(jnp.int32, (GS, C), 0)
    columns = lax.broadcasted_iota(jnp.int32, (GS, C), 1)
    return jnp.where(rows == (columns & (GS - 1)), 1.0, 0.0)


def group_total(row, same):
    wide = jnp.broadcast_to(row, (8, C))
    return jnp.dot(wide, jnp.where(same, 1.0, 0.0), precision=lax.Precision.HIGHEST)


def stats_kernel(x_ref, out_ref):
    rows = x_ref.shape[0]
    cells = rows * x_ref.shape[1]
    same = same_group()

    def add_up(r, total):
        return total + jnp.sum(x_ref[r].astype(F32), axis=0, keepdims=True)

    mean = lax.fori_loop(0, rows, add_up, jnp.zeros((1, C), F32)) / cells

    def products(r, total):
        high, low = split(x_ref[r].astype(F32) - mean)
        return total + lax.dot_general(
            high,
            jnp.concatenate([high, low], axis=1),
            (((0,), (0,)), ((), ())),
            preferred_element_type=F32,
        )

    total = lax.fori_loop(0, rows, products, jnp.zeros((C, 2 * C), F32))
    cross = total[:, C:]
    out_ref[0:GS] = fold(total[:, :C] + cross + cross.T, same) / cells
    out_ref[GS : 2 * GS] = fold(jnp.broadcast_to(mean, (C, C)).T, same)
    out_ref[2 * GS : 2 * GS + 8] = jnp.broadcast_to(mean, (8, C))


def merge_kernel(a_ref, b_ref, out_ref):
    a, b = a_ref[...], b_ref[...]
    half = 0.5 * (a + b)
    gap = b - a
    wide = jnp.concatenate([gap[2 * GS :]] * (GS // 8), axis=0)
    out_ref[0:GS] = half[0:GS] + 0.25 * gap[GS : 2 * GS] * wide
    out_ref[GS:] = half[GS:]


def add_kernel(a_ref, b_ref, out_ref):
    out_ref[...] = a_ref[...] + b_ref[...]


def shift_band(moved_ref, bands_ref, e, middle, left, right):
    d, pad, width = DILATION_RATE, 16, middle.shape[0]
    bands_ref[pad : pad + width] = middle.astype(F32)
    bands_ref[pad - 8 : pad] = left.astype(F32)
    bands_ref[pad + width : pad + width + 8] = right.astype(F32)
    moved_ref[0, e] = bands_ref[pad + d : pad + d + width].astype(BF16)
    moved_ref[1, e] = middle
    moved_ref[2, e] = bands_ref[pad - d : pad - d + width].astype(BF16)


def tap_rows(moved_ref, weight_ref, taps):
    bands = [moved_ref[b, band] for a, band in taps for b in range(3)]
    taps = [a for a, _ in taps]
    weights = [weight_ref[3 * a + b] for a in taps for b in range(3)]
    return dot(jnp.concatenate(bands, axis=1), jnp.concatenate(weights, axis=0))


def pack_kernel(up_ref, left_ref, right_ref, odd_ref, first_ref, second_ref):
    rows, width = up_ref.shape[0], up_ref.shape[1]
    d = DILATION_RATE
    odd = odd_ref[0:1] > 0.5
    for r in range(d):
        for begin, size, ref in ((0, width, up_ref), (width, 8, left_ref), (width + 8, 8, right_ref)):
            top, bottom = ref[r].astype(F32), ref[rows - d + r].astype(F32)
            first_ref[r, begin : begin + size] = jnp.where(odd, top, bottom).astype(BF16)
            second_ref[r, begin : begin + size] = jnp.where(odd, bottom, top).astype(BF16)


def bands_kernel(up_ref, left_ref, right_ref, w_ref, moved_ref, weight_ref, token_ref, bands_ref):
    rows = up_ref.shape[0]
    same = same_group()
    for tap in range(9):
        tile = jnp.concatenate([w_ref[tap].astype(F32)] * CHANNEL_GROUPS, axis=0)
        weight_ref[tap] = jnp.where(same, tile, 0.0).T.astype(BF16)

    def inner(r, carry):
        shift_band(moved_ref, bands_ref, r, up_ref[r], left_ref[r], right_ref[r])
        return carry

    lax.fori_loop(0, rows, inner, 0)
    leave(token_ref)


def near_kernel(moved_ref, weight_ref, out_ref, token_ref):
    rows = out_ref.shape[0]
    d = DILATION_RATE
    for first, last, taps in ((0, rows - d, {0: d, 1: 0}), (rows - d, d, {1: 0}), (d, rows, {1: 0, 2: -d})):

        def row(r, carry, taps=taps):
            out_ref[r] = tap_rows(moved_ref, weight_ref, [(a, r + step) for a, step in taps.items()])
            return carry

        lax.fori_loop(first, last, row, 0)
    leave(token_ref)


def far_kernel(even_ref, odd_ref, first_ref, second_ref, weight_ref, near_ref, moved_ref, out_ref, token_ref, bands_ref):
    rows, width = out_ref.shape[0], out_ref.shape[1]
    d = DILATION_RATE

    def outer(r, carry):
        first, second = first_ref[r], second_ref[r]
        for begin, place in ((0, odd_ref), (d, even_ref)):
            halo = jnp.where(place[0:1] > 0.5, first.astype(F32), second.astype(F32)).astype(BF16)
            shift_band(
                moved_ref, bands_ref, begin + r, halo[0:width], halo[width : width + 8], halo[width + 8 :]
            )
        return carry

    lax.fori_loop(0, d, outer, 0)
    back = 2 * d - rows
    for first, last, taps in ((0, rows - d, {2: 0}), (rows - d, d, {0: back, 2: 0}), (d, rows, {0: back})):

        def row(r, carry, taps=taps):
            far = tap_rows(moved_ref, weight_ref, [(a, r + step) for a, step in taps.items()])
            out_ref[r] = near_ref[r] + far
            return carry

        lax.fori_loop(first, last, row, 0)
    leave(token_ref)


def act_kernel(x_ref, stats_ref, gain_ref, bias_ref, turned_ref, white_ref, slope_ref, kept_ref, mean_ref):
    rows, width = x_ref.shape[0], x_ref.shape[1]
    same = same_group()
    eye = unit()
    gain, bias = gain_ref[0:1], bias_ref[0:1]
    mean = stats_ref[2 * GS : 2 * GS + 1]
    cov = stats_ref[0:GS] + EPSILON * eye
    trace = group_total(jnp.sum(cov * eye, axis=0, keepdims=True), same)[0:1]
    normed = cov / trace
    normed_wide = spread_split(normed, same)
    iterate = 1.5 * eye - 0.5 * normed
    for k in range(ITERS - 1):
        wide = spread_split(iterate, same)
        square = times(iterate, wide)
        scaled = times(iterate, normed_wide)
        scaled_wide = spread_split(scaled, same)
        cube_scaled = times(square, scaled_wide)
        kept_ref[k, 0] = iterate
        kept_ref[k, 1] = square
        kept_ref[k, 2] = scaled
        iterate = 1.5 * iterate - 0.5 * cube_scaled
    whitener = iterate * lax.rsqrt(trace)
    mean_wide = jnp.broadcast_to(mean, (8, C))
    kept_ref[ITERS - 1, 0] = whitener
    kept_ref[ITERS - 1, 1] = normed
    kept_ref[ITERS - 1, 2] = jnp.broadcast_to(trace, (GS, C))
    mean_ref[...] = mean_wide
    white_high, white_low = spread_split(whitener, same)
    rounded = white_high.astype(F32) + white_low.astype(F32)
    offset = jnp.dot(mean_wide, rounded, precision=lax.Precision.HIGHEST)[0:1]

    for r in range(rows):
        x = x_ref[r]
        white = dot(x, white_high) + dot(x, white_low) - offset
        pre = gain * white + bias
        gate = 0.5 * jnp.tanh(0.5 * pre) + 0.5
        act = pre * gate
        turned_ref[:, r * width : (r + 1) * width] = act.T.astype(BF16)
        white_ref[r] = white
        slope_ref[r] = gate + act * (1.0 - gate)


def tap_kernel(turned_ref, near_ref, far_ref, out_ref):
    rows, width = near_ref.shape[1], near_ref.shape[2]
    d = DILATION_RATE
    gap = rows - d
    same = same_group()

    def pair(b, first, count, ref, band):
        turned = turned_ref[:, first * width : (first + count) * width]
        return dot(turned, ref[b, band : band + count].reshape(count * width, C))

    def column(b, carry):
        out_ref[b] = fold(pair(b, 0, gap, near_ref, d) + pair(b, gap, d, far_ref, d), same)
        out_ref[3 + b] = fold(pair(b, 0, rows, near_ref, 0), same)
        out_ref[6 + b] = fold(pair(b, 0, d, far_ref, 0) + pair(b, d, gap, near_ref, 0), same)
        return carry

    lax.fori_loop(0, 3, column, 0)


def grad_kernel(x_ref, grad_ref, white_ref, slope_ref, kept_ref, mean_ref, gain_ref, back_ref, sums_ref):
    rows = x_ref.shape[0]
    same = same_group()
    gain = gain_ref[0:1]
    mean = mean_ref[0:1]
    white_high, white_low = spread_split(kept_ref[ITERS - 1, 0], same)

    def row(r, carry):
        gain_sum, bias_sum, products = carry
        pre_grad = grad_ref[r] * slope_ref[r]
        gain_sum = gain_sum + jnp.sum(pre_grad * white_ref[r], axis=0, keepdims=True)
        bias_sum = bias_sum + jnp.sum(pre_grad, axis=0, keepdims=True)
        high, low = split(pre_grad * gain)
        back_ref[r] = dot(high, white_high) + dot(low, white_high) + dot(high, white_low)
        products = products + lax.dot_general(
            x_ref[r], jnp.concatenate([high, low], axis=1), (((0,), (0,)), ((), ())), preferred_element_type=F32
        )
        return gain_sum, bias_sum, products

    nothing = jnp.zeros((1, C), F32)
    gain_sum, bias_sum, products = lax.fori_loop(0, rows, row, (nothing, nothing, jnp.zeros((C, 2 * C), F32)))
    mean_column = jnp.broadcast_to(mean, (C, C)).T
    full = products[:, :C] + products[:, C:] - mean_column * (gain * bias_sum)
    sums_ref[0:GS] = fold(full + full.T, same)
    line = lax.broadcasted_iota(jnp.int32, (8, C), 0)
    sums_ref[GS : GS + 8] = jnp.where(line == 0, gain_sum, jnp.where(line == 1, bias_sum, 0.0))


def prepare_kernel(kept_ref, wide_ref, cube_ref, token_ref):
    same = same_group()

    def put(place, packed):
        high, low = spread_split(packed, same)
        wide_ref[place, 0] = high
        wide_ref[place, 1] = low

    for k in range(ITERS - 1):
        iterate, square, scaled = kept_ref[k, 0], kept_ref[k, 1], kept_ref[k, 2]
        put(2 * k, scaled)
        put(2 * k + 1, times(iterate, (wide_ref[2 * k, 0], wide_ref[2 * k, 1])))
        cube_ref[k] = times(square, spread_split(iterate, same))
    put(2 * ITERS - 2, kept_ref[ITERS - 1, 1])
    leave(token_ref)


def final_kernel(cell_count, x_ref, back_ref, sums_ref, kept_ref, mean_ref, wide_ref, cube_ref, gain_ref, out_ref, vector_ref):
    rows = x_ref.shape[0]
    same = same_group()
    eye = unit()
    last = ITERS - 1
    whitener, normed = kept_ref[last, 0], kept_ref[last, 1]
    trace = kept_ref[last, 2, 0:1]
    mean = mean_ref[...]
    paired = sums_ref[0:GS]
    step = paired * lax.rsqrt(trace)
    wide = lambda place: (wide_ref[place, 0], wide_ref[place, 1])
    cubes = jnp.concatenate([cube_ref[k] for k in range(ITERS - 1)], axis=0)
    direct = times(cubes, spread_split(step, same))
    change = -0.5 * step
    for k in range(ITERS - 1):
        moved = direct[k * GS : (k + 1) * GS] + times(change, wide(2 * k + 1))
        moved = moved + times(kept_ref[k, 0], spread_split(times(change, wide(2 * k)), same))
        moved = moved + times(kept_ref[k, 1], spread_split(times(change, wide(2 * ITERS - 2)), same))
        change = 1.5 * change - 0.5 * moved
    inner = jnp.sum(change * normed + 0.5 * paired * whitener, axis=0, keepdims=True)
    symmetric = (change - eye * group_total(inner, same)[0:1]) / trace
    high, low = spread_split(symmetric * (1.0 / cell_count), same)
    rounded = high.astype(F32) + low.astype(F32)
    bias_sum = sums_ref[GS + 1 : GS + 2]
    weighted = jnp.broadcast_to(gain_ref[0:1] * bias_sum * (1.0 / cell_count), (8, C))
    constant = jnp.dot(mean, rounded, precision=lax.Precision.HIGHEST)
    constant = constant + jnp.dot(weighted, spread(whitener, same), precision=lax.Precision.HIGHEST)
    constant = constant[0:1]

    def row(r, carry):
        x = x_ref[r]
        out_ref[r] = (dot(x, high) + dot(x, low) + back_ref[r] - constant).astype(BF16)
        return carry

    lax.fori_loop(0, rows, row, 0)
    vector_ref[...] = sums_ref[GS:] * (1.0 / math.sqrt(cell_count))


def stages(axes):
    for axis in axes:
        size = lax.axis_size(axis)
        stride = 1
        while stride < size:
            yield axis, [(i, i ^ stride) for i in range(size)]
            stride *= 2


def add(part, other, after=()):
    return run(add_kernel, jax.ShapeDtypeStruct(part.shape, F32), (part, other), after=after)


def swap(earlier, later, axis):
    size = lax.axis_size(axis)
    got = []
    for begin, part in ((0, earlier), (1, later)):
        pairs = [(i, i + 1) for i in range(begin, size - 1, 2)]
        pairs = pairs + [(j, i) for i, j in pairs]
        got.append(lax.ppermute(part, axis, pairs) if pairs else jnp.zeros_like(part))
    return got


def shards(features, upstream, conv_weight, norm_gain, norm_bias):
    mos_n, rows, width, _ = features.shape
    axes = ("dp", "cols", "rows")
    cell_count = mos_n * rows * width
    for axis in axes:
        cell_count *= lax.axis_size(axis)
    stage_pairs = list(stages(axes))
    count = len(stage_pairs)
    d = DILATION_RATE
    x = features.reshape(rows, width, C)
    up = upstream.reshape(rows, width, C)
    gain = jnp.broadcast_to(norm_gain[None], (8, C))
    bias = jnp.broadcast_to(norm_bias[None], (8, C))
    shape = jax.ShapeDtypeStruct
    cells = (rows, width, C)

    stats = run(stats_kernel, shape((2 * GS + 8, C), F32), (x,), flops=10**9)
    odd = lax.axis_index("cols") % 2 == 1
    first, second = up[:, :8], up[:, -8:]
    first, second = swap(jnp.where(odd, first, second), jnp.where(odd, second, first), "cols")
    left, right = jnp.where(odd, first, second), jnp.where(odd, second, first)
    odd_line = jnp.broadcast_to((lax.axis_index("rows") % 2 == 1).astype(F32), (8, C))
    even_line = 1.0 - odd_line
    halo = shape((d, width + 16, C), BF16)
    first, second = swap(*run(pack_kernel, (halo, halo), (up, left, right, odd_line), after=(stats,)), "rows")
    scratch = (pltpu.VMEM((width + 32, C), F32),)
    for number, (axis, pairs) in enumerate(stage_pairs):
        other = lax.ppermute(stats, axis, pairs)
        token = ()
        if number == 1:
            near_bands, weights, *token = run(
                bands_kernel,
                (shape((3,) + cells, BF16), shape((9, C, C), BF16), TOKEN),
                (up, left, right, conv_weight.reshape(9, GS, C)),
                scratch=scratch,
                flops=10**9,
                after=(stats,),
            )
        if number == 2:
            near_grad, *token = run(
                near_kernel, (shape(cells, F32), TOKEN), (near_bands, weights), flops=10**9, after=(stats,)
            )
        if number == count - 1:
            far_bands, act_grad, *token = run(
                far_kernel,
                (shape((3, 2 * d, width, C), BF16), shape(cells, F32), TOKEN),
                (even_line, odd_line, first, second, weights, near_grad),
                scratch=scratch,
                flops=2 * 10**9,
                after=(stats,),
            )
        stats = run(merge_kernel, shape(stats.shape, F32), (stats, other), after=token)

    turned, white, slope, kept, mean = run(
        act_kernel,
        (
            shape((C, rows * width), BF16),
            shape(cells, F32),
            shape(cells, F32),
            shape((ITERS, 3, GS, C), F32),
            shape((8, C), F32),
        ),
        (x, stats, gain, bias),
        flops=2 * 10**9,
    )
    taps = run(tap_kernel, shape((9, GS, C), F32), (turned, near_bands, far_bands), flops=3 * 10**9)

    tap_axis, tap_pairs = stage_pairs[0]
    later = lax.axis_index(tap_axis) % 2
    halves = taps.reshape(2, -1, C)
    half = lax.dynamic_index_in_dim(halves, later, 0, False)
    half = add(half, lax.ppermute(lax.dynamic_index_in_dim(halves, 1 - later, 0, False), tap_axis, tap_pairs))

    back, sums = run(
        grad_kernel,
        (shape(cells, F32), shape((GS + 8, C), F32)),
        (x, act_grad, white, slope, kept, mean, gain),
        flops=2 * 10**9,
        after=(half,),
    )
    row_stages = [stage for stage in stage_pairs[1:] if stage[0] == "rows"]
    tap_stages = row_stages + [stage for stage in stage_pairs[1:] if stage[0] != "rows"]
    half = add(half, lax.ppermute(half, *tap_stages[0]), after=(sums,))
    for number, stage in enumerate(stage_pairs):
        other = lax.ppermute(sums, *stage)
        token = ()
        if number == 1:
            wide, cubes, *token = run(
                prepare_kernel,
                (shape((2 * ITERS - 1, 2, C, C), BF16), shape((ITERS - 1, GS, C), F32), TOKEN),
                (kept,),
                flops=10**9,
                after=(sums,),
            )
        sums = add(sums, other, after=token)
        if 2 <= number < count:
            last = number == count - 1
            half = add(half, lax.ppermute(half, *tap_stages[number - 1]), after=() if last else (sums,))
    input_grad, vectors = run(
        functools.partial(final_kernel, cell_count),
        (shape(cells, BF16), shape((8, C), F32)),
        (x, back, sums, kept, mean, wide, cubes, gain),
        flops=10**9,
        after=(half,),
    )
    half = half * (1.0 / math.sqrt(cell_count))
    other = lax.ppermute(half, tap_axis, tap_pairs)
    taps = jnp.where(later == 0, jnp.stack([half, other]), jnp.stack([other, half]))
    return (
        input_grad.reshape(features.shape),
        taps.reshape(3, 3, GS, C),
        vectors[0],
        vectors[1],
    )


def solution(mesh):
    placed = (P("dp", "rows", "cols", None), P("dp", "rows", "cols", None), P(), P(), P())
    return jax.shard_map(
        shards,
        mesh=mesh,
        in_specs=placed,
        out_specs=(P("dp", "rows", "cols", None), P(), P(), P()),
        check_vma=False,
    )
```

```python
import functools
import math

import jax
import jax.numpy as jnp
from jax import lax
from jax.experimental import pallas as pl
from jax.experimental.pallas import tpu as pltpu
from jax.sharding import PartitionSpec as P

C = 256
CHANNEL_GROUPS = 8
GS = 32
DILATION_RATE = 6
ITERS = 5
EPSILON = 1e-05

F32 = jnp.float32
BF16 = jnp.bfloat16
VMEM_SPEC = pl.BlockSpec(memory_space=pltpu.VMEM)
NO_COST = pl.CostEstimate(flops=0, bytes_accessed=0, transcendentals=0)


def run(body, out_shapes, operands, scratch=(), after=()):
    many = isinstance(out_shapes, (tuple, list))
    count = len(operands)

    def kernel(*refs):
        body(*refs[:count], *refs[count + len(after) :])

    return pl.pallas_call(
        kernel,
        out_shape=out_shapes,
        in_specs=[VMEM_SPEC] * count + [pl.BlockSpec(memory_space=pl.ANY)] * len(after),
        out_specs=[VMEM_SPEC] * len(out_shapes) if many else VMEM_SPEC,
        scratch_shapes=list(scratch),
        compiler_params=pltpu.CompilerParams(vmem_limit_bytes=8 * 2**20),
        cost_estimate=NO_COST,
    )(*operands, *after)


TOKEN = jax.ShapeDtypeStruct((8, 128), F32)


def leave(token_ref):
    token_ref[...] = jnp.zeros(token_ref.shape, F32)


def same_group():
    rows = lax.broadcasted_iota(jnp.int32, (C, C), 0)
    columns = lax.broadcasted_iota(jnp.int32, (C, C), 1)
    return (rows >> 5) == (columns >> 5)


def fold(full, same):
    kept = jnp.where(same, full, 0.0)
    total = kept[0:GS]
    for g in range(1, CHANNEL_GROUPS):
        total = total + kept[g * GS : (g + 1) * GS]
    return total


def spread(packed, same):
    return jnp.where(same, jnp.concatenate([packed] * CHANNEL_GROUPS, axis=0), 0)


def split(value):
    high = value.astype(BF16)
    low = (value - high.astype(F32)).astype(BF16)
    return high, low


def spread_split(packed, same):
    high, low = split(spread(packed, same))
    return high, low


def dot(a, b):
    return jnp.dot(a, b, preferred_element_type=F32)


def times(left, right):
    rows = left.shape[0]
    left_high, left_low = split(left)
    right_high, right_low = right
    both = dot(jnp.concatenate([left_high, left_low], axis=0), right_high)
    return both[:rows] + both[rows:] + dot(left_high, right_low)


def unit():
    rows = lax.broadcasted_iota(jnp.int32, (GS, C), 0)
    columns = lax.broadcasted_iota(jnp.int32, (GS, C), 1)
    return jnp.where(rows == (columns & (GS - 1)), 1.0, 0.0)


def group_total(row, same):
    wide = jnp.broadcast_to(row, (8, C))
    return jnp.dot(wide, jnp.where(same, 1.0, 0.0), precision=lax.Precision.HIGHEST)


def stats_kernel(x_ref, out_ref):
    rows = x_ref.shape[0]
    cells = rows * x_ref.shape[1]
    same = same_group()

    def add_up(r, total):
        return total + jnp.sum(x_ref[r].astype(F32), axis=0, keepdims=True)

    mean = lax.fori_loop(0, rows, add_up, jnp.zeros((1, C), F32)) / cells

    def products(r, total):
        high, low = split(x_ref[r].astype(F32) - mean)
        return total + lax.dot_general(
            high,
            jnp.concatenate([high, low], axis=1),
            (((0,), (0,)), ((), ())),
            preferred_element_type=F32,
        )

    total = lax.fori_loop(0, rows, products, jnp.zeros((C, 2 * C), F32))
    cross = total[:, C:]
    out_ref[0:GS] = fold(total[:, :C] + cross + cross.T, same) / cells
    out_ref[GS : 2 * GS] = fold(jnp.broadcast_to(mean, (C, C)).T, same)
    out_ref[2 * GS : 2 * GS + 8] = jnp.broadcast_to(mean, (8, C))


def merge_kernel(a_ref, b_ref, out_ref):
    a, b = a_ref[...], b_ref[...]
    half = 0.5 * (a + b)
    gap = b - a
    wide = jnp.concatenate([gap[2 * GS :]] * (GS // 8), axis=0)
    out_ref[0:GS] = half[0:GS] + 0.25 * gap[GS : 2 * GS] * wide
    out_ref[GS:] = half[GS:]


def add_kernel(a_ref, b_ref, out_ref):
    out_ref[...] = a_ref[...] + b_ref[...]


def shift_band(moved_ref, bands_ref, e, middle, left, right):
    d, pad, width = DILATION_RATE, 16, middle.shape[0]
    bands_ref[pad : pad + width] = middle.astype(F32)
    bands_ref[pad - 8 : pad] = left.astype(F32)
    bands_ref[pad + width : pad + width + 8] = right.astype(F32)
    moved_ref[0, e] = bands_ref[pad + d : pad + d + width].astype(BF16)
    moved_ref[1, e] = middle
    moved_ref[2, e] = bands_ref[pad - d : pad - d + width].astype(BF16)


def tap_rows(moved_ref, weight_ref, taps):
    bands = [moved_ref[b, band] for a, band in taps for b in range(3)]
    taps = [a for a, _ in taps]
    weights = [weight_ref[3 * a + b] for a in taps for b in range(3)]
    return dot(jnp.concatenate(bands, axis=1), jnp.concatenate(weights, axis=0))


def pack_kernel(up_ref, left_ref, right_ref, odd_ref, first_ref, second_ref, token_ref):
    rows, width = up_ref.shape[0], up_ref.shape[1]
    d = DILATION_RATE
    odd = odd_ref[0:1] > 0.5
    for r in range(d):
        for begin, size, ref in ((0, width, up_ref), (width, 8, left_ref), (width + 8, 8, right_ref)):
            top, bottom = ref[r].astype(F32), ref[rows - d + r].astype(F32)
            first_ref[r, begin : begin + size] = jnp.where(odd, top, bottom).astype(BF16)
            second_ref[r, begin : begin + size] = jnp.where(odd, bottom, top).astype(BF16)
    leave(token_ref)


def bands_kernel(up_ref, left_ref, right_ref, w_ref, moved_ref, weight_ref, token_ref, bands_ref):
    rows = up_ref.shape[0]
    same = same_group()
    for tap in range(9):
        tile = jnp.concatenate([w_ref[tap].astype(F32)] * CHANNEL_GROUPS, axis=0)
        weight_ref[tap] = jnp.where(same, tile, 0.0).T.astype(BF16)

    def inner(r, carry):
        shift_band(moved_ref, bands_ref, r, up_ref[r], left_ref[r], right_ref[r])
        return carry

    lax.fori_loop(0, rows, inner, 0)
    leave(token_ref)


def near_kernel(moved_ref, weight_ref, out_ref, token_ref):
    rows = out_ref.shape[0]
    d = DILATION_RATE
    for first, last, taps in ((0, rows - d, {0: d, 1: 0}), (rows - d, d, {1: 0}), (d, rows, {1: 0, 2: -d})):

        def row(r, carry, taps=taps):
            out_ref[r] = tap_rows(moved_ref, weight_ref, [(a, r + step) for a, step in taps.items()])
            return carry

        lax.fori_loop(first, last, row, 0)
    leave(token_ref)


def far_kernel(even_ref, odd_ref, first_ref, second_ref, weight_ref, near_ref, moved_ref, out_ref, token_ref, bands_ref):
    rows, width = out_ref.shape[0], out_ref.shape[1]
    d = DILATION_RATE

    def outer(r, carry):
        first, second = first_ref[r], second_ref[r]
        for begin, place in ((0, odd_ref), (d, even_ref)):
            halo = jnp.where(place[0:1] > 0.5, first.astype(F32), second.astype(F32)).astype(BF16)
            shift_band(
                moved_ref, bands_ref, begin + r, halo[0:width], halo[width : width + 8], halo[width + 8 :]
            )
        return carry

    lax.fori_loop(0, d, outer, 0)
    back = 2 * d - rows
    for first, last, taps in ((0, rows - d, {2: 0}), (rows - d, d, {0: back, 2: 0}), (d, rows, {0: back})):

        def row(r, carry, taps=taps):
            far = tap_rows(moved_ref, weight_ref, [(a, r + step) for a, step in taps.items()])
            out_ref[r] = near_ref[r] + far
            return carry

        lax.fori_loop(first, last, row, 0)
    leave(token_ref)


def act_kernel(x_ref, stats_ref, gain_ref, bias_ref, turned_ref, white_ref, slope_ref, kept_ref, mean_ref):
    rows, width = x_ref.shape[0], x_ref.shape[1]
    same = same_group()
    eye = unit()
    gain, bias = gain_ref[0:1], bias_ref[0:1]
    mean = stats_ref[2 * GS : 2 * GS + 1]
    cov = stats_ref[0:GS] + EPSILON * eye
    trace = group_total(jnp.sum(cov * eye, axis=0, keepdims=True), same)[0:1]
    normed = cov / trace
    normed_wide = spread_split(normed, same)
    iterate = 1.5 * eye - 0.5 * normed
    for k in range(ITERS - 1):
        wide = spread_split(iterate, same)
        square = times(iterate, wide)
        scaled = times(iterate, normed_wide)
        scaled_wide = spread_split(scaled, same)
        cube_scaled = times(square, scaled_wide)
        kept_ref[k, 0] = iterate
        kept_ref[k, 1] = square
        kept_ref[k, 2] = scaled
        iterate = 1.5 * iterate - 0.5 * cube_scaled
    whitener = iterate * lax.rsqrt(trace)
    mean_wide = jnp.broadcast_to(mean, (8, C))
    kept_ref[ITERS - 1, 0] = whitener
    kept_ref[ITERS - 1, 1] = normed
    kept_ref[ITERS - 1, 2] = jnp.broadcast_to(trace, (GS, C))
    mean_ref[...] = mean_wide
    white_high, white_low = spread_split(whitener, same)
    rounded = white_high.astype(F32) + white_low.astype(F32)
    offset = jnp.dot(mean_wide, rounded, precision=lax.Precision.HIGHEST)[0:1]

    for r in range(rows):
        x = x_ref[r]
        white = dot(x, white_high) + dot(x, white_low) - offset
        pre = gain * white + bias
        gate = 0.5 * jnp.tanh(0.5 * pre) + 0.5
        act = pre * gate
        turned_ref[:, r * width : (r + 1) * width] = act.T.astype(BF16)
        white_ref[r] = white
        slope_ref[r] = gate + act * (1.0 - gate)


def tap_kernel(turned_ref, near_ref, far_ref, out_ref):
    rows, width = near_ref.shape[1], near_ref.shape[2]
    d = DILATION_RATE
    gap = rows - d
    same = same_group()

    def pair(b, first, count, ref, band):
        turned = turned_ref[:, first * width : (first + count) * width]
        return dot(turned, ref[b, band : band + count].reshape(count * width, C))

    def column(b, carry):
        out_ref[b] = fold(pair(b, 0, gap, near_ref, d) + pair(b, gap, d, far_ref, d), same)
        out_ref[3 + b] = fold(pair(b, 0, rows, near_ref, 0), same)
        out_ref[6 + b] = fold(pair(b, 0, d, far_ref, 0) + pair(b, d, gap, near_ref, 0), same)
        return carry

    lax.fori_loop(0, 3, column, 0)


def grad_kernel(x_ref, grad_ref, white_ref, slope_ref, kept_ref, mean_ref, gain_ref, back_ref, sums_ref):
    rows = x_ref.shape[0]
    same = same_group()
    gain = gain_ref[0:1]
    mean = mean_ref[0:1]
    white_high, white_low = spread_split(kept_ref[ITERS - 1, 0], same)

    def row(r, carry):
        gain_sum, bias_sum, products = carry
        pre_grad = grad_ref[r] * slope_ref[r]
        gain_sum = gain_sum + jnp.sum(pre_grad * white_ref[r], axis=0, keepdims=True)
        bias_sum = bias_sum + jnp.sum(pre_grad, axis=0, keepdims=True)
        high, low = split(pre_grad * gain)
        back_ref[r] = dot(high, white_high) + dot(low, white_high) + dot(high, white_low)
        products = products + lax.dot_general(
            x_ref[r], jnp.concatenate([high, low], axis=1), (((0,), (0,)), ((), ())), preferred_element_type=F32
        )
        return gain_sum, bias_sum, products

    nothing = jnp.zeros((1, C), F32)
    gain_sum, bias_sum, products = lax.fori_loop(0, rows, row, (nothing, nothing, jnp.zeros((C, 2 * C), F32)))
    mean_column = jnp.broadcast_to(mean, (C, C)).T
    full = products[:, :C] + products[:, C:] - mean_column * (gain * bias_sum)
    sums_ref[0:GS] = fold(full + full.T, same)
    line = lax.broadcasted_iota(jnp.int32, (8, C), 0)
    sums_ref[GS : GS + 8] = jnp.where(line == 0, gain_sum, jnp.where(line == 1, bias_sum, 0.0))


def prepare_kernel(kept_ref, mean_ref, gain_ref, wide_ref, lines_ref, token_ref):
    same = same_group()

    def put(place, packed):
        high, low = spread_split(packed, same)
        wide_ref[place, 0] = high
        wide_ref[place, 1] = low

    for k in range(ITERS - 1):
        iterate, square, scaled = kept_ref[k, 0], kept_ref[k, 1], kept_ref[k, 2]
        put(2 * k, scaled)
        put(2 * k + 1, times(iterate, (wide_ref[2 * k, 0], wide_ref[2 * k, 1])))
        lines_ref[0, k] = iterate
        lines_ref[1, k] = square
        lines_ref[2, k] = times(square, spread_split(iterate, same))
    put(2 * ITERS - 2, kept_ref[ITERS - 1, 1])
    for k in range(3):
        lines_ref[3, k] = kept_ref[ITERS - 1, k]
    lines_ref[3, 3, 0:8] = mean_ref[...]
    lines_ref[3, 3, 8:16] = gain_ref[...]
    lines_ref[3, 3, 16:] = jnp.zeros((GS - 16, C), F32)
    leave(token_ref)


def final_kernel(cell_count, x_ref, back_ref, sums_ref, wide_ref, lines_ref, after_ref, out_ref, vector_ref, high_ref, low_ref, constant_ref):
    del after_ref

    @pl.when(pl.program_id(0) == 0)
    def _():
        derivative(cell_count, sums_ref, wide_ref, lines_ref, vector_ref, high_ref, low_ref, constant_ref)

    x = x_ref[0]
    moved = dot(x, high_ref[...]) + dot(x, low_ref[...])
    out_ref[0] = (moved + back_ref[0] - constant_ref[0:1]).astype(BF16)


def derivative(cell_count, sums_ref, wide_ref, lines_ref, vector_ref, high_ref, low_ref, constant_ref):
    same = same_group()
    eye = unit()
    whitener, normed = lines_ref[3, 0], lines_ref[3, 1]
    trace = lines_ref[3, 2, 0:1]
    mean, gain = lines_ref[3, 3, 0:8], lines_ref[3, 3, 8:16]
    paired = sums_ref[0:GS]
    step = paired * lax.rsqrt(trace)
    wide = lambda place: (wide_ref[place, 0], wide_ref[place, 1])
    direct = times(lines_ref[2].reshape((ITERS - 1) * GS, C), spread_split(step, same))
    change = -0.5 * step
    for k in range(ITERS - 1):
        moved = direct[k * GS : (k + 1) * GS] + times(change, wide(2 * k + 1))
        moved = moved + times(lines_ref[0, k], spread_split(times(change, wide(2 * k)), same))
        moved = moved + times(lines_ref[1, k], spread_split(times(change, wide(2 * ITERS - 2)), same))
        change = 1.5 * change - 0.5 * moved
    inner = jnp.sum(change * normed + 0.5 * paired * whitener, axis=0, keepdims=True)
    symmetric = (change - eye * group_total(inner, same)[0:1]) / trace
    high, low = spread_split(symmetric * (1.0 / cell_count), same)
    high_ref[...] = high
    low_ref[...] = low
    rounded = high.astype(F32) + low.astype(F32)
    bias_sum = sums_ref[GS + 1 : GS + 2]
    weighted = gain * bias_sum * (1.0 / cell_count)
    both = jnp.concatenate([mean, weighted], axis=1)
    constant_ref[...] = jnp.dot(
        both, jnp.concatenate([rounded, spread(whitener, same)], axis=0), precision=lax.Precision.HIGHEST
    )
    vector_ref[...] = sums_ref[GS:] * (1.0 / math.sqrt(cell_count))


def stages(axes):
    for axis in axes:
        size = lax.axis_size(axis)
        stride = 1
        while stride < size:
            yield axis, [(i, i ^ stride) for i in range(size)]
            stride *= 2


def add(part, other, after=()):
    if not after:
        return part + other
    return run(add_kernel, jax.ShapeDtypeStruct(part.shape, F32), (part, other), after=after)


def swap(earlier, later, axis):
    size = lax.axis_size(axis)
    got = []
    for begin, part in ((0, earlier), (1, later)):
        pairs = [(i, i + 1) for i in range(begin, size - 1, 2)]
        pairs = pairs + [(j, i) for i, j in pairs]
        got.append(lax.ppermute(part, axis, pairs) if pairs else jnp.zeros_like(part))
    return got


def shards(features, upstream, conv_weight, norm_gain, norm_bias):
    mos_n, rows, width, _ = features.shape
    axes = ("dp", "cols", "rows")
    cell_count = mos_n * rows * width
    for axis in axes:
        cell_count *= lax.axis_size(axis)
    stage_pairs = list(stages(axes))
    count = len(stage_pairs)
    d = DILATION_RATE
    x = features.reshape(rows, width, C)
    up = upstream.reshape(rows, width, C)
    gain = jnp.broadcast_to(norm_gain[None], (8, C))
    bias = jnp.broadcast_to(norm_bias[None], (8, C))
    shape = jax.ShapeDtypeStruct
    cells = (rows, width, C)

    odd = lax.axis_index("cols") % 2 == 1
    first, second = up[:, :8], up[:, -8:]
    first, second = swap(jnp.where(odd, first, second), jnp.where(odd, second, first), "cols")
    left, right = jnp.where(odd, first, second), jnp.where(odd, second, first)
    odd_line = jnp.broadcast_to((lax.axis_index("rows") % 2 == 1).astype(F32), (8, C))
    even_line = 1.0 - odd_line
    halo = shape((d, width + 16, C), BF16)
    first, second, token = run(pack_kernel, (halo, halo, TOKEN), (up, left, right, odd_line))
    first, second = swap(first, second, "rows")
    stats = run(stats_kernel, shape((2 * GS + 8, C), F32), (x,), after=(token,))
    scratch = (pltpu.VMEM((width + 32, C), F32),)
    for number, (axis, pairs) in enumerate(stage_pairs):
        other = lax.ppermute(stats, axis, pairs)
        token = ()
        if number == count - 3:
            near_bands, weights, *token = run(
                bands_kernel,
                (shape((3,) + cells, BF16), shape((9, C, C), BF16), TOKEN),
                (up, left, right, conv_weight.reshape(9, GS, C)),
                scratch=scratch,
                after=(stats,),
            )
        if number == count - 2:
            near_grad, *token = run(
                near_kernel, (shape(cells, F32), TOKEN), (near_bands, weights), after=(stats,)
            )
        if number == count - 1:
            far_bands, act_grad, *token = run(
                far_kernel,
                (shape((3, 2 * d, width, C), BF16), shape(cells, F32), TOKEN),
                (even_line, odd_line, first, second, weights, near_grad),
                scratch=scratch,
                after=(stats,),
            )
        stats = run(merge_kernel, shape(stats.shape, F32), (stats, other), after=token)

    turned, white, slope, kept, mean = run(
        act_kernel,
        (
            shape((C, rows * width), BF16),
            shape(cells, F32),
            shape(cells, F32),
            shape((ITERS, 3, GS, C), F32),
            shape((8, C), F32),
        ),
        (x, stats, gain, bias),
    )
    taps = run(tap_kernel, shape((9, GS, C), F32), (turned, near_bands, far_bands))

    tap_axis, tap_pairs = stage_pairs[0]
    later = lax.axis_index(tap_axis) % 2
    halves = taps.reshape(2, -1, C)
    half = lax.dynamic_index_in_dim(halves, later, 0, False)
    half = add(half, lax.ppermute(lax.dynamic_index_in_dim(halves, 1 - later, 0, False), tap_axis, tap_pairs))

    back, sums = run(
        grad_kernel,
        (shape(cells, F32), shape((GS + 8, C), F32)),
        (x, act_grad, white, slope, kept, mean, gain),
        after=(half,),
    )
    row_stages = [stage for stage in stage_pairs[1:] if stage[0] == "rows"]
    tap_stages = row_stages + [stage for stage in stage_pairs[1:] if stage[0] != "rows"]
    half = add(half, lax.ppermute(half, *tap_stages[0]), after=(sums,))
    for number, stage in enumerate(stage_pairs):
        other = lax.ppermute(sums, *stage)
        token = ()
        if number == count - 1:
            wide, lines, *token = run(
                prepare_kernel,
                (shape((2 * ITERS - 1, 2, C, C), BF16), shape((4, ITERS - 1, GS, C), F32), TOKEN),
                (kept, mean, gain),
                after=(sums,),
            )
        sums = add(sums, other, after=token)
        if 2 <= number < count:
            last = number == count - 1
            half = add(half, lax.ppermute(half, *tap_stages[number - 1]), after=() if last else (sums,))
    block = pl.BlockSpec((1, width, C), lambda r: (r, 0, 0))
    input_grad, vectors = pl.pallas_call(
        functools.partial(final_kernel, cell_count),
        grid=(rows,),
        out_shape=(shape(cells, BF16), shape((8, C), F32)),
        in_specs=[block, block] + [VMEM_SPEC] * 3 + [pl.BlockSpec(memory_space=pl.ANY)],
        out_specs=[block, VMEM_SPEC],
        scratch_shapes=[pltpu.VMEM((C, C), BF16), pltpu.VMEM((C, C), BF16), pltpu.VMEM((8, C), F32)],
        compiler_params=pltpu.CompilerParams(vmem_limit_bytes=8 * 2**20),
        cost_estimate=NO_COST,
    )(x, back, sums, wide, lines, half)
    half = half * (1.0 / math.sqrt(cell_count))
    other = lax.ppermute(half, tap_axis, tap_pairs)
    taps = jnp.where(later == 0, jnp.stack([half, other]), jnp.stack([other, half]))
    return (
        input_grad.reshape(features.shape),
        taps.reshape(3, 3, GS, C),
        vectors[0],
        vectors[1],
    )


def solution(mesh):
    placed = (P("dp", "rows", "cols", None), P("dp", "rows", "cols", None), P(), P(), P())
    return jax.shard_map(
        shards,
        mesh=mesh,
        in_specs=placed,
        out_specs=(P("dp", "rows", "cols", None), P(), P(), P()),
        check_vma=False,
    )
```

```python
import functools
import math

import jax
import jax.numpy as jnp
from jax import lax
from jax.experimental import pallas as pl
from jax.experimental.pallas import tpu as pltpu
from jax.sharding import PartitionSpec as P

C = 256
CHANNEL_GROUPS = 8
GS = 32
DILATION_RATE = 6
ITERS = 5
EPSILON = 1e-05

F32 = jnp.float32
BF16 = jnp.bfloat16
VMEM_SPEC = pl.BlockSpec(memory_space=pltpu.VMEM)
NO_COST = pl.CostEstimate(flops=0, bytes_accessed=0, transcendentals=0)


def run(body, out_shapes, operands, scratch=(), after=(), grid=(), in_blocks={}, out_blocks={}):
    many = isinstance(out_shapes, (tuple, list))
    count = len(operands)

    def kernel(*refs):
        body(*refs[:count], *refs[count + len(after) :])

    out_specs = [out_blocks.get(i, VMEM_SPEC) for i in range(len(out_shapes) if many else 1)]
    return pl.pallas_call(
        kernel,
        grid=grid,
        out_shape=out_shapes,
        in_specs=[in_blocks.get(i, VMEM_SPEC) for i in range(count)] + [pl.BlockSpec(memory_space=pl.ANY)] * len(after),
        out_specs=out_specs if many else out_specs[0],
        scratch_shapes=list(scratch),
        compiler_params=pltpu.CompilerParams(vmem_limit_bytes=10 * 2**20),
        cost_estimate=NO_COST,
    )(*operands, *after)


def at_first(step):
    pl.when(pl.program_id(0) == 0)(step)


def at_last(step):
    pl.when(pl.program_id(0) == pl.num_programs(0) - 1)(step)


TOKEN = jax.ShapeDtypeStruct((8, 128), F32)


def leave(token_ref):
    token_ref[...] = jnp.zeros(token_ref.shape, F32)


def same_group():
    rows = lax.broadcasted_iota(jnp.int32, (C, C), 0)
    columns = lax.broadcasted_iota(jnp.int32, (C, C), 1)
    return (rows >> 5) == (columns >> 5)


def fold(full, same):
    kept = jnp.where(same, full, 0.0)
    total = kept[0:GS]
    for g in range(1, CHANNEL_GROUPS):
        total = total + kept[g * GS : (g + 1) * GS]
    return total


def spread(packed, same):
    return jnp.where(same, jnp.concatenate([packed] * CHANNEL_GROUPS, axis=0), 0)


def split(value):
    high = value.astype(BF16)
    low = (value - high.astype(F32)).astype(BF16)
    return high, low


def spread_split(packed, same):
    high, low = split(spread(packed, same))
    return high, low


def dot(a, b):
    return jnp.dot(a, b, preferred_element_type=F32)


def times(left, right):
    rows = left.shape[0]
    left_high, left_low = split(left)
    right_high, right_low = right
    both = dot(jnp.concatenate([left_high, left_low], axis=0), right_high)
    return both[:rows] + both[rows:] + dot(left_high, right_low)


def unit():
    rows = lax.broadcasted_iota(jnp.int32, (GS, C), 0)
    columns = lax.broadcasted_iota(jnp.int32, (GS, C), 1)
    return jnp.where(rows == (columns & (GS - 1)), 1.0, 0.0)


def group_total(row, same):
    wide = jnp.broadcast_to(row, (8, C))
    return jnp.dot(wide, jnp.where(same, 1.0, 0.0), precision=lax.Precision.HIGHEST)


def stats_kernel(x_ref, out_ref):
    rows = x_ref.shape[0]
    cells = rows * x_ref.shape[1]
    same = same_group()

    def add_up(r, total):
        return total + jnp.sum(x_ref[r].astype(F32), axis=0, keepdims=True)

    mean = lax.fori_loop(0, rows, add_up, jnp.zeros((1, C), F32)) / cells

    def products(r, total):
        high, low = split(x_ref[r].astype(F32) - mean)
        return total + lax.dot_general(
            high,
            jnp.concatenate([high, low], axis=1),
            (((0,), (0,)), ((), ())),
            preferred_element_type=F32,
        )

    total = lax.fori_loop(0, rows, products, jnp.zeros((C, 2 * C), F32))
    cross = total[:, C:]
    out_ref[0:GS] = fold(total[:, :C] + cross + cross.T, same) / cells
    out_ref[GS : 2 * GS] = fold(jnp.broadcast_to(mean, (C, C)).T, same)
    out_ref[2 * GS : 2 * GS + 8] = jnp.broadcast_to(mean, (8, C))


def merge_kernel(a_ref, b_ref, out_ref):
    a, b = a_ref[...], b_ref[...]
    half = 0.5 * (a + b)
    gap = b - a
    wide = jnp.concatenate([gap[2 * GS :]] * (GS // 8), axis=0)
    out_ref[0:GS] = half[0:GS] + 0.25 * gap[GS : 2 * GS] * wide
    out_ref[GS:] = half[GS:]


def add_kernel(a_ref, b_ref, out_ref):
    out_ref[...] = a_ref[...] + b_ref[...]


def shift_band(moved_ref, bands_ref, e, middle, left, right):
    d, pad, width = DILATION_RATE, 16, middle.shape[0]
    bands_ref[pad : pad + width] = middle.astype(F32)
    bands_ref[pad - 8 : pad] = left.astype(F32)
    bands_ref[pad + width : pad + width + 8] = right.astype(F32)
    moved_ref[0, e] = bands_ref[pad + d : pad + d + width].astype(BF16)
    moved_ref[1, e] = middle
    moved_ref[2, e] = bands_ref[pad - d : pad - d + width].astype(BF16)


def tap_rows(moved_ref, weight_ref, taps):
    bands = [moved_ref[b, band] for a, band in taps for b in range(3)]
    taps = [a for a, _ in taps]
    weights = [weight_ref[3 * a + b] for a in taps for b in range(3)]
    return dot(jnp.concatenate(bands, axis=1), jnp.concatenate(weights, axis=0))


def pack_kernel(top_ref, bottom_ref, left_ref, right_ref, odd_ref, first_ref, second_ref, token_ref):
    rows, width = left_ref.shape[0], top_ref.shape[1]
    r = pl.program_id(0)
    odd = odd_ref[0:1] > 0.5
    low = rows - DILATION_RATE + r
    sides = ((top_ref[0], bottom_ref[0]), (left_ref[r], left_ref[low]), (right_ref[r], right_ref[low]))
    begin = 0
    for top, bottom in sides:
        top, bottom = top.astype(F32), bottom.astype(F32)
        size = top.shape[0]
        first_ref[0, begin : begin + size] = jnp.where(odd, top, bottom).astype(BF16)
        second_ref[0, begin : begin + size] = jnp.where(odd, bottom, top).astype(BF16)
        begin += size
    leave(token_ref)


def bands_kernel(up_ref, left_ref, right_ref, w_ref, moved_ref, weight_ref, token_ref, bands_ref):
    rows = up_ref.shape[0]
    same = same_group()
    for tap in range(9):
        tile = jnp.concatenate([w_ref[tap].astype(F32)] * CHANNEL_GROUPS, axis=0)
        weight_ref[tap] = jnp.where(same, tile, 0.0).T.astype(BF16)

    def inner(r, carry):
        shift_band(moved_ref, bands_ref, r, up_ref[r], left_ref[r], right_ref[r])
        return carry

    lax.fori_loop(0, rows, inner, 0)
    leave(token_ref)


def by_rows(rows, cases, step):
    r = pl.program_id(0)
    for first, last, shifts in cases:
        pl.when((r >= first) & (r < last))(functools.partial(step, r, shifts))


def near_kernel(moved_ref, weight_ref, out_ref, token_ref):
    rows, d = moved_ref.shape[1], DILATION_RATE

    def step(r, shifts):
        out_ref[0] = tap_rows(moved_ref, weight_ref, [(a, r + shift) for a, shift in shifts.items()])

    by_rows(rows, ((0, rows - d, {0: d, 1: 0}), (rows - d, d, {1: 0}), (d, rows, {1: 0, 2: -d})), step)
    leave(token_ref)


def far_kernel(rows, even_ref, odd_ref, first_ref, second_ref, weight_ref, near_ref, moved_ref, out_ref, token_ref, bands_ref):
    d, width = DILATION_RATE, out_ref.shape[1]

    @at_first
    def _():
        def outer(r, carry):
            first, second = first_ref[r], second_ref[r]
            for begin, place in ((0, odd_ref), (d, even_ref)):
                halo = jnp.where(place[0:1] > 0.5, first.astype(F32), second.astype(F32)).astype(BF16)
                shift_band(
                    moved_ref, bands_ref, begin + r, halo[0:width], halo[width : width + 8], halo[width + 8 :]
                )
            return carry

        lax.fori_loop(0, d, outer, 0)
        leave(token_ref)

    def step(r, shifts):
        out_ref[0] = near_ref[0] + tap_rows(moved_ref, weight_ref, [(a, r + shift) for a, shift in shifts.items()])

    back = 2 * d - rows
    by_rows(rows, ((0, rows - d, {2: 0}), (rows - d, d, {0: back, 2: 0}), (d, rows, {0: back})), step)


def newton(stats_ref, kept_ref, mean_ref, high_ref, low_ref, offset_ref):
    same = same_group()
    eye = unit()
    mean = stats_ref[2 * GS :]
    cov = stats_ref[0:GS] + EPSILON * eye
    trace = group_total(jnp.sum(cov * eye, axis=0, keepdims=True), same)[0:1]
    normed = cov / trace
    normed_wide = spread_split(normed, same)
    iterate = 1.5 * eye - 0.5 * normed
    for k in range(ITERS - 1):
        wide = spread_split(iterate, same)
        square = times(iterate, wide)
        scaled = times(iterate, normed_wide)
        cube_scaled = times(square, spread_split(scaled, same))
        kept_ref[k, 0] = iterate
        kept_ref[k, 1] = square
        kept_ref[k, 2] = scaled
        iterate = 1.5 * iterate - 0.5 * cube_scaled
    whitener = iterate * lax.rsqrt(trace)
    kept_ref[ITERS - 1, 0] = whitener
    kept_ref[ITERS - 1, 1] = normed
    kept_ref[ITERS - 1, 2] = jnp.broadcast_to(trace, (GS, C))
    mean_ref[...] = mean
    high, low = spread_split(whitener, same)
    high_ref[...] = high
    low_ref[...] = low
    rounded = high.astype(F32) + low.astype(F32)
    offset_ref[...] = jnp.dot(mean, rounded, precision=lax.Precision.HIGHEST)


def act_kernel(
    x_ref, stats_ref, gain_ref, bias_ref, turned_ref, slope_ref, kept_ref, mean_ref, high_ref, low_ref, offset_ref
):
    r, width = pl.program_id(0), x_ref.shape[1]

    @at_first
    def _():
        newton(stats_ref, kept_ref, mean_ref, high_ref, low_ref, offset_ref)

    x = x_ref[0]
    white = dot(x, high_ref[...]) + dot(x, low_ref[...]) - offset_ref[0:1]
    pre = gain_ref[0:1] * white + bias_ref[0:1]
    gate = 0.5 * jnp.tanh(0.5 * pre) + 0.5
    act = pre * gate
    turned_ref[:, pl.ds(pl.multiple_of(r * width, width), width)] = act.T.astype(BF16)
    slope_ref[0] = gate + act * (1.0 - gate)


def tap_kernel(turned_ref, near_ref, far_ref, out_ref):
    rows, width = near_ref.shape[1], near_ref.shape[2]
    d = DILATION_RATE
    gap = rows - d
    same = same_group()

    def pair(b, first, count, ref, band):
        turned = turned_ref[:, first * width : (first + count) * width]
        return dot(turned, ref[b, band : band + count].reshape(count * width, C))

    def column(b, carry):
        out_ref[b] = fold(pair(b, 0, gap, near_ref, d) + pair(b, gap, d, far_ref, d), same)
        out_ref[3 + b] = fold(pair(b, 0, rows, near_ref, 0), same)
        out_ref[6 + b] = fold(pair(b, 0, d, far_ref, 0) + pair(b, d, gap, near_ref, 0), same)
        return carry

    lax.fori_loop(0, 3, column, 0)


def grad_kernel(
    x_ref, grad_ref, slope_ref, kept_ref, mean_ref, gain_ref, back_ref, sums_ref, high_ref, low_ref, total_ref, bias_ref
):
    same = same_group()

    @at_first
    def _():
        weighted = (spread(kept_ref[ITERS - 1, 0], same) * gain_ref[0:1]).T
        high, low = split(weighted)
        high_ref[...] = high
        low_ref[...] = low
        total_ref[...] = jnp.zeros_like(total_ref)
        bias_ref[...] = jnp.zeros_like(bias_ref)

    pre_grad = grad_ref[0] * slope_ref[0]
    high, low = split(pre_grad)
    bias_ref[0:1] += jnp.sum(pre_grad, axis=0, keepdims=True)
    back_ref[0] = dot(high, high_ref[...]) + dot(low, high_ref[...]) + dot(high, low_ref[...])
    turn = lambda part: lax.dot_general(x_ref[0], part, (((0,), (0,)), ((), ())), preferred_element_type=F32)
    total_ref[...] += turn(high) + turn(low)

    @at_last
    def _():
        bias_sum = bias_ref[0:1]
        mean_column = jnp.broadcast_to(mean_ref[0:1], (C, C)).T
        full = total_ref[...] - mean_column * bias_sum
        gain_sum = jnp.sum(full * spread(kept_ref[ITERS - 1, 0], same), axis=0, keepdims=True)
        full = full * gain_ref[0:1]
        sums_ref[0:GS] = fold(full + full.T, same)
        line = lax.broadcasted_iota(jnp.int32, (8, C), 0)
        sums_ref[GS : GS + 8] = jnp.where(line == 0, gain_sum, jnp.where(line == 1, bias_sum, 0.0))


def prepare_kernel(kept_ref, mean_ref, gain_ref, wide_ref, lines_ref, token_ref):
    same = same_group()

    def put(place, packed):
        high, low = spread_split(packed, same)
        wide_ref[place, 0] = high
        wide_ref[place, 1] = low

    for k in range(ITERS - 1):
        iterate, square, scaled = kept_ref[k, 0], kept_ref[k, 1], kept_ref[k, 2]
        put(2 * k, scaled)
        put(2 * k + 1, times(iterate, (wide_ref[2 * k, 0], wide_ref[2 * k, 1])))
        lines_ref[0, k] = iterate
        lines_ref[1, k] = square
        lines_ref[2, k] = times(square, spread_split(iterate, same))
    put(2 * ITERS - 2, kept_ref[ITERS - 1, 1])
    for k in range(3):
        lines_ref[3, k] = kept_ref[ITERS - 1, k]
    lines_ref[3, 3, 0:8] = mean_ref[...]
    lines_ref[3, 3, 8:16] = gain_ref[...]
    lines_ref[3, 3, 16:] = jnp.zeros((GS - 16, C), F32)
    leave(token_ref)


def final_kernel(cell_count, x_ref, back_ref, sums_ref, wide_ref, lines_ref, out_ref, gain_out_ref, bias_out_ref, high_ref, low_ref, constant_ref):
    @at_first
    def _():
        outs = (gain_out_ref, bias_out_ref, high_ref, low_ref, constant_ref)
        derivative(cell_count, sums_ref, wide_ref, lines_ref, *outs)

    x = x_ref[0]
    moved = dot(x, high_ref[...]) + dot(x, low_ref[...])
    out_ref[0] = (moved + back_ref[0] - constant_ref[0:1]).astype(BF16)


def derivative(cell_count, sums_ref, wide_ref, lines_ref, gain_out_ref, bias_out_ref, high_ref, low_ref, constant_ref):
    same = same_group()
    eye = unit()
    whitener, normed = lines_ref[3, 0], lines_ref[3, 1]
    trace = lines_ref[3, 2, 0:1]
    mean, gain = lines_ref[3, 3, 0:8], lines_ref[3, 3, 8:16]
    paired = sums_ref[0:GS]
    step = paired * lax.rsqrt(trace)
    wide = lambda place: (wide_ref[place, 0], wide_ref[place, 1])
    direct = times(lines_ref[2].reshape((ITERS - 1) * GS, C), spread_split(step, same))
    change = -0.5 * step
    for k in range(ITERS - 1):
        moved = direct[k * GS : (k + 1) * GS] + times(change, wide(2 * k + 1))
        moved = moved + times(lines_ref[0, k], spread_split(times(change, wide(2 * k)), same))
        moved = moved + times(lines_ref[1, k], spread_split(times(change, wide(2 * ITERS - 2)), same))
        change = 1.5 * change - 0.5 * moved
    inner = jnp.sum(change * normed + 0.5 * paired * whitener, axis=0, keepdims=True)
    symmetric = (change - eye * group_total(inner, same)[0:1]) / trace
    high, low = spread_split(symmetric * (1.0 / cell_count), same)
    high_ref[...] = high
    low_ref[...] = low
    rounded = high.astype(F32) + low.astype(F32)
    bias_sum = sums_ref[GS + 1 : GS + 2]
    weighted = gain * bias_sum * (1.0 / cell_count)
    both = jnp.concatenate([mean, weighted], axis=1)
    constant_ref[...] = jnp.dot(
        both, jnp.concatenate([rounded, spread(whitener, same)], axis=0), precision=lax.Precision.HIGHEST
    )
    for line, ref in enumerate((gain_out_ref, bias_out_ref)):
        ref[...] = sums_ref[GS + line] * (1.0 / math.sqrt(cell_count))


def stages(axes):
    for axis in axes:
        size = lax.axis_size(axis)
        stride = 1
        while stride < size:
            yield axis, [(i, i ^ stride) for i in range(size)]
            stride *= 2


def add(part, other, after=()):
    if not after:
        return part + other
    return run(add_kernel, jax.ShapeDtypeStruct(part.shape, F32), (part, other), after=after)


def swap(earlier, later, axis):
    size = lax.axis_size(axis)
    got = []
    for begin, part in ((0, earlier), (1, later)):
        pairs = [(i, i + 1) for i in range(begin, size - 1, 2)]
        pairs = pairs + [(j, i) for i, j in pairs]
        got.append(lax.ppermute(part, axis, pairs) if pairs else jnp.zeros_like(part))
    return got


def shards(features, upstream, conv_weight, norm_gain, norm_bias):
    mos_n, rows, width, _ = features.shape
    axes = ("dp", "cols", "rows")
    cell_count = mos_n * rows * width
    for axis in axes:
        cell_count *= lax.axis_size(axis)
    stage_pairs = list(stages(axes))
    count = len(stage_pairs)
    d = DILATION_RATE
    x = features.reshape(rows, width, C)
    up = upstream.reshape(rows, width, C)
    gain = jnp.broadcast_to(norm_gain[None], (8, C))
    bias = jnp.broadcast_to(norm_bias[None], (8, C))
    shape = jax.ShapeDtypeStruct
    cells = (rows, width, C)

    odd = lax.axis_index("cols") % 2 == 1
    first, second = up[:, :8], up[:, -8:]
    first, second = swap(jnp.where(odd, first, second), jnp.where(odd, second, first), "cols")
    left, right = jnp.where(odd, first, second), jnp.where(odd, second, first)
    odd_line = jnp.broadcast_to((lax.axis_index("rows") % 2 == 1).astype(F32), (8, C))
    even_line = 1.0 - odd_line
    halo = shape((d, width + 16, C), BF16)
    block = pl.BlockSpec((1, width, C), lambda r: (r, 0, 0))
    low_block = pl.BlockSpec((1, width, C), lambda r: (rows - d + r, 0, 0))
    halo_block = pl.BlockSpec((1, width + 16, C), lambda r: (r, 0, 0))
    first, second, token = run(
        pack_kernel,
        (halo, halo, TOKEN),
        (up, up, left, right, odd_line),
        grid=(d,),
        in_blocks={0: block, 1: low_block},
        out_blocks={0: halo_block, 1: halo_block},
    )
    first, second = swap(first, second, "rows")
    stats = run(stats_kernel, shape((2 * GS + 8, C), F32), (x,), after=(token,))
    scratch = (pltpu.VMEM((width + 32, C), F32),)
    for number, (axis, pairs) in enumerate(stage_pairs):
        other = lax.ppermute(stats, axis, pairs)
        token = ()
        if number == count - 3:
            near_bands, weights, *token = run(
                bands_kernel,
                (shape((3,) + cells, BF16), shape((9, C, C), BF16), TOKEN),
                (up, left, right, conv_weight.reshape(9, GS, C)),
                scratch=scratch,
                after=(stats,),
            )
        if number == count - 2:
            near_grad, *token = run(
                near_kernel,
                (shape(cells, F32), TOKEN),
                (near_bands, weights),
                after=(stats,),
                grid=(rows,),
                out_blocks={0: block},
            )
        if number == count - 1:
            far_bands, act_grad, *token = run(
                functools.partial(far_kernel, rows),
                (shape((3, 2 * d, width, C), BF16), shape(cells, F32), TOKEN),
                (even_line, odd_line, first, second, weights, near_grad),
                scratch=scratch,
                after=(stats,),
                grid=(rows,),
                in_blocks={5: block},
                out_blocks={1: block},
            )
        stats = run(merge_kernel, shape(stats.shape, F32), (stats, other), after=token)

    square = pltpu.VMEM((C, C), BF16)
    turned, slope, kept, mean = run(
        act_kernel,
        (shape((C, rows * width), BF16), shape(cells, F32), shape((ITERS, 3, GS, C), F32), shape((8, C), F32)),
        (x, stats, gain, bias),
        scratch=(square, square, pltpu.VMEM((8, C), F32)),
        grid=(rows,),
        in_blocks={0: block},
        out_blocks={1: block},
    )
    taps = run(tap_kernel, shape((9, GS, C), F32), (turned, near_bands, far_bands))

    tap_axis, tap_pairs = stage_pairs[0]
    later = lax.axis_index(tap_axis) % 2
    halves = taps.reshape(2, -1, C)
    half = lax.dynamic_index_in_dim(halves, later, 0, False)
    half = add(half, lax.ppermute(lax.dynamic_index_in_dim(halves, 1 - later, 0, False), tap_axis, tap_pairs))

    whole = lambda array: pl.BlockSpec(array.shape, lambda r: (0,) * array.ndim)
    back, sums = run(
        grad_kernel,
        (shape(cells, F32), shape((GS + 8, C), F32)),
        (x, act_grad, slope, kept, mean, gain),
        scratch=(square, square, pltpu.VMEM((C, C), F32), pltpu.VMEM((8, C), F32)),
        after=(half,),
        grid=(rows,),
        in_blocks={0: block, 1: block, 2: block, 3: whole(kept), 4: whole(mean), 5: whole(gain)},
        out_blocks={0: block},
    )
    row_stages = [stage for stage in stage_pairs[1:] if stage[0] == "rows"]
    tap_stages = row_stages + [stage for stage in stage_pairs[1:] if stage[0] != "rows"]
    half = add(half, lax.ppermute(half, *tap_stages[0]), after=(sums,))
    for number, stage in enumerate(stage_pairs):
        other = lax.ppermute(sums, *stage)
        token = ()
        if number == count - 1:
            wide, lines, *token = run(
                prepare_kernel,
                (shape((2 * ITERS - 1, 2, C, C), BF16), shape((4, ITERS - 1, GS, C), F32), TOKEN),
                (kept, mean, gain),
                after=(sums,),
            )
        sums = add(sums, other, after=token)
        if 2 <= number < count:
            last = number == count - 1
            half = add(half, lax.ppermute(half, *tap_stages[number - 1]), after=() if last else (sums,))
    line_block = pl.BlockSpec((C,), lambda r: (0,))
    input_grad, gain_grad, bias_grad = run(
        functools.partial(final_kernel, cell_count),
        (shape(cells, BF16), shape((C,), F32), shape((C,), F32)),
        (x, back, sums, wide, lines),
        scratch=(square, square, pltpu.VMEM((8, C), F32)),
        after=(half,),
        grid=(rows,),
        in_blocks={0: block, 1: block},
        out_blocks={0: block, 1: line_block, 2: line_block},
    )
    half = half * (1.0 / math.sqrt(cell_count))
    other = lax.ppermute(half, tap_axis, tap_pairs)
    taps = jnp.where(later == 0, jnp.stack([half, other]), jnp.stack([other, half]))
    return (
        input_grad.reshape(features.shape),
        taps.reshape(3, 3, GS, C),
        gain_grad,
        bias_grad,
    )


def solution(mesh):
    placed = (P("dp", "rows", "cols", None), P("dp", "rows", "cols", None), P(), P(), P())
    return jax.shard_map(
        shards,
        mesh=mesh,
        in_specs=placed,
        out_specs=(P("dp", "rows", "cols", None), P(), P(), P()),
        check_vma=False,
    )
```

```python
import functools
import math

import jax
import jax.numpy as jnp
from jax import lax
from jax.experimental import pallas as pl
from jax.experimental.pallas import tpu as pltpu
from jax.sharding import PartitionSpec as P

C = 256
CHANNEL_GROUPS = 8
GS = 32
DILATION_RATE = 6
ITERS = 5
EPSILON = 1e-05

F32 = jnp.float32
BF16 = jnp.bfloat16
VMEM_SPEC = pl.BlockSpec(memory_space=pltpu.VMEM)
NO_COST = pl.CostEstimate(flops=0, bytes_accessed=0, transcendentals=0)


def run(body, out_shapes, operands, scratch=(), after=()):
    many = isinstance(out_shapes, (tuple, list))
    count = len(operands)

    def kernel(*refs):
        body(*refs[:count], *refs[count + len(after) :])

    return pl.pallas_call(
        kernel,
        out_shape=out_shapes,
        in_specs=[VMEM_SPEC] * count + [pl.BlockSpec(memory_space=pl.ANY)] * len(after),
        out_specs=[VMEM_SPEC] * len(out_shapes) if many else VMEM_SPEC,
        scratch_shapes=list(scratch),
        compiler_params=pltpu.CompilerParams(vmem_limit_bytes=8 * 2**20),
        cost_estimate=NO_COST,
    )(*operands, *after)


TOKEN = jax.ShapeDtypeStruct((8, 128), F32)


def leave(token_ref):
    token_ref[...] = jnp.zeros(token_ref.shape, F32)


def same_group():
    rows = lax.broadcasted_iota(jnp.int32, (C, C), 0)
    columns = lax.broadcasted_iota(jnp.int32, (C, C), 1)
    return (rows >> 5) == (columns >> 5)


def fold(full, same):
    kept = jnp.where(same, full, 0.0)
    total = kept[0:GS]
    for g in range(1, CHANNEL_GROUPS):
        total = total + kept[g * GS : (g + 1) * GS]
    return total


def spread(packed, same):
    return jnp.where(same, jnp.concatenate([packed] * CHANNEL_GROUPS, axis=0), 0)


def split(value):
    high = value.astype(BF16)
    low = (value - high.astype(F32)).astype(BF16)
    return high, low


def spread_split(packed, same):
    high, low = split(spread(packed, same))
    return high, low


def dot(a, b):
    return jnp.dot(a, b, preferred_element_type=F32)


def times(left, right):
    rows = left.shape[0]
    left_high, left_low = split(left)
    right_high, right_low = right
    both = dot(jnp.concatenate([left_high, left_low], axis=0), right_high)
    return both[:rows] + both[rows:] + dot(left_high, right_low)


def unit():
    rows = lax.broadcasted_iota(jnp.int32, (GS, C), 0)
    columns = lax.broadcasted_iota(jnp.int32, (GS, C), 1)
    return jnp.where(rows == (columns & (GS - 1)), 1.0, 0.0)


def group_total(row, same):
    wide = jnp.broadcast_to(row, (8, C))
    return jnp.dot(wide, jnp.where(same, 1.0, 0.0), precision=lax.Precision.HIGHEST)


def stats_kernel(x_ref, out_ref):
    rows = x_ref.shape[0]
    cells = rows * x_ref.shape[1]
    same = same_group()

    def add_up(r, total):
        return total + jnp.sum(x_ref[r].astype(F32), axis=0, keepdims=True)

    mean = lax.fori_loop(0, rows, add_up, jnp.zeros((1, C), F32)) / cells

    def products(r, total):
        high, low = split(x_ref[r].astype(F32) - mean)
        return total + lax.dot_general(
            high,
            jnp.concatenate([high, low], axis=1),
            (((0,), (0,)), ((), ())),
            preferred_element_type=F32,
        )

    total = lax.fori_loop(0, rows, products, jnp.zeros((C, 2 * C), F32))
    cross = total[:, C:]
    out_ref[0:GS] = fold(total[:, :C] + cross + cross.T, same) / cells
    out_ref[GS : 2 * GS] = fold(jnp.broadcast_to(mean, (C, C)).T, same)
    out_ref[2 * GS : 2 * GS + 8] = jnp.broadcast_to(mean, (8, C))


def merge_kernel(a_ref, b_ref, out_ref):
    a, b = a_ref[...], b_ref[...]
    half = 0.5 * (a + b)
    gap = b - a
    wide = jnp.concatenate([gap[2 * GS :]] * (GS // 8), axis=0)
    out_ref[0:GS] = half[0:GS] + 0.25 * gap[GS : 2 * GS] * wide
    out_ref[GS:] = half[GS:]


def add_kernel(a_ref, b_ref, out_ref):
    out_ref[...] = a_ref[...] + b_ref[...]


def shift_band(moved_ref, bands_ref, e, middle, left, right):
    d, pad, width = DILATION_RATE, 16, middle.shape[0]
    bands_ref[pad : pad + width] = middle.astype(F32)
    bands_ref[pad - 8 : pad] = left.astype(F32)
    bands_ref[pad + width : pad + width + 8] = right.astype(F32)
    moved_ref[0, e] = bands_ref[pad + d : pad + d + width].astype(BF16)
    moved_ref[1, e] = middle
    moved_ref[2, e] = bands_ref[pad - d : pad - d + width].astype(BF16)


def tap_rows(moved_ref, weight_ref, taps):
    bands = [moved_ref[b, band] for a, band in taps for b in range(3)]
    taps = [a for a, _ in taps]
    weights = [weight_ref[3 * a + b] for a in taps for b in range(3)]
    return dot(jnp.concatenate(bands, axis=1), jnp.concatenate(weights, axis=0))


def pack_kernel(up_ref, left_ref, right_ref, odd_ref, first_ref, second_ref, token_ref):
    rows, width = up_ref.shape[0], up_ref.shape[1]
    d = DILATION_RATE
    odd = odd_ref[0:1] > 0.5
    for r in range(d):
        for begin, size, ref in ((0, width, up_ref), (width, 8, left_ref), (width + 8, 8, right_ref)):
            top, bottom = ref[r].astype(F32), ref[rows - d + r].astype(F32)
            first_ref[r, begin : begin + size] = jnp.where(odd, top, bottom).astype(BF16)
            second_ref[r, begin : begin + size] = jnp.where(odd, bottom, top).astype(BF16)
    leave(token_ref)


def bands_kernel(up_ref, left_ref, right_ref, w_ref, moved_ref, weight_ref, token_ref, bands_ref):
    rows = up_ref.shape[0]
    same = same_group()
    for tap in range(9):
        tile = jnp.concatenate([w_ref[tap].astype(F32)] * CHANNEL_GROUPS, axis=0)
        weight_ref[tap] = jnp.where(same, tile, 0.0).T.astype(BF16)

    def inner(r, carry):
        shift_band(moved_ref, bands_ref, r, up_ref[r], left_ref[r], right_ref[r])
        return carry

    lax.fori_loop(0, rows, inner, 0)
    leave(token_ref)


def near_kernel(moved_ref, weight_ref, out_ref, token_ref):
    rows = out_ref.shape[0]
    d = DILATION_RATE
    for first, last, taps in ((0, rows - d, {0: d, 1: 0}), (rows - d, d, {1: 0}), (d, rows, {1: 0, 2: -d})):

        def row(r, carry, taps=taps):
            out_ref[r] = tap_rows(moved_ref, weight_ref, [(a, r + step) for a, step in taps.items()])
            return carry

        lax.fori_loop(first, last, row, 0)
    leave(token_ref)


def far_kernel(even_ref, odd_ref, first_ref, second_ref, weight_ref, near_ref, moved_ref, out_ref, token_ref, bands_ref):
    rows, width = out_ref.shape[0], out_ref.shape[1]
    d = DILATION_RATE

    def outer(r, carry):
        first, second = first_ref[r], second_ref[r]
        for begin, place in ((0, odd_ref), (d, even_ref)):
            halo = jnp.where(place[0:1] > 0.5, first.astype(F32), second.astype(F32)).astype(BF16)
            shift_band(
                moved_ref, bands_ref, begin + r, halo[0:width], halo[width : width + 8], halo[width + 8 :]
            )
        return carry

    lax.fori_loop(0, d, outer, 0)
    back = 2 * d - rows
    for first, last, taps in ((0, rows - d, {2: 0}), (rows - d, d, {0: back, 2: 0}), (d, rows, {0: back})):

        def row(r, carry, taps=taps):
            far = tap_rows(moved_ref, weight_ref, [(a, r + step) for a, step in taps.items()])
            out_ref[r] = near_ref[r] + far
            return carry

        lax.fori_loop(first, last, row, 0)
    leave(token_ref)


def act_kernel(x_ref, stats_ref, gain_ref, bias_ref, turned_ref, slope_ref, kept_ref, mean_ref):
    rows, width = x_ref.shape[0], x_ref.shape[1]
    same = same_group()
    eye = unit()
    gain, bias = gain_ref[0:1], bias_ref[0:1]
    mean = stats_ref[2 * GS : 2 * GS + 1]
    cov = stats_ref[0:GS] + EPSILON * eye
    trace = group_total(jnp.sum(cov * eye, axis=0, keepdims=True), same)[0:1]
    normed = cov / trace
    normed_wide = spread_split(normed, same)
    iterate = 1.5 * eye - 0.5 * normed
    for k in range(ITERS - 1):
        wide = spread_split(iterate, same)
        square = times(iterate, wide)
        scaled = times(iterate, normed_wide)
        scaled_wide = spread_split(scaled, same)
        cube_scaled = times(square, scaled_wide)
        kept_ref[k, 0] = iterate
        kept_ref[k, 1] = square
        kept_ref[k, 2] = scaled
        iterate = 1.5 * iterate - 0.5 * cube_scaled
    whitener = iterate * lax.rsqrt(trace)
    mean_wide = jnp.broadcast_to(mean, (8, C))
    kept_ref[ITERS - 1, 0] = whitener
    kept_ref[ITERS - 1, 1] = normed
    kept_ref[ITERS - 1, 2] = jnp.broadcast_to(trace, (GS, C))
    mean_ref[...] = mean_wide
    white_high, white_low = spread_split(whitener, same)
    rounded = white_high.astype(F32) + white_low.astype(F32)
    offset = jnp.dot(mean_wide, rounded, precision=lax.Precision.HIGHEST)[0:1]

    for r in range(rows):
        x = x_ref[r]
        white = dot(x, white_high) + dot(x, white_low) - offset
        pre = gain * white + bias
        gate = 0.5 * jnp.tanh(0.5 * pre) + 0.5
        act = pre * gate
        turned_ref[:, r * width : (r + 1) * width] = act.T.astype(BF16)
        slope_ref[r] = gate + act * (1.0 - gate)


def tap_kernel(turned_ref, near_ref, far_ref, out_ref):
    rows, width = near_ref.shape[1], near_ref.shape[2]
    d = DILATION_RATE
    gap = rows - d
    same = same_group()

    def pair(b, first, count, ref, band):
        turned = turned_ref[:, first * width : (first + count) * width]
        return dot(turned, ref[b, band : band + count].reshape(count * width, C))

    def column(b, carry):
        out_ref[b] = fold(pair(b, 0, gap, near_ref, d) + pair(b, gap, d, far_ref, d), same)
        out_ref[3 + b] = fold(pair(b, 0, rows, near_ref, 0), same)
        out_ref[6 + b] = fold(pair(b, 0, d, far_ref, 0) + pair(b, d, gap, near_ref, 0), same)
        return carry

    lax.fori_loop(0, 3, column, 0)


def grad_kernel(x_ref, grad_ref, slope_ref, kept_ref, mean_ref, gain_ref, back_ref, sums_ref):
    rows = x_ref.shape[0]
    same = same_group()
    gain = gain_ref[0:1]
    whitener = spread(kept_ref[ITERS - 1, 0], same)
    weighted_high, weighted_low = split((whitener * gain).T)

    def row(r, carry):
        bias_sum, total = carry
        pre_grad = grad_ref[r] * slope_ref[r]
        bias_sum = bias_sum + jnp.sum(pre_grad, axis=0, keepdims=True)
        high, low = split(pre_grad)
        back_ref[r] = dot(high, weighted_high) + dot(low, weighted_high) + dot(high, weighted_low)
        turn = lambda part: lax.dot_general(x_ref[r], part, (((0,), (0,)), ((), ())), preferred_element_type=F32)
        return bias_sum, total + turn(high) + turn(low)

    bias_sum, total = lax.fori_loop(0, rows, row, (jnp.zeros((1, C), F32), jnp.zeros((C, C), F32)))
    mean_column = jnp.broadcast_to(mean_ref[0:1], (C, C)).T
    full = total - mean_column * bias_sum
    gain_sum = jnp.sum(full * whitener, axis=0, keepdims=True)
    full = full * gain
    sums_ref[0:GS] = fold(full + full.T, same)
    line = lax.broadcasted_iota(jnp.int32, (8, C), 0)
    sums_ref[GS : GS + 8] = jnp.where(line == 0, gain_sum, jnp.where(line == 1, bias_sum, 0.0))


def prepare_kernel(kept_ref, mean_ref, gain_ref, wide_ref, lines_ref, token_ref):
    same = same_group()

    def put(place, packed):
        high, low = spread_split(packed, same)
        wide_ref[place, 0] = high
        wide_ref[place, 1] = low

    for k in range(ITERS - 1):
        iterate, square, scaled = kept_ref[k, 0], kept_ref[k, 1], kept_ref[k, 2]
        put(2 * k, scaled)
        put(2 * k + 1, times(iterate, (wide_ref[2 * k, 0], wide_ref[2 * k, 1])))
        lines_ref[0, k] = iterate
        lines_ref[1, k] = square
        lines_ref[2, k] = times(square, spread_split(iterate, same))
    put(2 * ITERS - 2, kept_ref[ITERS - 1, 1])
    for k in range(3):
        lines_ref[3, k] = kept_ref[ITERS - 1, k]
    lines_ref[3, 3, 0:8] = mean_ref[...]
    lines_ref[3, 3, 8:16] = gain_ref[...]
    lines_ref[3, 3, 16:] = jnp.zeros((GS - 16, C), F32)
    leave(token_ref)


def final_kernel(cell_count, x_ref, back_ref, sums_ref, wide_ref, lines_ref, out_ref, gain_out_ref, bias_out_ref):
    high, low, constant = derivative(cell_count, sums_ref, wide_ref, lines_ref)
    for r in range(x_ref.shape[0]):
        moved = dot(x_ref[r], high) + dot(x_ref[r], low)
        out_ref[r] = (moved + back_ref[r] - constant).astype(BF16)
    for line, ref in enumerate((gain_out_ref, bias_out_ref)):
        ref[...] = sums_ref[GS + line] * (1.0 / math.sqrt(cell_count))


def derivative(cell_count, sums_ref, wide_ref, lines_ref):
    same = same_group()
    eye = unit()
    whitener, normed = lines_ref[3, 0], lines_ref[3, 1]
    trace = lines_ref[3, 2, 0:1]
    mean, gain = lines_ref[3, 3, 0:8], lines_ref[3, 3, 8:16]
    paired = sums_ref[0:GS]
    step = paired * lax.rsqrt(trace)
    wide = lambda place: (wide_ref[place, 0], wide_ref[place, 1])
    direct = times(lines_ref[2].reshape((ITERS - 1) * GS, C), spread_split(step, same))
    change = -0.5 * step
    for k in range(ITERS - 1):
        moved = direct[k * GS : (k + 1) * GS] + times(change, wide(2 * k + 1))
        moved = moved + times(lines_ref[0, k], spread_split(times(change, wide(2 * k)), same))
        moved = moved + times(lines_ref[1, k], spread_split(times(change, wide(2 * ITERS - 2)), same))
        change = 1.5 * change - 0.5 * moved
    inner = jnp.sum(change * normed + 0.5 * paired * whitener, axis=0, keepdims=True)
    symmetric = (change - eye * group_total(inner, same)[0:1]) / trace
    high, low = spread_split(symmetric * (1.0 / cell_count), same)
    rounded = high.astype(F32) + low.astype(F32)
    bias_sum = sums_ref[GS + 1 : GS + 2]
    weighted = gain * bias_sum * (1.0 / cell_count)
    both = jnp.concatenate([mean, weighted], axis=1)
    constant = jnp.dot(
        both, jnp.concatenate([rounded, spread(whitener, same)], axis=0), precision=lax.Precision.HIGHEST
    )
    return high, low, constant[0:1]


def stages(axes):
    for axis in axes:
        size = lax.axis_size(axis)
        stride = 1
        while stride < size:
            yield axis, [(i, i ^ stride) for i in range(size)]
            stride *= 2


def add(part, other, after=()):
    if not after:
        return part + other
    return run(add_kernel, jax.ShapeDtypeStruct(part.shape, F32), (part, other), after=after)


def swap(earlier, later, axis):
    size = lax.axis_size(axis)
    got = []
    for begin, part in ((0, earlier), (1, later)):
        pairs = [(i, i + 1) for i in range(begin, size - 1, 2)]
        pairs = pairs + [(j, i) for i, j in pairs]
        got.append(lax.ppermute(part, axis, pairs) if pairs else jnp.zeros_like(part))
    return got


def shards(features, upstream, conv_weight, norm_gain, norm_bias):
    mos_n, rows, width, _ = features.shape
    axes = ("dp", "cols", "rows")
    cell_count = mos_n * rows * width
    for axis in axes:
        cell_count *= lax.axis_size(axis)
    stage_pairs = list(stages(axes))
    count = len(stage_pairs)
    d = DILATION_RATE
    x = features.reshape(rows, width, C)
    up = upstream.reshape(rows, width, C)
    gain = jnp.broadcast_to(norm_gain[None], (8, C))
    bias = jnp.broadcast_to(norm_bias[None], (8, C))
    shape = jax.ShapeDtypeStruct
    held = pltpu.VMEM
    cells = (rows, width, C)

    odd = lax.axis_index("cols") % 2 == 1
    first, second = up[:, :8], up[:, -8:]
    first, second = swap(jnp.where(odd, first, second), jnp.where(odd, second, first), "cols")
    left, right = jnp.where(odd, first, second), jnp.where(odd, second, first)
    odd_line = jnp.broadcast_to((lax.axis_index("rows") % 2 == 1).astype(F32), (8, C))
    even_line = 1.0 - odd_line
    halo = shape((d, width + 16, C), BF16)
    first, second, token = run(pack_kernel, (halo, halo, TOKEN), (up, left, right, odd_line))
    first, second = swap(first, second, "rows")
    stats = run(stats_kernel, shape((2 * GS + 8, C), F32), (x,), after=(token,))
    scratch = (pltpu.VMEM((width + 32, C), F32),)
    for number, (axis, pairs) in enumerate(stage_pairs):
        other = lax.ppermute(stats, axis, pairs)
        token = ()
        if number == count - 3:
            near_bands, weights, *token = run(
                bands_kernel,
                (held((3,) + cells, BF16), held((9, C, C), BF16), TOKEN),
                (up, left, right, conv_weight.reshape(9, GS, C)),
                scratch=scratch,
                after=(stats,),
            )
        if number == count - 2:
            near_grad, *token = run(
                near_kernel, (held(cells, F32), TOKEN), (near_bands, weights), after=(stats,)
            )
        if number == count - 1:
            far_bands, act_grad, *token = run(
                far_kernel,
                (held((3, 2 * d, width, C), BF16), held(cells, F32), TOKEN),
                (even_line, odd_line, first, second, weights, near_grad),
                scratch=scratch,
                after=(stats,),
            )
        stats = run(merge_kernel, shape(stats.shape, F32), (stats, other), after=token)

    turned, slope, kept, mean = run(
        act_kernel,
        (
            held((C, rows * width), BF16),
            held(cells, F32),
            held((ITERS, 3, GS, C), F32),
            held((8, C), F32),
        ),
        (x, stats, gain, bias),
    )
    taps = run(tap_kernel, shape((9, GS, C), F32), (turned, near_bands, far_bands))

    tap_axis, tap_pairs = stage_pairs[0]
    later = lax.axis_index(tap_axis) % 2
    halves = taps.reshape(2, -1, C)
    half = lax.dynamic_index_in_dim(halves, later, 0, False)
    half = add(half, lax.ppermute(lax.dynamic_index_in_dim(halves, 1 - later, 0, False), tap_axis, tap_pairs))

    back, sums = run(
        grad_kernel,
        (held(cells, F32), shape((GS + 8, C), F32)),
        (x, act_grad, slope, kept, mean, gain),
        after=(half,),
    )
    row_stages = [stage for stage in stage_pairs[1:] if stage[0] == "rows"]
    tap_stages = row_stages + [stage for stage in stage_pairs[1:] if stage[0] != "rows"]
    half = add(half, lax.ppermute(half, *tap_stages[0]), after=(sums,))
    for number, stage in enumerate(stage_pairs):
        other = lax.ppermute(sums, *stage)
        token = ()
        if number == count - 1:
            wide, lines, *token = run(
                prepare_kernel,
                (held((2 * ITERS - 1, 2, C, C), BF16), held((4, ITERS - 1, GS, C), F32), TOKEN),
                (kept, mean, gain),
                after=(sums,),
            )
        sums = add(sums, other, after=token)
        if 2 <= number < count:
            half = add(half, lax.ppermute(half, *tap_stages[number - 1]), after=(sums,))
    input_grad, gain_grad, bias_grad = run(
        functools.partial(final_kernel, cell_count),
        (shape(cells, BF16), shape((C,), F32), shape((C,), F32)),
        (x, back, sums, wide, lines),
        after=(half,),
    )
    half = half * (1.0 / math.sqrt(cell_count))
    other = lax.ppermute(half, tap_axis, tap_pairs)
    taps = jnp.where(later == 0, jnp.stack([half, other]), jnp.stack([other, half]))
    return (
        input_grad.reshape(features.shape),
        taps.reshape(3, 3, GS, C),
        gain_grad,
        bias_grad,
    )


def solution(mesh):
    placed = (P("dp", "rows", "cols", None), P("dp", "rows", "cols", None), P(), P(), P())
    return jax.shard_map(
        shards,
        mesh=mesh,
        in_specs=placed,
        out_specs=(P("dp", "rows", "cols", None), P(), P(), P()),
        check_vma=False,
    )
```

```python
import functools
import math

import jax
import jax.numpy as jnp
from jax import lax
from jax.experimental import pallas as pl
from jax.experimental.pallas import tpu as pltpu
from jax.sharding import PartitionSpec as P

C = 256
CHANNEL_GROUPS = 8
GS = 32
DILATION_RATE = 6
ITERS = 5
EPSILON = 1e-05

F32 = jnp.float32
BF16 = jnp.bfloat16
VMEM_SPEC = pl.BlockSpec(memory_space=pltpu.VMEM)
NO_COST = pl.CostEstimate(flops=0, bytes_accessed=0, transcendentals=0)


def run(body, out_shapes, operands, scratch=(), after=()):
    many = isinstance(out_shapes, (tuple, list))
    count = len(operands)

    def kernel(*refs):
        body(*refs[:count], *refs[count + len(after) :])

    return pl.pallas_call(
        kernel,
        out_shape=out_shapes,
        in_specs=[VMEM_SPEC] * count + [pl.BlockSpec(memory_space=pl.ANY)] * len(after),
        out_specs=[VMEM_SPEC] * len(out_shapes) if many else VMEM_SPEC,
        scratch_shapes=list(scratch),
        compiler_params=pltpu.CompilerParams(vmem_limit_bytes=8 * 2**20),
        cost_estimate=NO_COST,
    )(*operands, *after)


TOKEN = jax.ShapeDtypeStruct((8, 128), F32)


def leave(token_ref):
    token_ref[...] = jnp.zeros(token_ref.shape, F32)


def same_group():
    rows = lax.broadcasted_iota(jnp.int32, (C, C), 0)
    columns = lax.broadcasted_iota(jnp.int32, (C, C), 1)
    return (rows >> 5) == (columns >> 5)


def fold(full, same):
    kept = jnp.where(same, full, 0.0)
    total = kept[0:GS]
    for g in range(1, CHANNEL_GROUPS):
        total = total + kept[g * GS : (g + 1) * GS]
    return total


def spread(packed, same):
    return jnp.where(same, jnp.concatenate([packed] * CHANNEL_GROUPS, axis=0), 0)


def split(value):
    high = value.astype(BF16)
    low = (value - high.astype(F32)).astype(BF16)
    return high, low


def spread_split(packed, same):
    high, low = split(spread(packed, same))
    return high, low


def dot(a, b):
    return jnp.dot(a, b, preferred_element_type=F32)


def times(left, right):
    rows = left.shape[0]
    left_high, left_low = split(left)
    right_high, right_low = right
    both = dot(jnp.concatenate([left_high, left_low], axis=0), right_high)
    return both[:rows] + both[rows:] + dot(left_high, right_low)


def unit():
    rows = lax.broadcasted_iota(jnp.int32, (GS, C), 0)
    columns = lax.broadcasted_iota(jnp.int32, (GS, C), 1)
    return jnp.where(rows == (columns & (GS - 1)), 1.0, 0.0)


def group_total(row, same):
    wide = jnp.broadcast_to(row, (8, C))
    return jnp.dot(wide, jnp.where(same, 1.0, 0.0), precision=lax.Precision.HIGHEST)


def stats_kernel(x_ref, out_ref):
    rows = x_ref.shape[0]
    cells = rows * x_ref.shape[1]
    same = same_group()

    def add_up(r, total):
        return total + jnp.sum(x_ref[r].astype(F32), axis=0, keepdims=True)

    mean = lax.fori_loop(0, rows, add_up, jnp.zeros((1, C), F32)) / cells

    def products(r, total):
        high, low = split(x_ref[r].astype(F32) - mean)
        return total + lax.dot_general(
            high,
            jnp.concatenate([high, low], axis=1),
            (((0,), (0,)), ((), ())),
            preferred_element_type=F32,
        )

    total = lax.fori_loop(0, rows, products, jnp.zeros((C, 2 * C), F32))
    cross = total[:, C:]
    out_ref[0:GS] = fold(total[:, :C] + cross + cross.T, same) / cells
    out_ref[GS : 2 * GS] = fold(jnp.broadcast_to(mean, (C, C)).T, same)
    out_ref[2 * GS : 2 * GS + 8] = jnp.broadcast_to(mean, (8, C))


def merge_kernel(a_ref, b_ref, out_ref):
    a, b = a_ref[...], b_ref[...]
    half = 0.5 * (a + b)
    gap = b - a
    wide = jnp.concatenate([gap[2 * GS :]] * (GS // 8), axis=0)
    out_ref[0:GS] = half[0:GS] + 0.25 * gap[GS : 2 * GS] * wide
    out_ref[GS:] = half[GS:]


def add_kernel(a_ref, b_ref, out_ref):
    out_ref[...] = a_ref[...] + b_ref[...]


def shift_band(moved_ref, bands_ref, e, middle, left, right):
    d, pad, width = DILATION_RATE, 16, middle.shape[0]
    bands_ref[pad : pad + width] = middle.astype(F32)
    bands_ref[pad - 8 : pad] = left.astype(F32)
    bands_ref[pad + width : pad + width + 8] = right.astype(F32)
    moved_ref[0, e] = bands_ref[pad + d : pad + d + width].astype(BF16)
    moved_ref[1, e] = middle
    moved_ref[2, e] = bands_ref[pad - d : pad - d + width].astype(BF16)


def tap_rows(moved_ref, weight_ref, taps):
    bands = [moved_ref[b, band] for a, band in taps for b in range(3)]
    taps = [a for a, _ in taps]
    weights = [weight_ref[3 * a + b] for a in taps for b in range(3)]
    return dot(jnp.concatenate(bands, axis=1), jnp.concatenate(weights, axis=0))


def pack_kernel(up_ref, left_ref, right_ref, odd_ref, first_ref, second_ref, token_ref):
    rows, width = up_ref.shape[0], up_ref.shape[1]
    d = DILATION_RATE
    odd = odd_ref[0:1] > 0.5
    for r in range(d):
        for begin, size, ref in ((0, width, up_ref), (width, 8, left_ref), (width + 8, 8, right_ref)):
            top, bottom = ref[r].astype(F32), ref[rows - d + r].astype(F32)
            first_ref[r, begin : begin + size] = jnp.where(odd, top, bottom).astype(BF16)
            second_ref[r, begin : begin + size] = jnp.where(odd, bottom, top).astype(BF16)
    leave(token_ref)


def bands_kernel(up_ref, left_ref, right_ref, w_ref, moved_ref, weight_ref, token_ref, bands_ref):
    rows = up_ref.shape[0]
    same = same_group()
    for tap in range(9):
        tile = jnp.concatenate([w_ref[tap].astype(F32)] * CHANNEL_GROUPS, axis=0)
        weight_ref[tap] = jnp.where(same, tile, 0.0).T.astype(BF16)

    def inner(r, carry):
        shift_band(moved_ref, bands_ref, r, up_ref[r], left_ref[r], right_ref[r])
        return carry

    lax.fori_loop(0, rows, inner, 0)
    leave(token_ref)


def near_kernel(moved_ref, weight_ref, out_ref, token_ref):
    rows = out_ref.shape[0]
    d = DILATION_RATE
    for first, last, taps in ((0, rows - d, {0: d, 1: 0}), (rows - d, d, {1: 0}), (d, rows, {1: 0, 2: -d})):

        def row(r, carry, taps=taps):
            out_ref[r] = tap_rows(moved_ref, weight_ref, [(a, r + step) for a, step in taps.items()])
            return carry

        lax.fori_loop(first, last, row, 0)
    leave(token_ref)


def far_kernel(odd_ref, first_ref, second_ref, weight_ref, near_ref, moved_ref, out_ref, token_ref, bands_ref):
    rows, width = out_ref.shape[0], out_ref.shape[1]
    d = DILATION_RATE

    def outer(r, carry):
        odd = odd_ref[0:1] > 0.5
        first, second = first_ref[r].astype(F32), second_ref[r].astype(F32)
        for begin, halo in ((0, jnp.where(odd, first, second)), (d, jnp.where(odd, second, first))):
            halo = halo.astype(BF16)
            shift_band(
                moved_ref, bands_ref, begin + r, halo[0:width], halo[width : width + 8], halo[width + 8 :]
            )
        return carry

    lax.fori_loop(0, d, outer, 0)
    back = 2 * d - rows
    for first, last, taps in ((0, rows - d, {2: 0}), (rows - d, d, {0: back, 2: 0}), (d, rows, {0: back})):

        def row(r, carry, taps=taps):
            far = tap_rows(moved_ref, weight_ref, [(a, r + step) for a, step in taps.items()])
            out_ref[r] = near_ref[r] + far
            return carry

        lax.fori_loop(first, last, row, 0)
    leave(token_ref)


def act_kernel(x_ref, stats_ref, gain_ref, bias_ref, turned_ref, slope_ref, kept_ref, mean_ref):
    rows, width = x_ref.shape[0], x_ref.shape[1]
    same = same_group()
    eye = unit()
    gain, bias = gain_ref[0:1], bias_ref[0:1]
    mean = stats_ref[2 * GS : 2 * GS + 1]
    cov = stats_ref[0:GS] + EPSILON * eye
    trace = group_total(jnp.sum(cov * eye, axis=0, keepdims=True), same)[0:1]
    normed = cov / trace
    normed_wide = spread_split(normed, same)
    iterate = 1.5 * eye - 0.5 * normed
    for k in range(ITERS - 1):
        wide = spread_split(iterate, same)
        square = times(iterate, wide)
        scaled = times(iterate, normed_wide)
        scaled_wide = spread_split(scaled, same)
        cube_scaled = times(square, scaled_wide)
        kept_ref[k, 0] = iterate
        kept_ref[k, 1] = square
        kept_ref[k, 2] = scaled
        iterate = 1.5 * iterate - 0.5 * cube_scaled
    whitener = iterate * lax.rsqrt(trace)
    mean_wide = jnp.broadcast_to(mean, (8, C))
    kept_ref[ITERS - 1, 0] = whitener
    kept_ref[ITERS - 1, 1] = normed
    kept_ref[ITERS - 1, 2] = jnp.broadcast_to(trace, (GS, C))
    mean_ref[...] = mean_wide
    white_high, white_low = spread_split(whitener, same)
    rounded = white_high.astype(F32) + white_low.astype(F32)
    offset = jnp.dot(mean_wide, rounded, precision=lax.Precision.HIGHEST)[0:1]

    for r in range(rows):
        x = x_ref[r]
        white = dot(x, white_high) + dot(x, white_low) - offset
        pre = gain * white + bias
        gate = 0.5 * jnp.tanh(0.5 * pre) + 0.5
        act = pre * gate
        turned_ref[:, r * width : (r + 1) * width] = act.T.astype(BF16)
        slope_ref[r] = gate + act * (1.0 - gate)


def tap_kernel(turned_ref, near_ref, far_ref, later_ref, own_ref, other_ref, total_ref):
    rows, width = near_ref.shape[1], near_ref.shape[2]
    d = DILATION_RATE
    gap = rows - d
    same = same_group()

    def pair(b, first, count, ref, band):
        turned = turned_ref[:, first * width : (first + count) * width]
        return dot(turned, ref[b, band : band + count].reshape(count * width, C))

    def column(b, carry):
        total_ref[b] = fold(pair(b, 0, gap, near_ref, d) + pair(b, gap, d, far_ref, d), same)
        total_ref[3 + b] = fold(pair(b, 0, rows, near_ref, 0), same)
        total_ref[6 + b] = fold(pair(b, 0, d, far_ref, 0) + pair(b, d, gap, near_ref, 0), same)
        return carry

    lax.fori_loop(0, 3, column, 0)
    later = later_ref[0:1] > 0.5
    total = total_ref[...].reshape(9 * GS, C)
    first, second = total[: own_ref.shape[0]], total[own_ref.shape[0] :]
    own_ref[...] = jnp.where(later, second, first)
    other_ref[...] = jnp.where(later, first, second)


def join_kernel(scale, own_ref, other_ref, later_ref, out_ref):
    later = later_ref[0:1] > 0.5
    own, other = own_ref[...] * scale, other_ref[...] * scale
    size = own.shape[0]
    out_ref[:size] = jnp.where(later, other, own)
    out_ref[size:] = jnp.where(later, own, other)


def grad_kernel(x_ref, grad_ref, slope_ref, kept_ref, mean_ref, gain_ref, back_ref, sums_ref):
    rows = x_ref.shape[0]
    same = same_group()
    gain = gain_ref[0:1]
    whitener = spread(kept_ref[ITERS - 1, 0], same)
    weighted_high, weighted_low = split((whitener * gain).T)

    def row(r, carry):
        bias_sum, total = carry
        pre_grad = grad_ref[r] * slope_ref[r]
        bias_sum = bias_sum + jnp.sum(pre_grad, axis=0, keepdims=True)
        high, low = split(pre_grad)
        back_ref[r] = dot(high, weighted_high) + dot(low, weighted_high) + dot(high, weighted_low)
        turn = lambda part: lax.dot_general(x_ref[r], part, (((0,), (0,)), ((), ())), preferred_element_type=F32)
        return bias_sum, total + turn(high) + turn(low)

    bias_sum, total = lax.fori_loop(0, rows, row, (jnp.zeros((1, C), F32), jnp.zeros((C, C), F32)))
    mean_column = jnp.broadcast_to(mean_ref[0:1], (C, C)).T
    full = total - mean_column * bias_sum
    gain_sum = jnp.sum(full * whitener, axis=0, keepdims=True)
    full = full * gain
    sums_ref[0:GS] = fold(full + full.T, same)
    line = lax.broadcasted_iota(jnp.int32, (8, C), 0)
    sums_ref[GS : GS + 8] = jnp.where(line == 0, gain_sum, jnp.where(line == 1, bias_sum, 0.0))


def prepare_kernel(kept_ref, mean_ref, gain_ref, wide_ref, lines_ref, token_ref):
    same = same_group()

    def put(place, packed):
        high, low = spread_split(packed, same)
        wide_ref[place, 0] = high
        wide_ref[place, 1] = low

    for k in range(ITERS - 1):
        iterate, square, scaled = kept_ref[k, 0], kept_ref[k, 1], kept_ref[k, 2]
        put(2 * k, scaled)
        put(2 * k + 1, times(iterate, (wide_ref[2 * k, 0], wide_ref[2 * k, 1])))
        lines_ref[0, k] = iterate
        lines_ref[1, k] = square
        lines_ref[2, k] = times(square, spread_split(iterate, same))
    put(2 * ITERS - 2, kept_ref[ITERS - 1, 1])
    for k in range(3):
        lines_ref[3, k] = kept_ref[ITERS - 1, k]
    lines_ref[3, 3, 0:8] = mean_ref[...]
    lines_ref[3, 3, 8:16] = gain_ref[...]
    lines_ref[3, 3, 16:] = jnp.zeros((GS - 16, C), F32)
    leave(token_ref)


def final_kernel(cell_count, x_ref, back_ref, sums_ref, wide_ref, lines_ref, out_ref, gain_out_ref, bias_out_ref):
    high, low, constant = derivative(cell_count, sums_ref, wide_ref, lines_ref)
    for r in range(x_ref.shape[0]):
        moved = dot(x_ref[r], high) + dot(x_ref[r], low)
        out_ref[r] = (moved + back_ref[r] - constant).astype(BF16)
    for line, ref in enumerate((gain_out_ref, bias_out_ref)):
        ref[...] = sums_ref[GS + line] * (1.0 / math.sqrt(cell_count))


def derivative(cell_count, sums_ref, wide_ref, lines_ref):
    same = same_group()
    eye = unit()
    whitener, normed = lines_ref[3, 0], lines_ref[3, 1]
    trace = lines_ref[3, 2, 0:1]
    mean, gain = lines_ref[3, 3, 0:8], lines_ref[3, 3, 8:16]
    paired = sums_ref[0:GS]
    step = paired * lax.rsqrt(trace)
    wide = lambda place: (wide_ref[place, 0], wide_ref[place, 1])
    direct = times(lines_ref[2].reshape((ITERS - 1) * GS, C), spread_split(step, same))
    change = -0.5 * step
    for k in range(ITERS - 1):
        moved = direct[k * GS : (k + 1) * GS] + times(change, wide(2 * k + 1))
        moved = moved + times(lines_ref[0, k], spread_split(times(change, wide(2 * k)), same))
        moved = moved + times(lines_ref[1, k], spread_split(times(change, wide(2 * ITERS - 2)), same))
        change = 1.5 * change - 0.5 * moved
    inner = jnp.sum(change * normed + 0.5 * paired * whitener, axis=0, keepdims=True)
    symmetric = (change - eye * group_total(inner, same)[0:1]) / trace
    high, low = spread_split(symmetric * (1.0 / cell_count), same)
    rounded = high.astype(F32) + low.astype(F32)
    bias_sum = sums_ref[GS + 1 : GS + 2]
    weighted = gain * bias_sum * (1.0 / cell_count)
    both = jnp.concatenate([mean, weighted], axis=1)
    constant = jnp.dot(
        both, jnp.concatenate([rounded, spread(whitener, same)], axis=0), precision=lax.Precision.HIGHEST
    )
    return high, low, constant[0:1]


def stages(axes):
    for axis in axes:
        size = lax.axis_size(axis)
        stride = 1
        while stride < size:
            yield axis, [(i, i ^ stride) for i in range(size)]
            stride *= 2


def add(part, other, after=()):
    if not after:
        return part + other
    return run(add_kernel, jax.ShapeDtypeStruct(part.shape, F32), (part, other), after=after)


def swap(earlier, later, axis):
    size = lax.axis_size(axis)
    got = []
    for begin, part in ((0, earlier), (1, later)):
        pairs = [(i, i + 1) for i in range(begin, size - 1, 2)]
        pairs = pairs + [(j, i) for i, j in pairs]
        got.append(lax.ppermute(part, axis, pairs) if pairs else jnp.zeros_like(part))
    return got


def shards(features, upstream, conv_weight, norm_gain, norm_bias):
    mos_n, rows, width, _ = features.shape
    axes = ("dp", "cols", "rows")
    cell_count = mos_n * rows * width
    for axis in axes:
        cell_count *= lax.axis_size(axis)
    stage_pairs = list(stages(axes))
    count = len(stage_pairs)
    d = DILATION_RATE
    x = features.reshape(rows, width, C)
    up = upstream.reshape(rows, width, C)
    gain = jnp.broadcast_to(norm_gain[None], (8, C))
    bias = jnp.broadcast_to(norm_bias[None], (8, C))
    shape = jax.ShapeDtypeStruct
    held = pltpu.VMEM
    cells = (rows, width, C)

    odd = lax.axis_index("cols") % 2 == 1
    first, second = up[:, :8], up[:, -8:]
    first, second = swap(jnp.where(odd, first, second), jnp.where(odd, second, first), "cols")
    left, right = jnp.where(odd, first, second), jnp.where(odd, second, first)
    odd_line = jnp.broadcast_to((lax.axis_index("rows") % 2 == 1).astype(F32), (8, C))
    tap_axis, tap_pairs = stage_pairs[0]
    later_line = jnp.broadcast_to((lax.axis_index(tap_axis) % 2 == 1).astype(F32), (8, C))
    halo = shape((d, width + 16, C), BF16)
    first, second, token = run(pack_kernel, (halo, halo, TOKEN), (up, left, right, odd_line), after=(later_line,))
    first, second = swap(first, second, "rows")
    stats = run(stats_kernel, shape((2 * GS + 8, C), F32), (x,), after=(token,))
    scratch = (pltpu.VMEM((width + 32, C), F32),)
    for number, (axis, pairs) in enumerate(stage_pairs):
        other = lax.ppermute(stats, axis, pairs)
        token = ()
        if number == count - 3:
            near_bands, weights, *token = run(
                bands_kernel,
                (held((3,) + cells, BF16), held((9, C, C), BF16), TOKEN),
                (up, left, right, conv_weight.reshape(9, GS, C)),
                scratch=scratch,
                after=(stats,),
            )
        if number == count - 2:
            near_grad, *token = run(
                near_kernel, (held(cells, F32), TOKEN), (near_bands, weights), after=(stats,)
            )
        if number == count - 1:
            far_bands, act_grad, *token = run(
                far_kernel,
                (held((3, 2 * d, width, C), BF16), held(cells, F32), TOKEN),
                (odd_line, first, second, weights, near_grad),
                scratch=scratch,
                after=(stats,),
            )
        stats = run(merge_kernel, shape(stats.shape, F32), (stats, other), after=token)

    turned, slope, kept, mean = run(
        act_kernel,
        (
            held((C, rows * width), BF16),
            held(cells, F32),
            held((ITERS, 3, GS, C), F32),
            held((8, C), F32),
        ),
        (x, stats, gain, bias),
    )
    half = shape((9 * GS // 2, C), F32)
    half, other = run(
        tap_kernel,
        (half, half),
        (turned, near_bands, far_bands, later_line),
        scratch=(pltpu.VMEM((9, GS, C), F32),),
    )
    half = add(half, lax.ppermute(other, tap_axis, tap_pairs))

    back, sums = run(
        grad_kernel,
        (held(cells, F32), shape((GS + 8, C), F32)),
        (x, act_grad, slope, kept, mean, gain),
        after=(half,),
    )
    row_stages = [stage for stage in stage_pairs[1:] if stage[0] == "rows"]
    tap_stages = row_stages + [stage for stage in stage_pairs[1:] if stage[0] != "rows"]
    half = add(half, lax.ppermute(half, *tap_stages[0]), after=(sums,))
    for number, stage in enumerate(stage_pairs):
        other = lax.ppermute(sums, *stage)
        token = ()
        if number == count - 1:
            wide, lines, *token = run(
                prepare_kernel,
                (held((2 * ITERS - 1, 2, C, C), BF16), held((4, ITERS - 1, GS, C), F32), TOKEN),
                (kept, mean, gain),
                after=(sums,),
            )
        sums = add(sums, other, after=token)
        if 2 <= number < count:
            half = add(half, lax.ppermute(half, *tap_stages[number - 1]), after=(sums,))
    input_grad, gain_grad, bias_grad = run(
        functools.partial(final_kernel, cell_count),
        (shape(cells, BF16), shape((C,), F32), shape((C,), F32)),
        (x, back, sums, wide, lines),
        after=(half,),
    )
    other = lax.ppermute(half, tap_axis, tap_pairs)
    taps = run(
        functools.partial(join_kernel, 1.0 / math.sqrt(cell_count)),
        shape((9 * GS, C), F32),
        (half, other, later_line),
    )
    return (
        input_grad.reshape(features.shape),
        taps.reshape(3, 3, GS, C),
        gain_grad,
        bias_grad,
    )


def solution(mesh):
    placed = (P("dp", "rows", "cols", None), P("dp", "rows", "cols", None), P(), P(), P())
    return jax.shard_map(
        shards,
        mesh=mesh,
        in_specs=placed,
        out_specs=(P("dp", "rows", "cols", None), P(), P(), P()),
        check_vma=False,
    )
```

```python
import functools
import math

import jax
import jax.numpy as jnp
from jax import lax
from jax.experimental import pallas as pl
from jax.experimental.pallas import tpu as pltpu
from jax.sharding import PartitionSpec as P

C = 256
CHANNEL_GROUPS = 8
GS = 32
DILATION_RATE = 6
ITERS = 5
EPSILON = 1e-05

F32 = jnp.float32
BF16 = jnp.bfloat16
VMEM_SPEC = pl.BlockSpec(memory_space=pltpu.VMEM)
NO_COST = pl.CostEstimate(flops=0, bytes_accessed=0, transcendentals=0)


def run(body, out_shapes, operands, scratch=(), after=()):
    many = isinstance(out_shapes, (tuple, list))
    count = len(operands)

    def kernel(*refs):
        body(*refs[:count], *refs[count + len(after) :])

    return pl.pallas_call(
        kernel,
        out_shape=out_shapes,
        in_specs=[VMEM_SPEC] * count + [pl.BlockSpec(memory_space=pl.ANY)] * len(after),
        out_specs=[VMEM_SPEC] * len(out_shapes) if many else VMEM_SPEC,
        scratch_shapes=list(scratch),
        compiler_params=pltpu.CompilerParams(vmem_limit_bytes=8 * 2**20),
        cost_estimate=NO_COST,
    )(*operands, *after)


TOKEN = jax.ShapeDtypeStruct((8, 128), F32)


def leave(token_ref):
    token_ref[...] = jnp.zeros(token_ref.shape, F32)


def same_group():
    rows = lax.broadcasted_iota(jnp.int32, (C, C), 0)
    columns = lax.broadcasted_iota(jnp.int32, (C, C), 1)
    return (rows >> 5) == (columns >> 5)


def fold(full, same):
    kept = jnp.where(same, full, 0.0)
    total = kept[0:GS]
    for g in range(1, CHANNEL_GROUPS):
        total = total + kept[g * GS : (g + 1) * GS]
    return total


def spread(packed, same):
    return jnp.where(same, jnp.concatenate([packed] * CHANNEL_GROUPS, axis=0), 0)


def split(value):
    high = value.astype(BF16)
    low = (value - high.astype(F32)).astype(BF16)
    return high, low


def spread_split(packed, same):
    high, low = split(spread(packed, same))
    return high, low


def dot(a, b):
    return jnp.dot(a, b, preferred_element_type=F32)


def times(left, right):
    rows = left.shape[0]
    left_high, left_low = split(left)
    right_high, right_low = right
    both = dot(jnp.concatenate([left_high, left_low], axis=0), right_high)
    return both[:rows] + both[rows:] + dot(left_high, right_low)


def unit():
    rows = lax.broadcasted_iota(jnp.int32, (GS, C), 0)
    columns = lax.broadcasted_iota(jnp.int32, (GS, C), 1)
    return jnp.where(rows == (columns & (GS - 1)), 1.0, 0.0)


def group_total(row, same):
    wide = jnp.broadcast_to(row, (8, C))
    return jnp.dot(wide, jnp.where(same, 1.0, 0.0), precision=lax.Precision.HIGHEST)


def stats_kernel(x_ref, out_ref):
    rows = x_ref.shape[0]
    cells = rows * x_ref.shape[1]
    same = same_group()

    def add_up(r, total):
        return total + jnp.sum(x_ref[r].astype(F32), axis=0, keepdims=True)

    mean = lax.fori_loop(0, rows, add_up, jnp.zeros((1, C), F32)) / cells

    def products(r, total):
        high, low = split(x_ref[r].astype(F32) - mean)
        return total + lax.dot_general(
            high,
            jnp.concatenate([high, low], axis=1),
            (((0,), (0,)), ((), ())),
            preferred_element_type=F32,
        )

    total = lax.fori_loop(0, rows, products, jnp.zeros((C, 2 * C), F32))
    cross = total[:, C:]
    out_ref[0:GS] = fold(total[:, :C] + cross + cross.T, same) / cells
    out_ref[GS : 2 * GS] = fold(jnp.broadcast_to(mean, (C, C)).T, same)
    out_ref[2 * GS : 2 * GS + 8] = jnp.broadcast_to(mean, (8, C))


def merge_kernel(a_ref, b_ref, out_ref):
    a, b = a_ref[...], b_ref[...]
    half = 0.5 * (a + b)
    gap = b - a
    wide = jnp.concatenate([gap[2 * GS :]] * (GS // 8), axis=0)
    out_ref[0:GS] = half[0:GS] + 0.25 * gap[GS : 2 * GS] * wide
    out_ref[GS:] = half[GS:]


def add_kernel(a_ref, b_ref, out_ref, token_ref):
    out_ref[...] = a_ref[...] + b_ref[...]
    leave(token_ref)


def shift_band(moved_ref, bands_ref, e, middle, left, right):
    d, pad, width = DILATION_RATE, 16, middle.shape[0]
    bands_ref[pad : pad + width] = middle.astype(F32)
    bands_ref[pad - 8 : pad] = left.astype(F32)
    bands_ref[pad + width : pad + width + 8] = right.astype(F32)
    moved_ref[0, e] = bands_ref[pad + d : pad + d + width].astype(BF16)
    moved_ref[1, e] = middle
    moved_ref[2, e] = bands_ref[pad - d : pad - d + width].astype(BF16)


def tap_rows(moved_ref, weight_ref, taps):
    bands = [moved_ref[b, band] for a, band in taps for b in range(3)]
    taps = [a for a, _ in taps]
    weights = [weight_ref[3 * a + b] for a in taps for b in range(3)]
    return dot(jnp.concatenate(bands, axis=1), jnp.concatenate(weights, axis=0))


def edge_kernel(up_ref, odd_ref, first_ref, second_ref):
    odd = odd_ref[0:1] > 0.5
    for r in range(up_ref.shape[0]):
        left, right = up_ref[r, :8].astype(F32), up_ref[r, up_ref.shape[1] - 8 :].astype(F32)
        first_ref[r] = jnp.where(odd, left, right).astype(BF16)
        second_ref[r] = jnp.where(odd, right, left).astype(BF16)


def pack_kernel(
    up_ref, early_ref, late_ref, odd_column_ref, odd_ref, left_ref, right_ref, first_ref, second_ref, token_ref
):
    rows, width = up_ref.shape[0], up_ref.shape[1]
    d = DILATION_RATE
    odd_column, odd = odd_column_ref[0:1] > 0.5, odd_ref[0:1] > 0.5
    for r in range(rows):
        early, late = early_ref[r].astype(F32), late_ref[r].astype(F32)
        left_ref[r] = jnp.where(odd_column, early, late).astype(BF16)
        right_ref[r] = jnp.where(odd_column, late, early).astype(BF16)
    for r in range(d):
        for begin, size, ref in ((0, width, up_ref), (width, 8, left_ref), (width + 8, 8, right_ref)):
            top, bottom = ref[r].astype(F32), ref[rows - d + r].astype(F32)
            first_ref[r, begin : begin + size] = jnp.where(odd, top, bottom).astype(BF16)
            second_ref[r, begin : begin + size] = jnp.where(odd, bottom, top).astype(BF16)
    leave(token_ref)


def bands_kernel(up_ref, left_ref, right_ref, w_ref, moved_ref, weight_ref, token_ref, bands_ref):
    rows = up_ref.shape[0]
    same = same_group()
    for tap in range(9):
        tile = jnp.concatenate([w_ref[tap].astype(F32)] * CHANNEL_GROUPS, axis=0)
        weight_ref[tap] = jnp.where(same, tile, 0.0).T.astype(BF16)

    def inner(r, carry):
        shift_band(moved_ref, bands_ref, r, up_ref[r], left_ref[r], right_ref[r])
        return carry

    lax.fori_loop(0, rows, inner, 0)
    leave(token_ref)


def near_kernel(moved_ref, weight_ref, out_ref, token_ref):
    rows = out_ref.shape[0]
    d = DILATION_RATE
    for first, last, taps in ((0, rows - d, {0: d, 1: 0}), (rows - d, d, {1: 0}), (d, rows, {1: 0, 2: -d})):

        def row(r, carry, taps=taps):
            out_ref[r] = tap_rows(moved_ref, weight_ref, [(a, r + step) for a, step in taps.items()])
            return carry

        lax.fori_loop(first, last, row, 0)
    leave(token_ref)


def far_kernel(odd_ref, first_ref, second_ref, weight_ref, near_ref, moved_ref, out_ref, token_ref, bands_ref):
    rows, width = out_ref.shape[0], out_ref.shape[1]
    d = DILATION_RATE

    def outer(r, carry):
        odd = odd_ref[0:1] > 0.5
        first, second = first_ref[r].astype(F32), second_ref[r].astype(F32)
        for begin, halo in ((0, jnp.where(odd, first, second)), (d, jnp.where(odd, second, first))):
            halo = halo.astype(BF16)
            shift_band(
                moved_ref, bands_ref, begin + r, halo[0:width], halo[width : width + 8], halo[width + 8 :]
            )
        return carry

    lax.fori_loop(0, d, outer, 0)
    back = 2 * d - rows
    for first, last, taps in ((0, rows - d, {2: 0}), (rows - d, d, {0: back, 2: 0}), (d, rows, {0: back})):

        def row(r, carry, taps=taps):
            far = tap_rows(moved_ref, weight_ref, [(a, r + step) for a, step in taps.items()])
            out_ref[r] = near_ref[r] + far
            return carry

        lax.fori_loop(first, last, row, 0)
    leave(token_ref)


def act_kernel(x_ref, stats_ref, gain_ref, bias_ref, turned_ref, slope_ref, kept_ref, mean_ref):
    rows, width = x_ref.shape[0], x_ref.shape[1]
    same = same_group()
    eye = unit()
    gain, bias = gain_ref[0:1], bias_ref[0:1]
    mean = stats_ref[2 * GS : 2 * GS + 1]
    cov = stats_ref[0:GS] + EPSILON * eye
    trace = group_total(jnp.sum(cov * eye, axis=0, keepdims=True), same)[0:1]
    normed = cov / trace
    normed_wide = spread_split(normed, same)
    iterate = 1.5 * eye - 0.5 * normed
    for k in range(ITERS - 1):
        wide = spread_split(iterate, same)
        square = times(iterate, wide)
        scaled = times(iterate, normed_wide)
        scaled_wide = spread_split(scaled, same)
        cube_scaled = times(square, scaled_wide)
        kept_ref[k, 0] = iterate
        kept_ref[k, 1] = square
        kept_ref[k, 2] = scaled
        iterate = 1.5 * iterate - 0.5 * cube_scaled
    whitener = iterate * lax.rsqrt(trace)
    mean_wide = jnp.broadcast_to(mean, (8, C))
    kept_ref[ITERS - 1, 0] = whitener
    kept_ref[ITERS - 1, 1] = normed
    kept_ref[ITERS - 1, 2] = jnp.broadcast_to(trace, (GS, C))
    mean_ref[...] = mean_wide
    white_high, white_low = spread_split(whitener, same)
    rounded = white_high.astype(F32) + white_low.astype(F32)
    offset = jnp.dot(mean_wide, rounded, precision=lax.Precision.HIGHEST)[0:1]

    for r in range(rows):
        x = x_ref[r]
        white = dot(x, white_high) + dot(x, white_low) - offset
        pre = gain * white + bias
        gate = 0.5 * jnp.tanh(0.5 * pre) + 0.5
        act = pre * gate
        turned_ref[:, r * width : (r + 1) * width] = act.T.astype(BF16)
        slope_ref[r] = gate + act * (1.0 - gate)


def tap_kernel(turned_ref, near_ref, far_ref, later_ref, own_ref, other_ref, total_ref):
    rows, width = near_ref.shape[1], near_ref.shape[2]
    d = DILATION_RATE
    gap = rows - d
    same = same_group()

    def pair(b, first, count, ref, band):
        turned = turned_ref[:, first * width : (first + count) * width]
        return dot(turned, ref[b, band : band + count].reshape(count * width, C))

    def column(b, carry):
        total_ref[b] = fold(pair(b, 0, gap, near_ref, d) + pair(b, gap, d, far_ref, d), same)
        total_ref[3 + b] = fold(pair(b, 0, rows, near_ref, 0), same)
        total_ref[6 + b] = fold(pair(b, 0, d, far_ref, 0) + pair(b, d, gap, near_ref, 0), same)
        return carry

    lax.fori_loop(0, 3, column, 0)
    later = later_ref[0:1] > 0.5
    total = total_ref[...].reshape(9 * GS, C)
    first, second = total[: own_ref.shape[0]], total[own_ref.shape[0] :]
    own_ref[...] = jnp.where(later, second, first)
    other_ref[...] = jnp.where(later, first, second)


def join_kernel(scale, own_ref, other_ref, later_ref, out_ref):
    later = later_ref[0:1] > 0.5
    own, other = own_ref[...] * scale, other_ref[...] * scale
    size = own.shape[0]
    out_ref[:size] = jnp.where(later, other, own)
    out_ref[size:] = jnp.where(later, own, other)


def grad_kernel(x_ref, grad_ref, slope_ref, kept_ref, mean_ref, gain_ref, back_ref, sums_ref):
    rows = x_ref.shape[0]
    same = same_group()
    gain = gain_ref[0:1]
    whitener = spread(kept_ref[ITERS - 1, 0], same)
    weighted_high, weighted_low = split((whitener * gain).T)

    def row(r, carry):
        bias_sum, total = carry
        pre_grad = grad_ref[r] * slope_ref[r]
        bias_sum = bias_sum + jnp.sum(pre_grad, axis=0, keepdims=True)
        high, low = split(pre_grad)
        back_ref[r] = dot(high, weighted_high) + dot(low, weighted_high) + dot(high, weighted_low)
        turn = lambda part: lax.dot_general(x_ref[r], part, (((0,), (0,)), ((), ())), preferred_element_type=F32)
        return bias_sum, total + turn(high) + turn(low)

    bias_sum, total = lax.fori_loop(0, rows, row, (jnp.zeros((1, C), F32), jnp.zeros((C, C), F32)))
    mean_column = jnp.broadcast_to(mean_ref[0:1], (C, C)).T
    full = total - mean_column * bias_sum
    gain_sum = jnp.sum(full * whitener, axis=0, keepdims=True)
    full = full * gain
    sums_ref[0:GS] = fold(full + full.T, same)
    line = lax.broadcasted_iota(jnp.int32, (8, C), 0)
    sums_ref[GS : GS + 8] = jnp.where(line == 0, gain_sum, jnp.where(line == 1, bias_sum, 0.0))


def prepare_kernel(kept_ref, mean_ref, gain_ref, wide_ref, lines_ref, token_ref):
    same = same_group()

    def put(place, packed):
        high, low = spread_split(packed, same)
        wide_ref[place, 0] = high
        wide_ref[place, 1] = low

    for k in range(ITERS - 1):
        iterate, square, scaled = kept_ref[k, 0], kept_ref[k, 1], kept_ref[k, 2]
        put(2 * k, scaled)
        put(2 * k + 1, times(iterate, (wide_ref[2 * k, 0], wide_ref[2 * k, 1])))
        lines_ref[0, k] = iterate
        lines_ref[1, k] = square
        lines_ref[2, k] = times(square, spread_split(iterate, same))
    put(2 * ITERS - 2, kept_ref[ITERS - 1, 1])
    for k in range(3):
        lines_ref[3, k] = kept_ref[ITERS - 1, k]
    lines_ref[3, 3, 0:8] = mean_ref[...]
    lines_ref[3, 3, 8:16] = gain_ref[...]
    lines_ref[3, 3, 16:] = jnp.zeros((GS - 16, C), F32)
    leave(token_ref)


def final_kernel(cell_count, x_ref, back_ref, sums_ref, wide_ref, lines_ref, out_ref, gain_out_ref, bias_out_ref):
    high, low, constant = derivative(cell_count, sums_ref, wide_ref, lines_ref)
    for r in range(x_ref.shape[0]):
        moved = dot(x_ref[r], high) + dot(x_ref[r], low)
        out_ref[r] = (moved + back_ref[r] - constant).astype(BF16)
    for line, ref in enumerate((gain_out_ref, bias_out_ref)):
        ref[...] = sums_ref[GS + line] * (1.0 / math.sqrt(cell_count))


def derivative(cell_count, sums_ref, wide_ref, lines_ref):
    same = same_group()
    eye = unit()
    whitener, normed = lines_ref[3, 0], lines_ref[3, 1]
    trace = lines_ref[3, 2, 0:1]
    mean, gain = lines_ref[3, 3, 0:8], lines_ref[3, 3, 8:16]
    paired = sums_ref[0:GS]
    step = paired * lax.rsqrt(trace)
    wide = lambda place: (wide_ref[place, 0], wide_ref[place, 1])
    direct = times(lines_ref[2].reshape((ITERS - 1) * GS, C), spread_split(step, same))
    change = -0.5 * step
    for k in range(ITERS - 1):
        moved = direct[k * GS : (k + 1) * GS] + times(change, wide(2 * k + 1))
        moved = moved + times(lines_ref[0, k], spread_split(times(change, wide(2 * k)), same))
        moved = moved + times(lines_ref[1, k], spread_split(times(change, wide(2 * ITERS - 2)), same))
        change = 1.5 * change - 0.5 * moved
    inner = jnp.sum(change * normed + 0.5 * paired * whitener, axis=0, keepdims=True)
    symmetric = (change - eye * group_total(inner, same)[0:1]) / trace
    high, low = spread_split(symmetric * (1.0 / cell_count), same)
    rounded = high.astype(F32) + low.astype(F32)
    bias_sum = sums_ref[GS + 1 : GS + 2]
    weighted = gain * bias_sum * (1.0 / cell_count)
    both = jnp.concatenate([mean, weighted], axis=1)
    constant = jnp.dot(
        both, jnp.concatenate([rounded, spread(whitener, same)], axis=0), precision=lax.Precision.HIGHEST
    )
    return high, low, constant[0:1]


def stages(axes):
    for axis in axes:
        size = lax.axis_size(axis)
        stride = 1
        while stride < size:
            yield axis, [(i, i ^ stride) for i in range(size)]
            stride *= 2


def add(part, other, after=()):
    return run(add_kernel, (jax.ShapeDtypeStruct(part.shape, F32), TOKEN), (part, other), after=after)


def swap(earlier, later, axis):
    size = lax.axis_size(axis)
    got = []
    for begin, part in ((0, earlier), (1, later)):
        pairs = [(i, i + 1) for i in range(begin, size - 1, 2)]
        pairs = pairs + [(j, i) for i, j in pairs]
        got.append(lax.ppermute(part, axis, pairs) if pairs else jnp.zeros_like(part))
    return got


def shards(features, upstream, conv_weight, norm_gain, norm_bias):
    mos_n, rows, width, _ = features.shape
    axes = ("dp", "cols", "rows")
    cell_count = mos_n * rows * width
    for axis in axes:
        cell_count *= lax.axis_size(axis)
    stage_pairs = list(stages(axes))
    count = len(stage_pairs)
    d = DILATION_RATE
    x = features.reshape(rows, width, C)
    up = upstream.reshape(rows, width, C)
    gain = jnp.broadcast_to(norm_gain[None], (8, C))
    bias = jnp.broadcast_to(norm_bias[None], (8, C))
    shape = jax.ShapeDtypeStruct
    held = pltpu.VMEM
    cells = (rows, width, C)

    odd_line = lambda axis: jnp.broadcast_to((lax.axis_index(axis) % 2 == 1).astype(F32), (8, C))
    tap_axis, tap_pairs = stage_pairs[0]
    odd_column, odd_row, later_line = odd_line("cols"), odd_line("rows"), odd_line(tap_axis)
    edge = shape((rows, 8, C), BF16)
    first, second = run(edge_kernel, (edge, edge), (up, odd_column), after=(odd_row, later_line))
    first, second = swap(first, second, "cols")
    halo = shape((d, width + 16, C), BF16)
    left, right, first, second, token = run(
        pack_kernel, (edge, edge, halo, halo, TOKEN), (up, first, second, odd_column, odd_row)
    )
    first, second = swap(first, second, "rows")
    stats = run(stats_kernel, shape((2 * GS + 8, C), F32), (x,), after=(token,))
    scratch = (pltpu.VMEM((width + 32, C), F32),)
    for number, (axis, pairs) in enumerate(stage_pairs):
        other = lax.ppermute(stats, axis, pairs)
        token = ()
        if number == count - 3:
            near_bands, weights, *token = run(
                bands_kernel,
                (held((3,) + cells, BF16), held((9, C, C), BF16), TOKEN),
                (up, left, right, conv_weight.reshape(9, GS, C)),
                scratch=scratch,
                after=(stats,),
            )
        if number == count - 2:
            near_grad, *token = run(
                near_kernel, (held(cells, F32), TOKEN), (near_bands, weights), after=(stats,)
            )
        if number == count - 1:
            far_bands, act_grad, *token = run(
                far_kernel,
                (held((3, 2 * d, width, C), BF16), held(cells, F32), TOKEN),
                (odd_row, first, second, weights, near_grad),
                scratch=scratch,
                after=(stats,),
            )
        stats = run(merge_kernel, shape(stats.shape, F32), (stats, other), after=token)

    turned, slope, kept, mean = run(
        act_kernel,
        (
            held((C, rows * width), BF16),
            held(cells, F32),
            held((ITERS, 3, GS, C), F32),
            held((8, C), F32),
        ),
        (x, stats, gain, bias),
    )
    half = shape((9 * GS // 2, C), F32)
    half, other = run(
        tap_kernel,
        (half, half),
        (turned, near_bands, far_bands, later_line),
        scratch=(pltpu.VMEM((9, GS, C), F32),),
    )
    half, _ = add(half, lax.ppermute(other, tap_axis, tap_pairs))

    back, sums = run(
        grad_kernel,
        (held(cells, F32), shape((GS + 8, C), F32)),
        (x, act_grad, slope, kept, mean, gain),
        after=(half,),
    )
    row_stages = [stage for stage in stage_pairs[1:] if stage[0] == "rows"]
    tap_stages = row_stages + [stage for stage in stage_pairs[1:] if stage[0] != "rows"]
    in_flight = lax.ppermute(half, *tap_stages[0])
    for number, stage in enumerate(stage_pairs):
        other = lax.ppermute(sums, *stage)
        token = ()
        if number == 1 or 2 < number:
            half, *token = add(half, in_flight, after=(sums,))
            in_flight = lax.ppermute(half, *tap_stages[max(number - 1, 1)])
        if number == count - 1:
            wide, lines, tag = run(
                prepare_kernel,
                (held((2 * ITERS - 1, 2, C, C), BF16), held((4, ITERS - 1, GS, C), F32), TOKEN),
                (kept, mean, gain),
                after=(sums,),
            )
            token = [*token, tag]
        sums, _ = add(sums, other, after=token)
    half, _ = add(half, in_flight, after=(sums,))
    input_grad, gain_grad, bias_grad = run(
        functools.partial(final_kernel, cell_count),
        (shape(cells, BF16), shape((C,), F32), shape((C,), F32)),
        (x, back, sums, wide, lines),
        after=(half,),
    )
    other = lax.ppermute(half, tap_axis, tap_pairs)
    taps = run(
        functools.partial(join_kernel, 1.0 / math.sqrt(cell_count)),
        shape((9 * GS, C), F32),
        (half, other, later_line),
    )
    return (
        input_grad.reshape(features.shape),
        taps.reshape(3, 3, GS, C),
        gain_grad,
        bias_grad,
    )


def solution(mesh):
    placed = (P("dp", "rows", "cols", None), P("dp", "rows", "cols", None), P(), P(), P())
    return jax.shard_map(
        shards,
        mesh=mesh,
        in_specs=placed,
        out_specs=(P("dp", "rows", "cols", None), P(), P(), P()),
        check_vma=False,
    )
```

```python
import functools
import math

import jax
import jax.numpy as jnp
from jax import lax
from jax.experimental import pallas as pl
from jax.experimental.pallas import tpu as pltpu
from jax.sharding import PartitionSpec as P

C = 256
CHANNEL_GROUPS = 8
GS = 32
DILATION_RATE = 6
ITERS = 5
EPSILON = 1e-05

F32 = jnp.float32
BF16 = jnp.bfloat16
VMEM_SPEC = pl.BlockSpec(memory_space=pltpu.VMEM)
NO_COST = pl.CostEstimate(flops=0, bytes_accessed=0, transcendentals=0)


def run(body, out_shapes, operands, scratch=(), after=()):
    many = isinstance(out_shapes, (tuple, list))
    count = len(operands)

    def kernel(*refs):
        body(*refs[:count], *refs[count + len(after) :])

    return pl.pallas_call(
        kernel,
        out_shape=out_shapes,
        in_specs=[VMEM_SPEC] * count + [pl.BlockSpec(memory_space=pl.ANY)] * len(after),
        out_specs=[VMEM_SPEC] * len(out_shapes) if many else VMEM_SPEC,
        scratch_shapes=list(scratch),
        compiler_params=pltpu.CompilerParams(vmem_limit_bytes=8 * 2**20),
        cost_estimate=NO_COST,
    )(*operands, *after)


TOKEN = jax.ShapeDtypeStruct((8, 128), F32)


def leave(token_ref):
    token_ref[...] = jnp.zeros(token_ref.shape, F32)


def same_group():
    rows = lax.broadcasted_iota(jnp.int32, (C, C), 0)
    columns = lax.broadcasted_iota(jnp.int32, (C, C), 1)
    return (rows >> 5) == (columns >> 5)


def fold(full, same):
    kept = jnp.where(same, full, 0.0)
    total = kept[0:GS]
    for g in range(1, CHANNEL_GROUPS):
        total = total + kept[g * GS : (g + 1) * GS]
    return total


def spread(packed, same):
    return jnp.where(same, jnp.concatenate([packed] * CHANNEL_GROUPS, axis=0), 0)


def split(value):
    high = value.astype(BF16)
    low = (value - high.astype(F32)).astype(BF16)
    return high, low


def spread_split(packed, same):
    high, low = split(spread(packed, same))
    return high, low


def dot(a, b):
    return jnp.dot(a, b, preferred_element_type=F32)


def times(left, right):
    rows = left.shape[0]
    left_high, left_low = split(left)
    right_high, right_low = right
    both = dot(jnp.concatenate([left_high, left_low], axis=0), right_high)
    return both[:rows] + both[rows:] + dot(left_high, right_low)


def unit():
    rows = lax.broadcasted_iota(jnp.int32, (GS, C), 0)
    columns = lax.broadcasted_iota(jnp.int32, (GS, C), 1)
    return jnp.where(rows == (columns & (GS - 1)), 1.0, 0.0)


def group_total(row, same):
    wide = jnp.broadcast_to(row, (8, C))
    return jnp.dot(wide, jnp.where(same, 1.0, 0.0), precision=lax.Precision.HIGHEST)


def stats_kernel(x_ref, out_ref):
    rows = x_ref.shape[0]
    cells = rows * x_ref.shape[1]
    same = same_group()

    def add_up(r, total):
        return total + jnp.sum(x_ref[r].astype(F32), axis=0, keepdims=True)

    mean = lax.fori_loop(0, rows, add_up, jnp.zeros((1, C), F32)) / cells

    def products(r, total):
        high, low = split(x_ref[r].astype(F32) - mean)
        return total + lax.dot_general(
            high,
            jnp.concatenate([high, low], axis=1),
            (((0,), (0,)), ((), ())),
            preferred_element_type=F32,
        )

    total = lax.fori_loop(0, rows, products, jnp.zeros((C, 2 * C), F32))
    cross = total[:, C:]
    out_ref[0:GS] = fold(total[:, :C] + cross + cross.T, same) / cells
    out_ref[GS : 2 * GS] = fold(jnp.broadcast_to(mean, (C, C)).T, same)
    out_ref[2 * GS : 2 * GS + 8] = jnp.broadcast_to(mean, (8, C))


def merge_kernel(a_ref, b_ref, out_ref):
    a, b = a_ref[...], b_ref[...]
    half = 0.5 * (a + b)
    gap = b - a
    wide = jnp.concatenate([gap[2 * GS :]] * (GS // 8), axis=0)
    out_ref[0:GS] = half[0:GS] + 0.25 * gap[GS : 2 * GS] * wide
    out_ref[GS:] = half[GS:]


def add_kernel(a_ref, b_ref, out_ref):
    out_ref[...] = a_ref[...] + b_ref[...]


def shift_band(moved_ref, bands_ref, e, middle, left, right):
    d, pad, width = DILATION_RATE, 16, middle.shape[0]
    bands_ref[pad : pad + width] = middle.astype(F32)
    bands_ref[pad - 8 : pad] = left.astype(F32)
    bands_ref[pad + width : pad + width + 8] = right.astype(F32)
    moved_ref[0, e] = bands_ref[pad + d : pad + d + width].astype(BF16)
    moved_ref[1, e] = middle
    moved_ref[2, e] = bands_ref[pad - d : pad - d + width].astype(BF16)


def tap_rows(moved_ref, weight_ref, taps):
    bands = [moved_ref[b, band] for a, band in taps for b in range(3)]
    taps = [a for a, _ in taps]
    weights = [weight_ref[3 * a + b] for a in taps for b in range(3)]
    return dot(jnp.concatenate(bands, axis=1), jnp.concatenate(weights, axis=0))


def pick(odd, first, second):
    return jnp.where(odd, first.astype(F32), second.astype(F32)).astype(BF16)


def pack_kernel(up_ref, odd_row_ref, odd_column_ref, first_ref, second_ref, early_ref, late_ref, token_ref):
    rows, width = up_ref.shape[0], up_ref.shape[1]
    d = DILATION_RATE
    odd_row, odd_column = odd_row_ref[0:1] > 0.5, odd_column_ref[0:1] > 0.5
    for r in range(d):
        top, bottom = up_ref[r], up_ref[rows - d + r]
        first_ref[r] = pick(odd_row, top, bottom)
        second_ref[r] = pick(odd_row, bottom, top)
    for r in range(rows):
        left, right = up_ref[r, :8], up_ref[r, width - 8 :]
        early_ref[r] = pick(odd_column, left, right)
        late_ref[r] = pick(odd_column, right, left)
    leave(token_ref)


def rim_kernel(first_ref, second_ref, odd_row_ref, odd_column_ref, early_ref, late_ref, token_ref):
    d, width = first_ref.shape[0], first_ref.shape[1]
    odd_row, odd_column = odd_row_ref[0:1] > 0.5, odd_column_ref[0:1] > 0.5
    for r in range(d):
        first = [first_ref[r, :8], first_ref[r, width - 8 :]]
        second = [second_ref[r, :8], second_ref[r, width - 8 :]]
        for place, one, two in ((r, first, second), (d + r, second, first)):
            left, right = pick(odd_row, one[0], two[0]), pick(odd_row, one[1], two[1])
            early_ref[place] = pick(odd_column, left, right)
            late_ref[place] = pick(odd_column, right, left)
    leave(token_ref)


def bands_kernel(up_ref, early_ref, late_ref, odd_column_ref, w_ref, moved_ref, weight_ref, token_ref, bands_ref):
    rows = up_ref.shape[0]
    same = same_group()
    for tap in range(9):
        tile = jnp.concatenate([w_ref[tap].astype(F32)] * CHANNEL_GROUPS, axis=0)
        weight_ref[tap] = jnp.where(same, tile, 0.0).T.astype(BF16)

    def inner(r, carry):
        early, late = early_ref[r], late_ref[r]
        odd = odd_column_ref[0:1] > 0.5
        shift_band(moved_ref, bands_ref, r, up_ref[r], pick(odd, early, late), pick(odd, late, early))
        return carry

    lax.fori_loop(0, rows, inner, 0)
    leave(token_ref)


def near_kernel(moved_ref, weight_ref, out_ref, token_ref):
    rows = out_ref.shape[0]
    d = DILATION_RATE
    for first, last, taps in ((0, rows - d, {0: d, 1: 0}), (rows - d, d, {1: 0}), (d, rows, {1: 0, 2: -d})):

        def row(r, carry, taps=taps):
            out_ref[r] = tap_rows(moved_ref, weight_ref, [(a, r + step) for a, step in taps.items()])
            return carry

        lax.fori_loop(first, last, row, 0)
    leave(token_ref)


def far_kernel(
    odd_row_ref, odd_column_ref, first_ref, second_ref, early_ref, late_ref, weight_ref, near_ref,
    moved_ref, out_ref, token_ref, bands_ref,
):
    rows, width = out_ref.shape[0], out_ref.shape[1]
    d = DILATION_RATE

    def outer(r, carry):
        odd_row, odd_column = odd_row_ref[0:1] > 0.5, odd_column_ref[0:1] > 0.5
        first, second = first_ref[r], second_ref[r]
        for begin, halo in ((0, pick(odd_row, first, second)), (d, pick(odd_row, second, first))):
            early, late = early_ref[begin + r], late_ref[begin + r]
            left, right = pick(odd_column, early, late), pick(odd_column, late, early)
            shift_band(moved_ref, bands_ref, begin + r, halo, left, right)
        return carry

    lax.fori_loop(0, d, outer, 0)
    back = 2 * d - rows
    for first, last, taps in ((0, rows - d, {2: 0}), (rows - d, d, {0: back, 2: 0}), (d, rows, {0: back})):

        def row(r, carry, taps=taps):
            far = tap_rows(moved_ref, weight_ref, [(a, r + step) for a, step in taps.items()])
            out_ref[r] = near_ref[r] + far
            return carry

        lax.fori_loop(first, last, row, 0)
    leave(token_ref)


def act_kernel(x_ref, stats_ref, gain_ref, bias_ref, turned_ref, slope_ref, kept_ref, mean_ref):
    rows, width = x_ref.shape[0], x_ref.shape[1]
    same = same_group()
    eye = unit()
    gain, bias = gain_ref[0:1], bias_ref[0:1]
    mean = stats_ref[2 * GS : 2 * GS + 1]
    cov = stats_ref[0:GS] + EPSILON * eye
    trace = group_total(jnp.sum(cov * eye, axis=0, keepdims=True), same)[0:1]
    normed = cov / trace
    normed_wide = spread_split(normed, same)
    iterate = 1.5 * eye - 0.5 * normed
    for k in range(ITERS - 1):
        wide = spread_split(iterate, same)
        square = times(iterate, wide)
        scaled = times(iterate, normed_wide)
        scaled_wide = spread_split(scaled, same)
        cube_scaled = times(square, scaled_wide)
        kept_ref[k, 0] = iterate
        kept_ref[k, 1] = square
        kept_ref[k, 2] = scaled
        iterate = 1.5 * iterate - 0.5 * cube_scaled
    whitener = iterate * lax.rsqrt(trace)
    mean_wide = jnp.broadcast_to(mean, (8, C))
    kept_ref[ITERS - 1, 0] = whitener
    kept_ref[ITERS - 1, 1] = normed
    kept_ref[ITERS - 1, 2] = jnp.broadcast_to(trace, (GS, C))
    mean_ref[...] = mean_wide
    white_high, white_low = spread_split(whitener, same)
    rounded = white_high.astype(F32) + white_low.astype(F32)
    offset = jnp.dot(mean_wide, rounded, precision=lax.Precision.HIGHEST)[0:1]

    for r in range(rows):
        x = x_ref[r]
        white = dot(x, white_high) + dot(x, white_low) - offset
        pre = gain * white + bias
        gate = 0.5 * jnp.tanh(0.5 * pre) + 0.5
        act = pre * gate
        turned_ref[:, r * width : (r + 1) * width] = act.T.astype(BF16)
        slope_ref[r] = gate + act * (1.0 - gate)


def tap_kernel(turned_ref, near_ref, far_ref, later_ref, own_ref, other_ref, total_ref):
    rows, width = near_ref.shape[1], near_ref.shape[2]
    d = DILATION_RATE
    gap = rows - d
    same = same_group()

    def pair(b, first, count, ref, band):
        turned = turned_ref[:, first * width : (first + count) * width]
        return dot(turned, ref[b, band : band + count].reshape(count * width, C))

    def column(b, carry):
        total_ref[b] = fold(pair(b, 0, gap, near_ref, d) + pair(b, gap, d, far_ref, d), same)
        total_ref[3 + b] = fold(pair(b, 0, rows, near_ref, 0), same)
        total_ref[6 + b] = fold(pair(b, 0, d, far_ref, 0) + pair(b, d, gap, near_ref, 0), same)
        return carry

    lax.fori_loop(0, 3, column, 0)
    later = later_ref[0:1] > 0.5
    total = total_ref[...].reshape(9 * GS, C)
    first, second = total[: own_ref.shape[0]], total[own_ref.shape[0] :]
    own_ref[...] = jnp.where(later, second, first)
    other_ref[...] = jnp.where(later, first, second)


def join_kernel(scale, own_ref, other_ref, later_ref, out_ref):
    later = later_ref[0:1] > 0.5
    own, other = own_ref[...] * scale, other_ref[...] * scale
    size = own.shape[0]
    out_ref[:size] = jnp.where(later, other, own)
    out_ref[size:] = jnp.where(later, own, other)


def grad_kernel(x_ref, grad_ref, slope_ref, kept_ref, mean_ref, gain_ref, back_ref, sums_ref):
    rows = x_ref.shape[0]
    same = same_group()
    gain = gain_ref[0:1]
    whitener = spread(kept_ref[ITERS - 1, 0], same)
    weighted_high, weighted_low = split((whitener * gain).T)

    def row(r, carry):
        bias_sum, total = carry
        pre_grad = grad_ref[r] * slope_ref[r]
        bias_sum = bias_sum + jnp.sum(pre_grad, axis=0, keepdims=True)
        high, low = split(pre_grad)
        back_ref[r] = dot(high, weighted_high) + dot(low, weighted_high) + dot(high, weighted_low)
        turn = lambda part: lax.dot_general(x_ref[r], part, (((0,), (0,)), ((), ())), preferred_element_type=F32)
        return bias_sum, total + turn(high) + turn(low)

    bias_sum, total = lax.fori_loop(0, rows, row, (jnp.zeros((1, C), F32), jnp.zeros((C, C), F32)))
    mean_column = jnp.broadcast_to(mean_ref[0:1], (C, C)).T
    full = total - mean_column * bias_sum
    gain_sum = jnp.sum(full * whitener, axis=0, keepdims=True)
    full = full * gain
    sums_ref[0:GS] = fold(full + full.T, same)
    line = lax.broadcasted_iota(jnp.int32, (8, C), 0)
    sums_ref[GS : GS + 8] = jnp.where(line == 0, gain_sum, jnp.where(line == 1, bias_sum, 0.0))


def prepare_kernel(kept_ref, mean_ref, gain_ref, wide_ref, lines_ref, token_ref):
    same = same_group()

    def put(place, packed):
        high, low = spread_split(packed, same)
        wide_ref[place, 0] = high
        wide_ref[place, 1] = low

    for k in range(ITERS - 1):
        iterate, square, scaled = kept_ref[k, 0], kept_ref[k, 1], kept_ref[k, 2]
        put(2 * k, scaled)
        put(2 * k + 1, times(iterate, (wide_ref[2 * k, 0], wide_ref[2 * k, 1])))
        lines_ref[0, k] = iterate
        lines_ref[1, k] = square
        lines_ref[2, k] = times(square, spread_split(iterate, same))
    put(2 * ITERS - 2, kept_ref[ITERS - 1, 1])
    for k in range(3):
        lines_ref[3, k] = kept_ref[ITERS - 1, k]
    lines_ref[3, 3, 0:8] = mean_ref[...]
    lines_ref[3, 3, 8:16] = gain_ref[...]
    lines_ref[3, 3, 16:] = jnp.zeros((GS - 16, C), F32)
    leave(token_ref)


def final_kernel(cell_count, x_ref, back_ref, sums_ref, wide_ref, lines_ref, out_ref, gain_out_ref, bias_out_ref):
    high, low, constant = derivative(cell_count, sums_ref, wide_ref, lines_ref)
    for r in range(x_ref.shape[0]):
        moved = dot(x_ref[r], high) + dot(x_ref[r], low)
        out_ref[r] = (moved + back_ref[r] - constant).astype(BF16)
    for line, ref in enumerate((gain_out_ref, bias_out_ref)):
        ref[...] = sums_ref[GS + line] * (1.0 / math.sqrt(cell_count))


def derivative(cell_count, sums_ref, wide_ref, lines_ref):
    same = same_group()
    eye = unit()
    whitener, normed = lines_ref[3, 0], lines_ref[3, 1]
    trace = lines_ref[3, 2, 0:1]
    mean, gain = lines_ref[3, 3, 0:8], lines_ref[3, 3, 8:16]
    paired = sums_ref[0:GS]
    step = paired * lax.rsqrt(trace)
    wide = lambda place: (wide_ref[place, 0], wide_ref[place, 1])
    direct = times(lines_ref[2].reshape((ITERS - 1) * GS, C), spread_split(step, same))
    change = -0.5 * step
    for k in range(ITERS - 1):
        moved = direct[k * GS : (k + 1) * GS] + times(change, wide(2 * k + 1))
        moved = moved + times(lines_ref[0, k], spread_split(times(change, wide(2 * k)), same))
        moved = moved + times(lines_ref[1, k], spread_split(times(change, wide(2 * ITERS - 2)), same))
        change = 1.5 * change - 0.5 * moved
    inner = jnp.sum(change * normed + 0.5 * paired * whitener, axis=0, keepdims=True)
    symmetric = (change - eye * group_total(inner, same)[0:1]) / trace
    high, low = spread_split(symmetric * (1.0 / cell_count), same)
    rounded = high.astype(F32) + low.astype(F32)
    bias_sum = sums_ref[GS + 1 : GS + 2]
    weighted = gain * bias_sum * (1.0 / cell_count)
    both = jnp.concatenate([mean, weighted], axis=1)
    constant = jnp.dot(
        both, jnp.concatenate([rounded, spread(whitener, same)], axis=0), precision=lax.Precision.HIGHEST
    )
    return high, low, constant[0:1]


def stages(axes):
    for axis in axes:
        size = lax.axis_size(axis)
        stride = 1
        while stride < size:
            yield axis, [(i, i ^ stride) for i in range(size)]
            stride *= 2


def add(part, other, after=()):
    if not after:
        return part + other
    return run(add_kernel, jax.ShapeDtypeStruct(part.shape, F32), (part, other), after=after)


def swap(earlier, later, axis):
    size = lax.axis_size(axis)
    got = []
    for begin, part in ((0, earlier), (1, later)):
        pairs = [(i, i + 1) for i in range(begin, size - 1, 2)]
        pairs = pairs + [(j, i) for i, j in pairs]
        got.append(lax.ppermute(part, axis, pairs) if pairs else jnp.zeros_like(part))
    return got


def shards(features, upstream, conv_weight, norm_gain, norm_bias):
    mos_n, rows, width, _ = features.shape
    axes = ("dp", "cols", "rows")
    cell_count = mos_n * rows * width
    for axis in axes:
        cell_count *= lax.axis_size(axis)
    stage_pairs = list(stages(axes))
    count = len(stage_pairs)
    d = DILATION_RATE
    x = features.reshape(rows, width, C)
    up = upstream.reshape(rows, width, C)
    gain = jnp.broadcast_to(norm_gain[None], (8, C))
    bias = jnp.broadcast_to(norm_bias[None], (8, C))
    shape = jax.ShapeDtypeStruct
    held = pltpu.VMEM
    cells = (rows, width, C)

    odd_line = lambda axis: jnp.broadcast_to((lax.axis_index(axis) % 2 == 1).astype(F32), (8, C))
    tap_axis, tap_pairs = stage_pairs[0]
    odd_column, odd_row, later_line = odd_line("cols"), odd_line("rows"), odd_line(tap_axis)
    edge, halo, rim = (shape((size[0], size[1], C), BF16) for size in ((rows, 8), (d, width), (2 * d, 8)))
    first, second, early, late, token = run(
        pack_kernel, (halo, halo, edge, edge, TOKEN), (up, odd_row, odd_column), after=(later_line,)
    )
    first, second = swap(first, second, "rows")
    early, late = swap(early, late, "cols")
    stats = run(stats_kernel, shape((2 * GS + 8, C), F32), (x,), after=(token,))
    scratch = (pltpu.VMEM((width + 32, C), F32),)
    for number, (axis, pairs) in enumerate(stage_pairs):
        other = lax.ppermute(stats, axis, pairs)
        token = ()
        if number == count - 3:
            near_bands, weights, *token = run(
                bands_kernel,
                (held((3,) + cells, BF16), held((9, C, C), BF16), TOKEN),
                (up, early, late, odd_column, conv_weight.reshape(9, GS, C)),
                scratch=scratch,
                after=(stats,),
            )
        if number == count - 2:
            near_grad, tag = run(near_kernel, (held(cells, F32), TOKEN), (near_bands, weights), after=(stats,))
            rims = run(rim_kernel, (rim, rim, TOKEN), (first, second, odd_row, odd_column), after=(tag,))
            token = (rims[2],)
            rims = swap(rims[0], rims[1], "cols")
        if number == count - 1:
            far_bands, act_grad, *token = run(
                far_kernel,
                (held((3, 2 * d, width, C), BF16), held(cells, F32), TOKEN),
                (odd_row, odd_column, first, second, *rims, weights, near_grad),
                scratch=scratch,
                after=(stats,),
            )
        stats = run(merge_kernel, shape(stats.shape, F32), (stats, other), after=token)

    turned, slope, kept, mean = run(
        act_kernel,
        (
            held((C, rows * width), BF16),
            held(cells, F32),
            held((ITERS, 3, GS, C), F32),
            held((8, C), F32),
        ),
        (x, stats, gain, bias),
    )
    half = shape((9 * GS // 2, C), F32)
    half, other = run(
        tap_kernel,
        (half, half),
        (turned, near_bands, far_bands, later_line),
        scratch=(pltpu.VMEM((9, GS, C), F32),),
    )
    half = add(half, lax.ppermute(other, tap_axis, tap_pairs))

    back, sums = run(
        grad_kernel,
        (held(cells, F32), shape((GS + 8, C), F32)),
        (x, act_grad, slope, kept, mean, gain),
        after=(half,),
    )
    row_stages = [stage for stage in stage_pairs[1:] if stage[0] == "rows"]
    tap_stages = row_stages + [stage for stage in stage_pairs[1:] if stage[0] != "rows"]
    half = add(half, lax.ppermute(half, *tap_stages[0]), after=(sums,))
    for number, stage in enumerate(stage_pairs):
        other = lax.ppermute(sums, *stage)
        token = ()
        if number == count - 1:
            wide, lines, *token = run(
                prepare_kernel,
                (held((2 * ITERS - 1, 2, C, C), BF16), held((4, ITERS - 1, GS, C), F32), TOKEN),
                (kept, mean, gain),
                after=(sums,),
            )
        sums = add(sums, other, after=token)
        if 2 <= number < count:
            half = add(half, lax.ppermute(half, *tap_stages[number - 1]), after=(sums,))
    input_grad, gain_grad, bias_grad = run(
        functools.partial(final_kernel, cell_count),
        (shape(cells, BF16), shape((C,), F32), shape((C,), F32)),
        (x, back, sums, wide, lines),
        after=(half,),
    )
    other = lax.ppermute(half, tap_axis, tap_pairs)
    taps = run(
        functools.partial(join_kernel, 1.0 / math.sqrt(cell_count)),
        shape((9 * GS, C), F32),
        (half, other, later_line),
    )
    return (
        input_grad.reshape(features.shape),
        taps.reshape(3, 3, GS, C),
        gain_grad,
        bias_grad,
    )


def solution(mesh):
    placed = (P("dp", "rows", "cols", None), P("dp", "rows", "cols", None), P(), P(), P())
    return jax.shard_map(
        shards,
        mesh=mesh,
        in_specs=placed,
        out_specs=(P("dp", "rows", "cols", None), P(), P(), P()),
        check_vma=False,
    )
```

```python
import functools
import math

import jax
import jax.numpy as jnp
from jax import lax
from jax.experimental import pallas as pl
from jax.experimental.pallas import tpu as pltpu
from jax.sharding import PartitionSpec as P

C = 256
CHANNEL_GROUPS = 8
GS = 32
DILATION_RATE = 6
ITERS = 5
EPSILON = 1e-05

F32 = jnp.float32
BF16 = jnp.bfloat16
VMEM_SPEC = pl.BlockSpec(memory_space=pltpu.VMEM)
NO_COST = pl.CostEstimate(flops=0, bytes_accessed=0, transcendentals=0)


def run(body, out_shapes, operands, scratch=(), after=()):
    many = isinstance(out_shapes, (tuple, list))
    count = len(operands)

    def kernel(*refs):
        body(*refs[:count], *refs[count + len(after) :])

    return pl.pallas_call(
        kernel,
        out_shape=out_shapes,
        in_specs=[VMEM_SPEC] * count + [pl.BlockSpec(memory_space=pl.ANY)] * len(after),
        out_specs=[VMEM_SPEC] * len(out_shapes) if many else VMEM_SPEC,
        scratch_shapes=list(scratch),
        compiler_params=pltpu.CompilerParams(vmem_limit_bytes=8 * 2**20),
        cost_estimate=NO_COST,
    )(*operands, *after)


TOKEN = jax.ShapeDtypeStruct((8, 128), F32)


def leave(token_ref):
    token_ref[...] = jnp.zeros(token_ref.shape, F32)


def same_group():
    rows = lax.broadcasted_iota(jnp.int32, (C, C), 0)
    columns = lax.broadcasted_iota(jnp.int32, (C, C), 1)
    return (rows >> 5) == (columns >> 5)


def fold(full, same):
    kept = jnp.where(same, full, 0.0)
    total = kept[0:GS]
    for g in range(1, CHANNEL_GROUPS):
        total = total + kept[g * GS : (g + 1) * GS]
    return total


def spread(packed, same):
    return jnp.where(same, jnp.concatenate([packed] * CHANNEL_GROUPS, axis=0), 0)


def split(value):
    high = value.astype(BF16)
    low = (value - high.astype(F32)).astype(BF16)
    return high, low


def spread_split(packed, same):
    high, low = split(spread(packed, same))
    return high, low


def dot(a, b):
    return jnp.dot(a, b, preferred_element_type=F32)


def times(left, right):
    rows = left.shape[0]
    left_high, left_low = split(left)
    right_high, right_low = right
    both = dot(jnp.concatenate([left_high, left_low], axis=0), right_high)
    return both[:rows] + both[rows:] + dot(left_high, right_low)


def unit():
    rows = lax.broadcasted_iota(jnp.int32, (GS, C), 0)
    columns = lax.broadcasted_iota(jnp.int32, (GS, C), 1)
    return jnp.where(rows == (columns & (GS - 1)), 1.0, 0.0)


def group_total(row, same):
    wide = jnp.broadcast_to(row, (8, C))
    return jnp.dot(wide, jnp.where(same, 1.0, 0.0), precision=lax.Precision.HIGHEST)


def stats_kernel(x_ref, out_ref):
    rows = x_ref.shape[0]
    cells = rows * x_ref.shape[1]
    same = same_group()

    def add_up(r, total):
        return total + jnp.sum(x_ref[r].astype(F32), axis=0, keepdims=True)

    mean = lax.fori_loop(0, rows, add_up, jnp.zeros((1, C), F32)) / cells

    def products(r, total):
        high, low = split(x_ref[r].astype(F32) - mean)
        return total + lax.dot_general(
            high,
            jnp.concatenate([high, low], axis=1),
            (((0,), (0,)), ((), ())),
            preferred_element_type=F32,
        )

    total = lax.fori_loop(0, rows, products, jnp.zeros((C, 2 * C), F32))
    cross = total[:, C:]
    out_ref[0:GS] = fold(total[:, :C] + cross + cross.T, same) / cells
    out_ref[GS : 2 * GS] = fold(jnp.broadcast_to(mean, (C, C)).T, same)
    out_ref[2 * GS : 2 * GS + 8] = jnp.broadcast_to(mean, (8, C))


def merge_kernel(a_ref, b_ref, out_ref):
    a, b = a_ref[...], b_ref[...]
    half = 0.5 * (a + b)
    gap = b - a
    wide = jnp.concatenate([gap[2 * GS :]] * (GS // 8), axis=0)
    out_ref[0:GS] = half[0:GS] + 0.25 * gap[GS : 2 * GS] * wide
    out_ref[GS:] = half[GS:]


def add_kernel(a_ref, b_ref, out_ref):
    out_ref[...] = a_ref[...] + b_ref[...]


def shift_band(moved_ref, bands_ref, e, middle, left, right):
    d, pad, width = DILATION_RATE, 16, middle.shape[0]
    bands_ref[pad : pad + width] = middle.astype(F32)
    bands_ref[pad - 8 : pad] = left.astype(F32)
    bands_ref[pad + width : pad + width + 8] = right.astype(F32)
    moved_ref[0, e] = bands_ref[pad + d : pad + d + width].astype(BF16)
    moved_ref[1, e] = middle
    moved_ref[2, e] = bands_ref[pad - d : pad - d + width].astype(BF16)


def tap_rows(moved_ref, weight_ref, taps):
    bands = [moved_ref[b, band] for a, band in taps for b in range(3)]
    taps = [a for a, _ in taps]
    weights = [weight_ref[3 * a + b] for a in taps for b in range(3)]
    return dot(jnp.concatenate(bands, axis=1), jnp.concatenate(weights, axis=0))


def pack_kernel(up_ref, left_ref, right_ref, odd_ref, first_ref, second_ref, token_ref):
    rows, width = up_ref.shape[0], up_ref.shape[1]
    d = DILATION_RATE
    odd = odd_ref[0:1] > 0.5
    for r in range(d):
        for begin, size, ref in ((0, width, up_ref), (width, 8, left_ref), (width + 8, 8, right_ref)):
            top, bottom = ref[r].astype(F32), ref[rows - d + r].astype(F32)
            first_ref[r, begin : begin + size] = jnp.where(odd, top, bottom).astype(BF16)
            second_ref[r, begin : begin + size] = jnp.where(odd, bottom, top).astype(BF16)
    leave(token_ref)


def bands_kernel(up_ref, left_ref, right_ref, w_ref, moved_ref, weight_ref, token_ref, bands_ref):
    rows = up_ref.shape[0]
    same = same_group()
    for tap in range(9):
        tile = jnp.concatenate([w_ref[tap].astype(F32)] * CHANNEL_GROUPS, axis=0)
        weight_ref[tap] = jnp.where(same, tile, 0.0).T.astype(BF16)

    def inner(r, carry):
        shift_band(moved_ref, bands_ref, r, up_ref[r], left_ref[r], right_ref[r])
        return carry

    lax.fori_loop(0, rows, inner, 0)
    leave(token_ref)


def near_kernel(moved_ref, weight_ref, out_ref, token_ref):
    rows = out_ref.shape[0]
    d = DILATION_RATE
    for first, last, taps in ((0, rows - d, {0: d, 1: 0}), (rows - d, d, {1: 0}), (d, rows, {1: 0, 2: -d})):

        def row(r, carry, taps=taps):
            out_ref[r] = tap_rows(moved_ref, weight_ref, [(a, r + step) for a, step in taps.items()])
            return carry

        lax.fori_loop(first, last, row, 0)
    leave(token_ref)


def far_kernel(odd_ref, first_ref, second_ref, weight_ref, near_ref, moved_ref, out_ref, token_ref, bands_ref):
    rows, width = out_ref.shape[0], out_ref.shape[1]
    d = DILATION_RATE

    def outer(r, carry):
        odd = odd_ref[0:1] > 0.5
        first, second = first_ref[r].astype(F32), second_ref[r].astype(F32)
        for begin, halo in ((0, jnp.where(odd, first, second)), (d, jnp.where(odd, second, first))):
            halo = halo.astype(BF16)
            shift_band(
                moved_ref, bands_ref, begin + r, halo[0:width], halo[width : width + 8], halo[width + 8 :]
            )
        return carry

    lax.fori_loop(0, d, outer, 0)
    back = 2 * d - rows
    for first, last, taps in ((0, rows - d, {2: 0}), (rows - d, d, {0: back, 2: 0}), (d, rows, {0: back})):

        def row(r, carry, taps=taps):
            far = tap_rows(moved_ref, weight_ref, [(a, r + step) for a, step in taps.items()])
            out_ref[r] = near_ref[r] + far
            return carry

        lax.fori_loop(first, last, row, 0)
    leave(token_ref)


def act_kernel(x_ref, stats_ref, gain_ref, bias_ref, turned_ref, slope_ref, kept_ref, mean_ref):
    rows, width = x_ref.shape[0], x_ref.shape[1]
    same = same_group()
    eye = unit()
    gain, bias = gain_ref[0:1], bias_ref[0:1]
    mean = stats_ref[2 * GS : 2 * GS + 1]
    cov = stats_ref[0:GS] + EPSILON * eye
    trace = group_total(jnp.sum(cov * eye, axis=0, keepdims=True), same)[0:1]
    normed = cov / trace
    normed_wide = spread_split(normed, same)
    iterate = 1.5 * eye - 0.5 * normed
    for k in range(ITERS - 1):
        wide = spread_split(iterate, same)
        square = times(iterate, wide)
        scaled = times(iterate, normed_wide)
        scaled_wide = spread_split(scaled, same)
        cube_scaled = times(square, scaled_wide)
        kept_ref[k, 0] = iterate
        kept_ref[k, 1] = square
        kept_ref[k, 2] = scaled
        iterate = 1.5 * iterate - 0.5 * cube_scaled
    whitener = iterate * lax.rsqrt(trace)
    mean_wide = jnp.broadcast_to(mean, (8, C))
    kept_ref[ITERS - 1, 0] = whitener
    kept_ref[ITERS - 1, 1] = normed
    kept_ref[ITERS - 1, 2] = jnp.broadcast_to(trace, (GS, C))
    mean_ref[...] = mean_wide
    white_high, white_low = spread_split(whitener, same)
    rounded = white_high.astype(F32) + white_low.astype(F32)
    offset = jnp.dot(mean_wide, rounded, precision=lax.Precision.HIGHEST)[0:1]

    for r in range(rows):
        x = x_ref[r]
        white = dot(x, white_high) + dot(x, white_low) - offset
        pre = gain * white + bias
        gate = 0.5 * jnp.tanh(0.5 * pre) + 0.5
        act = pre * gate
        turned_ref[:, r * width : (r + 1) * width] = act.T.astype(BF16)
        slope_ref[r] = gate + act * (1.0 - gate)


def tap_kernel(turned_ref, near_ref, far_ref, later_ref, own_ref, other_ref, total_ref):
    rows, width = near_ref.shape[1], near_ref.shape[2]
    d = DILATION_RATE
    gap = rows - d
    same = same_group()

    def pair(b, first, count, ref, band):
        turned = turned_ref[:, first * width : (first + count) * width]
        return dot(turned, ref[b, band : band + count].reshape(count * width, C))

    def column(b, carry):
        total_ref[b] = fold(pair(b, 0, gap, near_ref, d) + pair(b, gap, d, far_ref, d), same)
        total_ref[3 + b] = fold(pair(b, 0, rows, near_ref, 0), same)
        total_ref[6 + b] = fold(pair(b, 0, d, far_ref, 0) + pair(b, d, gap, near_ref, 0), same)
        return carry

    lax.fori_loop(0, 3, column, 0)
    later = later_ref[0:1] > 0.5
    total = total_ref[...].reshape(9 * GS, C)
    first, second = total[: own_ref.shape[0]], total[own_ref.shape[0] :]
    own_ref[...] = jnp.where(later, second, first)
    other_ref[...] = jnp.where(later, first, second)


def join_kernel(scale, own_ref, other_ref, later_ref, out_ref):
    later = later_ref[0:1] > 0.5
    own, other = own_ref[...] * scale, other_ref[...] * scale
    size = own.shape[0]
    out_ref[:size] = jnp.where(later, other, own)
    out_ref[size:] = jnp.where(later, own, other)


def grad_kernel(x_ref, grad_ref, slope_ref, kept_ref, mean_ref, gain_ref, back_ref, sums_ref):
    rows = x_ref.shape[0]
    same = same_group()
    gain = gain_ref[0:1]
    whitener = spread(kept_ref[ITERS - 1, 0], same)
    weighted_high, weighted_low = split((whitener * gain).T)

    def row(r, carry):
        bias_sum, total = carry
        pre_grad = grad_ref[r] * slope_ref[r]
        bias_sum = bias_sum + jnp.sum(pre_grad, axis=0, keepdims=True)
        high, low = split(pre_grad)
        back_ref[r] = dot(high, weighted_high) + dot(low, weighted_high) + dot(high, weighted_low)
        turn = lambda part: lax.dot_general(x_ref[r], part, (((0,), (0,)), ((), ())), preferred_element_type=F32)
        return bias_sum, total + turn(high) + turn(low)

    bias_sum, total = lax.fori_loop(0, rows, row, (jnp.zeros((1, C), F32), jnp.zeros((C, C), F32)))
    mean_column = jnp.broadcast_to(mean_ref[0:1], (C, C)).T
    full = total - mean_column * bias_sum
    gain_sum = jnp.sum(full * whitener, axis=0, keepdims=True)
    full = full * gain
    sums_ref[0:GS] = fold(full + full.T, same)
    line = lax.broadcasted_iota(jnp.int32, (8, C), 0)
    sums_ref[GS : GS + 8] = jnp.where(line == 0, gain_sum, jnp.where(line == 1, bias_sum, 0.0))


def prepare_kernel(kept_ref, mean_ref, gain_ref, wide_ref, lines_ref, token_ref):
    same = same_group()

    def put(place, packed):
        high, low = spread_split(packed, same)
        wide_ref[place, 0] = high
        wide_ref[place, 1] = low

    for k in range(ITERS - 1):
        iterate, square, scaled = kept_ref[k, 0], kept_ref[k, 1], kept_ref[k, 2]
        put(2 * k, scaled)
        put(2 * k + 1, times(iterate, (wide_ref[2 * k, 0], wide_ref[2 * k, 1])))
        lines_ref[0, k] = iterate
        lines_ref[1, k] = square
        lines_ref[2, k] = times(square, spread_split(iterate, same))
    put(2 * ITERS - 2, kept_ref[ITERS - 1, 1])
    for k in range(3):
        lines_ref[3, k] = kept_ref[ITERS - 1, k]
    lines_ref[3, 3, 0:8] = mean_ref[...]
    lines_ref[3, 3, 8:16] = gain_ref[...]
    lines_ref[3, 3, 16:] = jnp.zeros((GS - 16, C), F32)
    leave(token_ref)


def final_kernel(cell_count, x_ref, back_ref, sums_ref, wide_ref, lines_ref, out_ref, gain_out_ref, bias_out_ref):
    high, low, constant = derivative(cell_count, sums_ref, wide_ref, lines_ref)
    for r in range(x_ref.shape[0]):
        moved = dot(x_ref[r], high) + dot(x_ref[r], low)
        out_ref[r] = (moved + back_ref[r] - constant).astype(BF16)
    for line, ref in enumerate((gain_out_ref, bias_out_ref)):
        ref[...] = sums_ref[GS + line] * (1.0 / math.sqrt(cell_count))


def derivative(cell_count, sums_ref, wide_ref, lines_ref):
    same = same_group()
    eye = unit()
    whitener, normed = lines_ref[3, 0], lines_ref[3, 1]
    trace = lines_ref[3, 2, 0:1]
    mean, gain = lines_ref[3, 3, 0:8], lines_ref[3, 3, 8:16]
    paired = sums_ref[0:GS]
    step = paired * lax.rsqrt(trace)
    wide = lambda place: (wide_ref[place, 0], wide_ref[place, 1])
    direct = times(lines_ref[2].reshape((ITERS - 1) * GS, C), spread_split(step, same))
    change = -0.5 * step
    for k in range(ITERS - 1):
        moved = direct[k * GS : (k + 1) * GS] + times(change, wide(2 * k + 1))
        moved = moved + times(lines_ref[0, k], spread_split(times(change, wide(2 * k)), same))
        moved = moved + times(lines_ref[1, k], spread_split(times(change, wide(2 * ITERS - 2)), same))
        change = 1.5 * change - 0.5 * moved
    inner = jnp.sum(change * normed + 0.5 * paired * whitener, axis=0, keepdims=True)
    symmetric = (change - eye * group_total(inner, same)[0:1]) / trace
    high, low = spread_split(symmetric * (1.0 / cell_count), same)
    rounded = high.astype(F32) + low.astype(F32)
    bias_sum = sums_ref[GS + 1 : GS + 2]
    weighted = gain * bias_sum * (1.0 / cell_count)
    both = jnp.concatenate([mean, weighted], axis=1)
    constant = jnp.dot(
        both, jnp.concatenate([rounded, spread(whitener, same)], axis=0), precision=lax.Precision.HIGHEST
    )
    return high, low, constant[0:1]


def stages(axes):
    for axis in axes:
        size = lax.axis_size(axis)
        stride = 1
        while stride < size:
            yield axis, [(i, i ^ stride) for i in range(size)]
            stride *= 2


def add(part, other, after=()):
    if not after:
        return part + other
    return run(add_kernel, jax.ShapeDtypeStruct(part.shape, F32), (part, other), after=after)


def swap(earlier, later, axis):
    size = lax.axis_size(axis)
    got = []
    for begin, part in ((0, earlier), (1, later)):
        pairs = [(i, i + 1) for i in range(begin, size - 1, 2)]
        pairs = pairs + [(j, i) for i, j in pairs]
        got.append(lax.ppermute(part, axis, pairs) if pairs else jnp.zeros_like(part))
    return got


def shards(features, upstream, conv_weight, norm_gain, norm_bias):
    mos_n, rows, width, _ = features.shape
    axes = ("dp", "cols", "rows")
    cell_count = mos_n * rows * width
    for axis in axes:
        cell_count *= lax.axis_size(axis)
    stage_pairs = list(stages(axes))
    count = len(stage_pairs)
    d = DILATION_RATE
    x = features.reshape(rows, width, C)
    up = upstream.reshape(rows, width, C)
    gain = jnp.broadcast_to(norm_gain[None], (8, C))
    bias = jnp.broadcast_to(norm_bias[None], (8, C))
    shape = jax.ShapeDtypeStruct
    held = pltpu.VMEM
    cells = (rows, width, C)

    odd = lax.axis_index("cols") % 2 == 1
    first, second = up[:, :8], up[:, -8:]
    first, second = swap(jnp.where(odd, first, second), jnp.where(odd, second, first), "cols")
    left, right = jnp.where(odd, first, second), jnp.where(odd, second, first)
    odd_line = jnp.broadcast_to((lax.axis_index("rows") % 2 == 1).astype(F32), (8, C))
    tap_axis, tap_pairs = stage_pairs[0]
    later_line = jnp.broadcast_to((lax.axis_index(tap_axis) % 2 == 1).astype(F32), (8, C))
    halo = shape((d, width + 16, C), BF16)
    first, second, token = run(pack_kernel, (halo, halo, TOKEN), (up, left, right, odd_line), after=(later_line,))
    first, second = swap(first, second, "rows")
    stats = run(stats_kernel, shape((2 * GS + 8, C), F32), (x,), after=(token,))
    scratch = (pltpu.VMEM((width + 32, C), F32),)
    for number, (axis, pairs) in enumerate(stage_pairs):
        other = lax.ppermute(stats, axis, pairs)
        token = ()
        if number == count - 3:
            near_bands, weights, *token = run(
                bands_kernel,
                (held((3,) + cells, BF16), held((9, C, C), BF16), TOKEN),
                (up, left, right, conv_weight.reshape(9, GS, C)),
                scratch=scratch,
                after=(stats,),
            )
        if number == count - 2:
            near_grad, *token = run(
                near_kernel, (held(cells, F32), TOKEN), (near_bands, weights), after=(stats,)
            )
        if number == count - 1:
            far_bands, act_grad, *token = run(
                far_kernel,
                (held((3, 2 * d, width, C), BF16), held(cells, F32), TOKEN),
                (odd_line, first, second, weights, near_grad),
                scratch=scratch,
                after=(stats,),
            )
        stats = run(merge_kernel, shape(stats.shape, F32), (stats, other), after=token)

    turned, slope, kept, mean = run(
        act_kernel,
        (
            held((C, rows * width), BF16),
            held(cells, F32),
            held((ITERS, 3, GS, C), F32),
            held((8, C), F32),
        ),
        (x, stats, gain, bias),
    )
    half = shape((9 * GS // 2, C), F32)
    half, other = run(
        tap_kernel,
        (half, half),
        (turned, near_bands, far_bands, later_line),
        scratch=(pltpu.VMEM((9, GS, C), F32),),
    )
    half = add(half, lax.ppermute(other, tap_axis, tap_pairs))

    back, sums = run(
        grad_kernel,
        (held(cells, F32), shape((GS + 8, C), F32)),
        (x, act_grad, slope, kept, mean, gain),
        after=(half,),
    )
    row_stages = [stage for stage in stage_pairs[1:] if stage[0] == "rows"]
    tap_stages = row_stages + [stage for stage in stage_pairs[1:] if stage[0] != "rows"]
    in_flight = lax.ppermute(half, *tap_stages[0])
    for number, stage in enumerate(stage_pairs):
        other = lax.ppermute(sums, *stage)
        token = ()
        if number == count - 1:
            wide, lines, *token = run(
                prepare_kernel,
                (held((2 * ITERS - 1, 2, C, C), BF16), held((4, ITERS - 1, GS, C), F32), TOKEN),
                (kept, mean, gain),
                after=(sums,),
            )
        sums = add(sums, other, after=token)
        if number == 0:
            half = add(half, in_flight, after=(sums,))
        if 2 <= number < count:
            half = add(half, lax.ppermute(half, *tap_stages[number - 1]), after=(sums,))
    input_grad, gain_grad, bias_grad = run(
        functools.partial(final_kernel, cell_count),
        (shape(cells, BF16), shape((C,), F32), shape((C,), F32)),
        (x, back, sums, wide, lines),
        after=(half,),
    )
    other = lax.ppermute(half, tap_axis, tap_pairs)
    taps = run(
        functools.partial(join_kernel, 1.0 / math.sqrt(cell_count)),
        shape((9 * GS, C), F32),
        (half, other, later_line),
    )
    return (
        input_grad.reshape(features.shape),
        taps.reshape(3, 3, GS, C),
        gain_grad,
        bias_grad,
    )


def solution(mesh):
    placed = (P("dp", "rows", "cols", None), P("dp", "rows", "cols", None), P(), P(), P())
    return jax.shard_map(
        shards,
        mesh=mesh,
        in_specs=placed,
        out_specs=(P("dp", "rows", "cols", None), P(), P(), P()),
        check_vma=False,
    )
```
